32 devices in a mesh: dp: 8 (over z, x), fsdp: 4 (over y, core).
Axes of the slice: x: 2, y: 2, z: 4, core: 2. Of those that a mesh axis runs over, the one named last changes fastest.
Arguments:
- inputs: bfloat16 [64, 8, 16, 1152], P(('dp', 'fsdp')), may hold values from -6 to 6
- out_cotangent: bfloat16 [64, 8, 16, 1152], P(('dp', 'fsdp')), may hold values from -6 to 6
- lengths: int32 [64], P(('dp', 'fsdp')), may hold values from 8 to 16, as said below
- timesteps: int32 [64], P(('dp', 'fsdp')), may hold values from 0 to 999
- labels: int32 [64], P(('dp', 'fsdp')), may hold values from 0 to 100
- time_table: bfloat16 [1000, 1152], replicated, may hold values from -6 to 6
- class_table: bfloat16 [101, 1152], replicated, may hold values from -6 to 6
- ada_weight: bfloat16 [1152, 6912], P('fsdp', 'dp'), may hold values from -0.1875 to 0.1875
- qkv_weight: bfloat16 [1152, 3456], P('fsdp', 'dp'), may hold values from -0.1875 to 0.1875
- proj_weight: bfloat16 [1152, 1152], P('fsdp', 'dp'), may hold values from -0.625 to 0.625
- up_weight: bfloat16 [1152, 4608], P('fsdp', 'dp'), may hold values from -0.1875 to 0.1875
- down_weight: bfloat16 [4608, 1152], P('fsdp', 'dp'), may hold values from -0.09375 to 0.09375
Outputs:
- activations: bfloat16 [64, 8, 16, 1152], P(('dp', 'fsdp'))
- input_grad: bfloat16 [64, 8, 16, 1152], P(('dp', 'fsdp'))
- ada_grad: float32 [1152, 6912], P('fsdp', 'dp')
- qkv_grad: float32 [1152, 3456], P('fsdp', 'dp')
- proj_grad: float32 [1152, 1152], P('fsdp', 'dp')
- up_grad: float32 [1152, 4608], P('fsdp', 'dp')
- down_grad: float32 [4608, 1152], P('fsdp', 'dp')
The draws below stay inside these ranges and needn't reach their ends.
Inputs may be any that keep to these rules, and one draw needn't show every extreme that they name: `lengths`: every clip has 8 to 16 live frames; some clip has exactly 16 and some exactly 8.
All inputs are finite; a program needn't handle non-finite values.
Results may differ from the reference program's by a relative error of at most 0.019.
The reference program's roundings to bfloat16 on the way count: a program that leaves them out, or rounds other values in their place, can miss the bound.
Values may be sent and summed in bfloat16 or wider, within the bound.
No kernel may reach another device: no remote copies, remote signals or barrier semaphores. Data moves between devices by JAX's collectives and lax.ppermute only.
A program may use at most 256 MiB of HBM per device.

```python
import math
from functools import partial
import jax
import jax.numpy as jnp
from jax import lax

D = 1152
HEADS = 16
FF = 4608
FRAMES = 16
POS_DEV = 8
STEPS = 1000
CLASSES = 101
CLIPS = 64


def draw_lengths(key, part):
    key = jax.random.fold_in(key, 7)
    first_key, second_key, third_key = jax.random.split(key, 3)
    drawn = jax.random.randint(first_key, (CLIPS,), FRAMES // 2, FRAMES + 1)
    top_slot = jax.random.randint(second_key, (), 0, CLIPS)
    other_slot = (top_slot + 1 + jax.random.randint(third_key, (), 0, CLIPS - 1)) % CLIPS
    drawn = drawn.at[top_slot].set(FRAMES)
    drawn = drawn.at[other_slot].set(FRAMES // 2)
    return drawn.astype(jnp.int32)


def set_ends(array, rng, low, top_value):
    spot = [jax.random.randint(jax.random.fold_in(rng, axis), (), 0, length) for axis, length in enumerate(array.shape)]
    longest = array.shape.index(max(array.shape))
    beside = spot[:longest] + [(spot[longest] + 1) % array.shape[longest]] + spot[longest + 1:]
    return array.at[tuple(spot)].set(low).at[tuple(beside)].set(top_value)


def level_of(rng, dims, shards, least, largest):
    gain, own = 1.0, jax.random.fold_in(rng, 6)
    for dim, parts in shards:
        steps = jnp.exp(jax.random.uniform(jax.random.fold_in(own, dim), (parts,), jnp.float32, least / len(shards), largest / len(shards)))
        gain = gain * jnp.repeat(steps, dims[dim] // parts).reshape([-1 if axis == dim else 1 for axis in range(len(dims))])
    return gain


def centred(rng, dims, scale, bound, shards=(), kind=jnp.bfloat16):
    result = scale * jax.random.normal(rng, dims, jnp.float32)
    if shards:
        result = result * level_of(rng, dims, shards, -0.22, 0.18)
    return jnp.clip(result, -bound, bound).astype(kind)


def setup_inputs(seed: int = 0) -> dict:
    keys = jax.random.split(jax.random.key(seed), 13)
    return {
        "inputs": centred(keys[0], (CLIPS, POS_DEV, FRAMES, D), 1.0, 6.0, ((0, 32),)),
        "out_cotangent": centred(keys[1], (CLIPS, POS_DEV, FRAMES, D), 1.0, 6.0, ((0, 32),)),
        "lengths": draw_lengths(jax.random.fold_in(keys[12], 71), 0),
        "timesteps": set_ends(jax.random.randint(keys[3], (CLIPS,), 0, STEPS), jax.random.fold_in(keys[3], 1), 0, STEPS - 1).astype(jnp.int32),
        "labels": set_ends(jax.random.randint(keys[4], (CLIPS,), 0, CLASSES), jax.random.fold_in(keys[4], 1), 0, CLASSES - 1).astype(jnp.int32),
        "time_table": centred(keys[5], (STEPS, D), 1.0, 6.0),
        "class_table": centred(keys[6], (CLASSES, D), 1.0, 6.0),
        "ada_weight": centred(keys[7], (D, 6 * D), D ** -0.5, 0.1875, ((0, 4), (1, 8))),
        "qkv_weight": centred(keys[8], (D, 3 * D), D ** -0.5, 0.1875, ((0, 4), (1, 8))),
        "proj_weight": centred(keys[9], (D, D), (D // 12) ** -0.5, 0.625, ((0, 4), (1, 8))),
        "up_weight": centred(keys[10], (D, FF), D ** -0.5, 0.1875, ((0, 4), (1, 8))),
        "down_weight": centred(keys[11], (FF, D), FF ** -0.5, 0.09375, ((0, 4), (1, 8))),
    }


@jax.custom_vjp
def low(v):
    return lax.optimization_barrier(v.astype(jnp.bfloat16)).astype(jnp.float32)

@jax.custom_vjp
def low_back(v):
    return v

def low_keep(v):
    return (low(v), None)

def low_pass(kept, grad):
    return (grad,)

def back_keep(v):
    return (v, None)

def back_low(kept, grad):
    return (low(grad),)
low.defvjp(low_keep, low_pass)
low_back.defvjp(back_keep, back_low)

def exact_einsum(form, left, right):
    return jnp.einsum(form, left, right, precision=lax.Precision.HIGHEST)

def norm_mod(values, shift_add, scale_mul):
    center = values - lax.optimization_barrier(jnp.mean(values, -1, keepdims=True))
    spread = lax.optimization_barrier(jnp.mean(center * center, -1, keepdims=True))
    return center * lax.rsqrt(spread + 1e-06) * (1.0 + scale_mul) + shift_add

def clip_block(weights, pack):
    qkv_weight, proj_weight, up_weight, down_weight = weights
    tokens, modulation, clip_lengths = pack
    model_width = tokens.shape[-1]
    head_size = model_width // HEADS
    attn_scale = 1.0 / math.sqrt(head_size)
    pieces = [modulation[:, None, None, offset * model_width:(offset + 1) * model_width] for offset in range(6)]
    shift_one, scale_one, gate_one, shift_two, scale_two, gate_two = pieces
    hidden_one = low(norm_mod(tokens, shift_one, scale_one))
    mixed = low(low_back(exact_einsum('gpfd,de->gpfe', hidden_one, qkv_weight)))
    shaped = mixed.reshape(tokens.shape[:3] + (3, HEADS, head_size))
    queries = shaped[:, :, :, 0]
    key_part = shaped[:, :, :, 1]
    value_part = shaped[:, :, :, 2]
    raw_scores = exact_einsum('gpqhe,gpkhe->gphqk', queries, key_part) * attn_scale
    key_live = lax.iota(jnp.int32, FRAMES)[None, :] < clip_lengths[:, None].astype(jnp.int32)
    scores = jnp.where(key_live[:, None, None, None, :], low_back(raw_scores), -1e+30)
    row_max = lax.optimization_barrier(jnp.max(scores, -1, keepdims=True))
    exp_scores = jnp.exp(scores - row_max)
    attn_probs = exp_scores / lax.optimization_barrier(jnp.sum(exp_scores, -1, keepdims=True))
    attended = low(low_back(exact_einsum('gphqk,gpkhe->gpqhe', low(attn_probs), value_part)))
    branch = low_back(exact_einsum('gpfd,de->gpfe', attended.reshape(tokens.shape), proj_weight))
    middle = tokens + gate_one * branch
    hidden_two = low(norm_mod(middle, shift_two, scale_two))
    up_proj = low_back(exact_einsum('gpfd,de->gpfe', hidden_two, up_weight))
    activ = low(jax.nn.gelu(up_proj, approximate=True))
    ffn_out = low_back(exact_einsum('gpfe,ed->gpfd', activ, down_weight))
    return middle + gate_two * ffn_out

def forward_pass(cond, clip_lengths, tokens, ada_weight, qkv_weight, proj_weight, up_weight, down_weight):
    modulation = jnp.dot(low(cond), ada_weight, precision=lax.Precision.HIGHEST)
    group = math.gcd(CLIPS, max(1, 4096 // (POS_DEV * FRAMES)))
    count = CLIPS // group
    packs = (tokens.reshape((count, group) + tokens.shape[1:]), modulation.reshape(count, group, modulation.shape[-1]), clip_lengths.reshape(count, group))
    block_fn = jax.checkpoint(partial(clip_block, (qkv_weight, proj_weight, up_weight, down_weight)))
    results = lax.map(block_fn, packs)
    return results.reshape(tokens.shape)

def reference(inputs, out_cotangent, lengths, timesteps, labels, time_table, class_table, ada_weight, qkv_weight, proj_weight, up_weight, down_weight):
    cond = jax.nn.silu(time_table[timesteps].astype(jnp.float32) + class_table[labels].astype(jnp.float32))
    bound_fn = partial(forward_pass, cond, lengths)
    outputs, pull_back = jax.vjp(bound_fn, inputs.astype(jnp.float32), ada_weight.astype(jnp.float32), qkv_weight.astype(jnp.float32), proj_weight.astype(jnp.float32), up_weight.astype(jnp.float32), down_weight.astype(jnp.float32))
    grads = pull_back(out_cotangent.astype(jnp.float32))
    return (outputs.astype(jnp.bfloat16), grads[0].astype(jnp.bfloat16), grads[1], grads[2], grads[3], grads[4], grads[5])
```

```python
import functools
import math

import jax
import jax.numpy as jnp
from jax import lax
from jax.experimental import pallas as pl
from jax.experimental.pallas import tpu as pltpu
from jax.sharding import PartitionSpec as P

HEADS = 16
AXES = ("dp", "fsdp")
EPS = 1e-06
F32, LOW = jnp.float32, jnp.bfloat16


def norm_mod(values, shift_add, scale_mul):
    center = values - jnp.mean(values, -1, keepdims=True)
    spread = jnp.mean(center * center, -1, keepdims=True)
    return center * lax.rsqrt(spread + 1e-06) * (1.0 + scale_mul) + shift_add


def gelu_tanh(values):
    return jax.nn.gelu(values, approximate=True)


def gather_five(shards):
    row_set = (
        lax.all_gather(shards[0], "fsdp", axis=0, tiled=True),
        lax.all_gather(shards[1], "fsdp", axis=0, tiled=True),
        lax.all_gather(shards[2], "fsdp", axis=0, tiled=True),
        lax.all_gather(shards[3], "fsdp", axis=0, tiled=True),
        lax.all_gather(shards[4], "fsdp", axis=0, tiled=True),
    )
    return (
        lax.all_gather(row_set[0], "dp", axis=1, tiled=True),
        lax.all_gather(row_set[1], "dp", axis=1, tiled=True),
        lax.all_gather(row_set[2], "dp", axis=1, tiled=True),
        lax.all_gather(row_set[3], "dp", axis=1, tiled=True),
        lax.all_gather(row_set[4], "dp", axis=1, tiled=True),
    )


def scatter_five(totals):
    row_set = (
        lax.psum_scatter(
            totals[0].astype(jnp.bfloat16), "fsdp", scatter_dimension=0, tiled=True
        ).astype(jnp.float32),
        lax.psum_scatter(
            totals[1].astype(jnp.bfloat16), "fsdp", scatter_dimension=0, tiled=True
        ).astype(jnp.float32),
        lax.psum_scatter(
            totals[2].astype(jnp.bfloat16), "fsdp", scatter_dimension=0, tiled=True
        ).astype(jnp.float32),
        lax.psum_scatter(
            totals[3].astype(jnp.bfloat16), "fsdp", scatter_dimension=0, tiled=True
        ).astype(jnp.float32),
        lax.psum_scatter(
            totals[4].astype(jnp.bfloat16), "fsdp", scatter_dimension=0, tiled=True
        ).astype(jnp.float32),
    )
    return (
        lax.psum_scatter(
            row_set[0].astype(jnp.bfloat16), "dp", scatter_dimension=1, tiled=True
        ).astype(jnp.float32),
        lax.psum_scatter(
            row_set[1].astype(jnp.bfloat16), "dp", scatter_dimension=1, tiled=True
        ).astype(jnp.float32),
        lax.psum_scatter(
            row_set[2].astype(jnp.bfloat16), "dp", scatter_dimension=1, tiled=True
        ).astype(jnp.float32),
        lax.psum_scatter(
            row_set[3].astype(jnp.bfloat16), "dp", scatter_dimension=1, tiled=True
        ).astype(jnp.float32),
        lax.psum_scatter(
            row_set[4].astype(jnp.bfloat16), "dp", scatter_dimension=1, tiled=True
        ).astype(jnp.float32),
    )


def fetch_weights(ada_weight, core_shards):
    return tuple(gather_five((ada_weight,) + tuple(core_shards)))


def matmul_tn(left, right):
    return lax.dot_general(
        left, right, (((0,), (0,)), ((), ())), preferred_element_type=jnp.float32
    )


def matmul_nt(left, right):
    return lax.dot_general(
        left, right, (((1,), (1,)), ((), ())), preferred_element_type=jnp.float32
    )


def general_body(
    inputs,
    out_cotangent,
    lengths,
    timesteps,
    labels,
    time_table,
    class_table,
    ada_weight,
    qkv_weight,
    proj_weight,
    up_weight,
    down_weight,
):
    core_shards = (qkv_weight, proj_weight, up_weight, down_weight)
    clip_count, positions, frames, model_width = inputs.shape
    row_count = clip_count * positions * frames
    seq_count = clip_count * positions
    span = positions * frames
    head_size = model_width // HEADS
    attn_scale = 1.0 / math.sqrt(head_size)
    ada_full, qkv_full, proj_full, up_full, down_full = fetch_weights(ada_weight, core_shards)
    time_onehot = (timesteps[:, None] == lax.iota(jnp.int32, time_table.shape[0])[None, :]).astype(
        jnp.bfloat16
    )
    class_onehot = (labels[:, None] == lax.iota(jnp.int32, class_table.shape[0])[None, :]).astype(
        jnp.bfloat16
    )
    embedded = jnp.dot(time_onehot, time_table, preferred_element_type=jnp.float32) + jnp.dot(
        class_onehot, class_table, preferred_element_type=jnp.float32
    )
    cond_low = jax.nn.silu(embedded).astype(jnp.bfloat16)
    modulation = jnp.dot(cond_low, ada_full, preferred_element_type=jnp.float32)
    pieces = [
        modulation[:, None, offset * model_width : (offset + 1) * model_width]
        for offset in range(6)
    ]
    shift_one, scale_one, gate_one, shift_two, scale_two, gate_two = pieces
    residual = inputs.astype(jnp.float32).reshape(clip_count, span, model_width)
    hidden_one = (
        norm_mod(residual, shift_one, scale_one)
        .astype(jnp.bfloat16)
        .reshape(row_count, model_width)
    )
    mixed = jnp.dot(hidden_one, qkv_full, preferred_element_type=jnp.float32).astype(jnp.bfloat16)
    shaped = mixed.reshape(seq_count, frames, 3, HEADS, head_size)
    queries = shaped[:, :, 0]
    key_part = shaped[:, :, 1]
    value_part = shaped[:, :, 2]
    clip_live = lax.iota(jnp.int32, frames)[None, :] < lengths[:, None]
    key_live = jnp.repeat(clip_live, positions, axis=0)
    scores = (
        jnp.einsum("sqhe,skhe->shqk", queries, key_part, preferred_element_type=jnp.float32)
        * attn_scale
    )
    scores = jnp.where(key_live[:, None, None, :], scores, -1e30)
    row_max = jnp.max(scores, -1, keepdims=True)
    exp_scores = jnp.exp(scores - row_max)
    attn_probs = exp_scores / jnp.sum(exp_scores, -1, keepdims=True)
    probs_low = attn_probs.astype(jnp.bfloat16)
    attended = jnp.einsum(
        "shqk,skhe->sqhe", probs_low, value_part, preferred_element_type=jnp.float32
    )
    attended_low = attended.astype(jnp.bfloat16).reshape(row_count, model_width)
    branch = jnp.dot(attended_low, proj_full, preferred_element_type=jnp.float32).reshape(
        clip_count, span, model_width
    )
    middle = residual + gate_one * branch
    hidden_two = (
        norm_mod(middle, shift_two, scale_two).astype(jnp.bfloat16).reshape(row_count, model_width)
    )
    up_proj = jnp.dot(hidden_two, up_full, preferred_element_type=jnp.float32)
    activ_low = gelu_tanh(up_proj).astype(jnp.bfloat16)
    ffn_out = jnp.dot(activ_low, down_full, preferred_element_type=jnp.float32).reshape(
        clip_count, span, model_width
    )
    result = (middle + gate_two * ffn_out).astype(jnp.bfloat16).reshape(inputs.shape)
    ada_full, qkv_full, proj_full, up_full, down_full = fetch_weights(ada_weight, core_shards)
    grad_out = out_cotangent.astype(jnp.float32).reshape(clip_count, span, model_width)
    d_gate_two = jnp.sum(grad_out * ffn_out, axis=1)
    d_ffn = (grad_out * gate_two).astype(jnp.bfloat16).reshape(row_count, model_width)
    d_activ = matmul_nt(d_ffn, down_full)
    down_total = matmul_tn(activ_low, d_ffn)
    gelu_value, gelu_pull = jax.vjp(gelu_tanh, up_proj)
    d_up = gelu_pull(d_activ)[0].astype(jnp.bfloat16)
    d_hidden_two = matmul_nt(d_up, up_full)
    up_total = matmul_tn(hidden_two, d_up)
    norm_value, norm_pull = jax.vjp(norm_mod, middle, shift_two, scale_two)
    d_middle_norm, d_shift_two, d_scale_two = norm_pull(
        d_hidden_two.reshape(clip_count, span, model_width)
    )
    d_middle = grad_out + d_middle_norm
    d_gate_one = jnp.sum(d_middle * branch, axis=1)
    d_branch = (d_middle * gate_one).astype(jnp.bfloat16).reshape(row_count, model_width)
    d_attended = (
        matmul_nt(d_branch, proj_full)
        .astype(jnp.bfloat16)
        .reshape(seq_count, frames, HEADS, head_size)
    )
    proj_total = matmul_tn(attended_low, d_branch)
    d_value = jnp.einsum(
        "shqk,sqhe->skhe", probs_low, d_attended, preferred_element_type=jnp.float32
    )
    d_probs = jnp.einsum(
        "sqhe,skhe->shqk", d_attended, value_part, preferred_element_type=jnp.float32
    )
    d_scores = attn_probs * (d_probs - jnp.sum(attn_probs * d_probs, -1, keepdims=True))
    d_scores_low = d_scores.astype(jnp.bfloat16)
    d_query = (
        jnp.einsum("shqk,skhe->sqhe", d_scores_low, key_part, preferred_element_type=jnp.float32)
        * attn_scale
    )
    d_key = (
        jnp.einsum("shqk,sqhe->skhe", d_scores_low, queries, preferred_element_type=jnp.float32)
        * attn_scale
    )
    d_mixed = (
        jnp.stack([d_query, d_key, d_value], axis=2)
        .astype(jnp.bfloat16)
        .reshape(row_count, 3 * model_width)
    )
    d_hidden_one = matmul_nt(d_mixed, qkv_full)
    qkv_total = matmul_tn(hidden_one, d_mixed)
    norm_first, first_pull = jax.vjp(norm_mod, residual, shift_one, scale_one)
    d_input_norm, d_shift_one, d_scale_one = first_pull(
        d_hidden_one.reshape(clip_count, span, model_width)
    )
    input_grad = (d_middle + d_input_norm).astype(jnp.bfloat16).reshape(inputs.shape)
    d_modulation = jnp.concatenate(
        [
            d_shift_one[:, 0],
            d_scale_one[:, 0],
            d_gate_one,
            d_shift_two[:, 0],
            d_scale_two[:, 0],
            d_gate_two,
        ],
        axis=-1,
    )
    ada_total = jnp.dot(
        cond_low.astype(jnp.float32).T, d_modulation, precision=lax.Precision.HIGHEST
    )
    ada_grad, qkv_grad, proj_grad, up_grad, down_grad = scatter_five(
        (ada_total, qkv_total, proj_total, up_total, down_total)
    )
    return (result, input_grad, ada_grad, qkv_grad, proj_grad, up_grad, down_grad)


def dot_nn(left, right):
    return lax.dot_general(left, right, (((1,), (0,)), ((), ())), preferred_element_type=F32)


def dot_nt(left, right):
    return lax.dot_general(left, right, (((1,), (1,)), ((), ())), preferred_element_type=F32)


def dot_tn(left, right):
    return lax.dot_general(left, right, (((0,), (0,)), ((), ())), preferred_element_type=F32)


def stats(values):
    mean = jnp.mean(values, -1, keepdims=True)
    center = values - mean
    spread = jnp.mean(center * center, -1, keepdims=True)
    inverse = lax.rsqrt(spread + EPS)
    return center * inverse, inverse


def here(names):
    return lax.axis_index(names[0]), lax.axis_index(names[1])


def start_blocks(half_refs, weight_ref, sems):
    column, row = here(AXES)
    row_parts = weight_ref.shape[1]
    copies = {}
    for relative, halves in enumerate(half_refs):
        copies[relative] = []
        for part, ref in enumerate(halves):
            height = ref.shape[0]
            copy = pltpu.make_async_copy(
                ref,
                weight_ref.at[
                    column ^ (relative // row_parts),
                    row ^ (relative % row_parts),
                    pl.ds(part * height, height),
                ],
                sems.at[relative, part],
            )
            copy.start()
            copies[relative].append(copy)
    return copies


def pair_mask(span, frames, live):
    query = lax.broadcasted_iota(jnp.int32, (span, span), 0)
    key = lax.broadcasted_iota(jnp.int32, (span, span), 1)
    return ((query // frames) == (key // frames)) & ((key % frames) < live)


def head_probs(queries, keys, live_mask, scale):
    scores = dot_nt(queries, keys) * scale
    scores = jnp.where(live_mask, scores, -1e30)
    exp_scores = jnp.exp(scores - jnp.max(scores, -1, keepdims=True))
    return exp_scores / jnp.sum(exp_scores, -1, keepdims=True)


def head_slices(ref, which, head, rows, size):
    per = ref.shape[2] // size
    slot = which * HEADS + head
    return ref[slot // per, rows, (slot % per) * size : (slot % per + 1) * size]


def attn_forward_kernel(sizes, *refs):
    clips, span, frames, width, qkv_cols, proj_cols, chunk = sizes
    column_parts, row_parts = sizes_parts(refs[-2])
    blocks = column_parts * row_parts
    lengths, tokens, mod = refs[:3]
    half_refs = [(refs[3 + i], refs[3 + blocks + i]) for i in range(blocks)]
    hidden, mixed, attended, branch, middle, hidden_two = refs[3 + 2 * blocks : 9 + 2 * blocks]
    weight, sems = refs[9 + 2 * blocks :]
    copies = start_blocks(half_refs, weight, sems)
    size = width // HEADS
    part_width = width // row_parts
    scale = 1.0 / math.sqrt(size)

    def first_norm(step, carry):
        rows = pl.ds(pl.multiple_of(step * chunk, chunk), chunk)
        clip_mod = mod[step * chunk // span]
        unit, _ = stats(tokens[rows, :].astype(F32))
        value = (unit * (1.0 + clip_mod[1:2]) + clip_mod[0:1]).astype(LOW)
        for part in range(row_parts):
            hidden[part, rows, :] = value[:, part * part_width : (part + 1) * part_width]
        return carry

    lax.fori_loop(0, clips * span // chunk, first_norm, 0)
    column, row = here(AXES)
    for relative in range(column_parts):
        for other in range(row_parts):
            for copy in copies[relative * row_parts + other]:
                copy.wait()
        place = column ^ relative
        total = dot_nn(hidden[0], weight[place, 0, :, 0:qkv_cols])
        for part in range(1, row_parts):
            total += dot_nn(hidden[part], weight[place, part, :, 0:qkv_cols])
        mixed[place] = total.astype(LOW)

    per = part_width // size
    for clip in range(clips):
        rows = slice(clip * span, (clip + 1) * span)
        live_mask = pair_mask(span, frames, lengths[clip])
        for head in range(HEADS):
            probs = head_probs(
                head_slices(mixed, 0, head, rows, size),
                head_slices(mixed, 1, head, rows, size),
                live_mask,
                scale,
            )
            value = dot_nn(probs.astype(LOW), head_slices(mixed, 2, head, rows, size))
            attended[head // per, rows, (head % per) * size : (head % per + 1) * size] = (
                value.astype(LOW)
            )

    for place in range(column_parts):
        total = dot_nn(attended[0], weight[place, 0, :, qkv_cols : qkv_cols + proj_cols])
        for part in range(1, row_parts):
            total += dot_nn(attended[part], weight[place, part, :, qkv_cols : qkv_cols + proj_cols])
        branch[:, place * proj_cols : (place + 1) * proj_cols] = total

    def second_norm(step, carry):
        rows = pl.ds(pl.multiple_of(step * chunk, chunk), chunk)
        clip_mod = mod[step * chunk // span]
        value = tokens[rows, :].astype(F32) + clip_mod[2:3] * branch[rows, :]
        middle[rows, :] = value
        unit, _ = stats(value)
        hidden_two[rows, :] = (unit * (1.0 + clip_mod[4:5]) + clip_mod[3:4]).astype(LOW)
        return carry

    lax.fori_loop(0, clips * span // chunk, second_norm, 0)


def sizes_parts(weight_ref):
    return weight_ref.shape[0], weight_ref.shape[1]


def attn_backward_kernel(sizes, *refs):
    clips, span, frames, width, qkv_cols, proj_cols, chunk = sizes
    column_parts, row_parts = sizes_parts(refs[-5])
    blocks = column_parts * row_parts
    lengths, tokens, cotangent, mod, middle, branch, mixed, grad_own, grad_far = refs[:9]
    half_refs = [(refs[9 + i], refs[9 + blocks + i]) for i in range(blocks)]
    input_grad, d_both, d_mod = refs[9 + 2 * blocks : 12 + 2 * blocks]
    weight, sems, d_middle, d_attended, d_hidden = refs[12 + 2 * blocks :]
    copies = start_blocks(half_refs, weight, sems)
    size = width // HEADS
    part_width = width // row_parts
    scale = 1.0 / math.sqrt(size)
    steps = span // chunk
    zero_row = jnp.zeros((1, width), F32)

    for clip in range(clips):
        clip_mod = mod[clip]

        def second_back(step, carry, clip=clip, clip_mod=clip_mod):
            d_shift, d_scale, d_gate = carry
            rows = pl.ds(pl.multiple_of(clip * span + step * chunk, chunk), chunk)
            grad = grad_own[rows, :] + grad_far[rows, :].astype(F32)
            unit, inverse = stats(middle[rows, :])
            d_unit = grad * (1.0 + clip_mod[4:5])
            d_value = cotangent[rows, :].astype(F32) + inverse * (
                d_unit
                - jnp.mean(d_unit, -1, keepdims=True)
                - unit * jnp.mean(d_unit * unit, -1, keepdims=True)
            )
            d_middle[rows, :] = d_value
            d_branch = (d_value * clip_mod[2:3]).astype(LOW)
            for place in range(column_parts):
                d_both[place, rows, qkv_cols : qkv_cols + proj_cols] = d_branch[
                    :, place * proj_cols : (place + 1) * proj_cols
                ]
            return (
                d_shift + jnp.sum(grad, 0, keepdims=True),
                d_scale + jnp.sum(grad * unit, 0, keepdims=True),
                d_gate + jnp.sum(d_value * branch[rows, :], 0, keepdims=True),
            )

        sums = lax.fori_loop(0, steps, second_back, (zero_row, zero_row, zero_row))
        d_mod[clip, 2:3, :] = sums[2]
        d_mod[clip, 3:4, :] = sums[0]
        d_mod[clip, 4:5, :] = sums[1]
        d_mod[clip, 5:6, :] = zero_row

    for group in copies.values():
        for copy in group:
            copy.wait()

    proj = slice(qkv_cols, qkv_cols + proj_cols)
    for part in range(row_parts):
        total = dot_nt(d_both[0, :, proj], weight[0, part, :, proj])
        for place in range(1, column_parts):
            total += dot_nt(d_both[place, :, proj], weight[place, part, :, proj])
        d_attended[part] = total.astype(LOW)

    per = part_width // size
    for clip in range(clips):
        rows = slice(clip * span, (clip + 1) * span)
        live_mask = pair_mask(span, frames, lengths[clip])
        for head in range(HEADS):
            queries = head_slices(mixed, 0, head, rows, size)
            keys = head_slices(mixed, 1, head, rows, size)
            values = head_slices(mixed, 2, head, rows, size)
            probs = head_probs(queries, keys, live_mask, scale)
            grad = d_attended[head // per, rows, (head % per) * size : (head % per + 1) * size]
            d_value = dot_tn(probs.astype(LOW), grad)
            d_probs = dot_nt(grad, values)
            d_scores = (probs * (d_probs - jnp.sum(probs * d_probs, -1, keepdims=True))).astype(LOW)
            d_query = dot_nn(d_scores, keys) * scale
            d_key = dot_tn(d_scores, queries) * scale
            cols = qkv_cols // size
            for which, piece in enumerate((d_query, d_key, d_value)):
                slot = which * HEADS + head
                d_both[
                    slot // cols, rows, (slot % cols) * size : (slot % cols + 1) * size
                ] = piece.astype(LOW)

    for part in range(row_parts):
        total = dot_nt(d_both[0, :, 0:qkv_cols], weight[0, part, :, 0:qkv_cols])
        for place in range(1, column_parts):
            total += dot_nt(d_both[place, :, 0:qkv_cols], weight[place, part, :, 0:qkv_cols])
        d_hidden[:, part * part_width : (part + 1) * part_width] = total

    for clip in range(clips):
        clip_mod = mod[clip]

        def first_back(step, carry, clip=clip, clip_mod=clip_mod):
            d_shift, d_scale = carry
            rows = pl.ds(pl.multiple_of(clip * span + step * chunk, chunk), chunk)
            grad = d_hidden[rows, :]
            unit, inverse = stats(tokens[rows, :].astype(F32))
            d_unit = grad * (1.0 + clip_mod[1:2])
            input_grad[rows, :] = (
                d_middle[rows, :]
                + inverse
                * (
                    d_unit
                    - jnp.mean(d_unit, -1, keepdims=True)
                    - unit * jnp.mean(d_unit * unit, -1, keepdims=True)
                )
            ).astype(LOW)
            return (
                d_shift + jnp.sum(grad, 0, keepdims=True),
                d_scale + jnp.sum(grad * unit, 0, keepdims=True),
            )

        sums = lax.fori_loop(0, steps, first_back, (zero_row, zero_row))
        d_mod[clip, 0:1, :] = sums[0]
        d_mod[clip, 1:2, :] = sums[1]


def attn_weight_kernel(sizes, *refs):
    qkv_cols, proj_cols, half = sizes
    own, far = refs[:3], refs[3:6]
    outs = refs[6:]
    column_parts, row_parts = own[2].shape[0], own[0].shape[0]
    column, row = here(AXES)
    for other in range(row_parts // 2):
        part = row ^ (2 * other)
        for relative in range(column_parts):
            place = column ^ relative
            x_bit, z_bits = relative % 2, relative // 2
            groups = column_parts // 2
            first = outs[other * groups + z_bits]
            second = outs[(2 + x_bit) * groups + z_bits]
            total = dot_tn(own[0][part], own[2][place, :, 0:qkv_cols]) + dot_tn(
                far[0][part], far[2][place, :, 0:qkv_cols]
            )
            first[x_bit, :, 0:qkv_cols] = total[:half].astype(LOW)
            second[other, :, 0:qkv_cols] = total[half:].astype(LOW)
            proj = slice(qkv_cols, qkv_cols + proj_cols)
            total = dot_tn(own[1][part], own[2][place, :, proj]) + dot_tn(
                far[1][part], far[2][place, :, proj]
            )
            first[x_bit, :, proj] = total[:half].astype(LOW)
            second[other, :, proj] = total[half:].astype(LOW)


def feed_kernel(chunk, *refs):
    hidden, d_outs = refs[0:2], refs[2:4]
    blocks = refs[4:-7]
    outs, blocks = blocks[-8:], blocks[:-8]
    up_weight, down_weight, sems, up_proj, d_activ, activ_s, d_up_s = refs[-7:]
    activ, d_up, d_hidden, partial = outs[0:2], outs[2:4], outs[4:6], outs[6:8]
    column, _ = here(AXES)
    copies = []
    for relative, ref in enumerate(blocks):
        half = ref.shape[0] // 2
        place = pl.ds(pl.multiple_of((column ^ relative) * half, 16), half)
        for which, weight in enumerate((up_weight, down_weight)):
            copy = pltpu.make_async_copy(
                ref.at[pl.ds(which * half, half)], weight.at[place], sems.at[relative, which]
            )
            copy.start()
            copies.append(copy)
    for copy in copies:
        copy.wait()
    tilt = math.sqrt(2.0 / math.pi)
    for index in range(2):
        up_proj[...] = dot_nt(hidden[index][...], up_weight[...])
        d_activ[...] = dot_nn(d_outs[index][...], down_weight[...])

        def gelu(step, carry, index=index):
            rows = pl.ds(pl.multiple_of(step * chunk, chunk), chunk)
            value = up_proj[rows, :]
            square = value * value
            bend = jnp.tanh(tilt * value * (1.0 + 0.044715 * square))
            activ_low = (0.5 * value * (1.0 + bend)).astype(LOW)
            slope = 0.5 * (1.0 + bend) + 0.5 * value * (1.0 - bend * bend) * (
                tilt * (1.0 + 3.0 * 0.044715 * square)
            )
            activ[index][rows, :] = activ_low
            d_up[index][rows, :] = (d_activ[rows, :] * slope).astype(LOW)
            return carry

        lax.fori_loop(0, up_proj.shape[0] // chunk, gelu, 0)
        d_hidden[index][...] = dot_nn(d_up[index][...], up_weight[...]).astype(
            d_hidden[index].dtype
        )
        partial[index][...] = dot_nt(activ[index][...], down_weight[...]).astype(
            partial[index].dtype
        )


def feed_weight_kernel(tile, *refs):
    count = (len(refs) - 3) // 2
    hidden, d_outs, activ, d_up = refs[0:4], refs[4:8], refs[8:12], refs[12:16]
    outs = refs[16:-3]
    up_grad, down_grad, sems = refs[-3:]
    column, _ = here(AXES)

    def product(step, carry):
        cols = pl.ds(pl.multiple_of(step * tile, tile), tile)
        for left, right, grad in ((d_up, hidden, up_grad), (d_outs, activ, down_grad)):
            total = dot_tn(left[0][:, cols], right[0][...])
            for index in range(1, 4):
                total += dot_tn(left[index][:, cols], right[index][...])
            grad[cols, :] = total.astype(LOW)
        return carry

    lax.fori_loop(0, up_grad.shape[0] // tile, product, 0)
    copies = []
    for relative, ref in enumerate(outs):
        half = ref.shape[0] // 2
        place = pl.ds(pl.multiple_of((column ^ relative) * half, 16), half)
        for which, grad in enumerate((up_grad, down_grad)):
            copy = pltpu.make_async_copy(
                grad.at[place], ref.at[pl.ds(which * half, half)], sems.at[relative, which]
            )
            copy.start()
            copies.append(copy)
    for copy in copies:
        copy.wait()


VMEM_SPEC = pl.BlockSpec(memory_space=pltpu.VMEM)
SMEM_SPEC = pl.BlockSpec(memory_space=pltpu.SMEM)
ANY_SPEC = pl.BlockSpec(memory_space=pl.ANY)
PARAMS = pltpu.CompilerParams(vmem_limit_bytes=56 * 1024 * 1024)


def shape_of(dims, kind=LOW):
    return jax.ShapeDtypeStruct(dims, kind)


def cost(flops, moved, special=0):
    return pl.CostEstimate(flops=flops, bytes_accessed=moved, transcendentals=special)


def swap(value, mask, count):
    return lax.ppermute(value, AXES, [(i, i ^ mask) for i in range(count)])


def spread(block, stages, count):
    have = {0: block}
    for masks in stages:
        fresh = dict(have)
        for mask in masks:
            for relative, value in have.items():
                fresh[relative ^ mask] = swap(value, mask, count)
        have = fresh
    return have


def padded_exchange(rows, count):
    length = rows.shape[1]
    tiles = -(-length // 1024) * 8
    rows = jnp.pad(rows, ((0, 0), (0, tiles * 128 - length))).reshape(count, tiles, 128)
    got = lax.all_to_all(rows, AXES, 0, 0, tiled=True)
    return got.reshape(count, tiles * 128)[:, :length]


def fast_body(
    column_parts,
    row_parts,
    inputs,
    out_cotangent,
    lengths,
    timesteps,
    labels,
    time_table,
    class_table,
    ada_weight,
    qkv_weight,
    proj_weight,
    up_weight,
    down_weight,
):
    count = column_parts * row_parts
    clips, positions, frames, width = inputs.shape
    span = positions * frames
    row_count = clips * span
    qkv_cols, proj_cols = qkv_weight.shape[1], proj_weight.shape[1]
    height = qkv_weight.shape[0]
    part_width = width // row_parts
    hidden_part = up_weight.shape[1] * column_parts // row_parts
    sub = up_weight.shape[1] // row_parts
    x_mask = row_parts
    z_masks = tuple(row_parts * 2 * i for i in range(1, column_parts // 2))
    half = height // 2

    own_block = jnp.concatenate([qkv_weight, proj_weight], axis=1)
    first_half = spread(own_block[:half], (z_masks, (x_mask,), (2,), (1,)), count)
    second_half = spread(own_block[half:], (z_masks, (2,), (x_mask,), (1,)), count)
    halves = [first_half[i] for i in range(count)] + [second_half[i] for i in range(count)]

    cond_rows = [
        lax.dynamic_slice_in_dim(time_table, timesteps[i], 1, 0).astype(F32)
        + lax.dynamic_slice_in_dim(class_table, labels[i], 1, 0).astype(F32)
        for i in range(clips)
    ]
    cond_low = jax.nn.silu(jnp.concatenate(cond_rows, 0)).astype(LOW)
    cond_send = cond_low.reshape(clips, row_parts, part_width).transpose(1, 0, 2)
    cond_send = jnp.broadcast_to(
        cond_send.reshape(1, row_parts, clips * part_width),
        (column_parts, row_parts, clips * part_width),
    ).reshape(count, clips * part_width)
    cond_all = padded_exchange(cond_send, count).reshape(count * clips, part_width)
    ada_cols = ada_weight.shape[1]
    mod_part = jnp.dot(cond_all, ada_weight, preferred_element_type=F32)
    mod_got = padded_exchange(mod_part.reshape(count, clips * ada_cols), count)
    mod_own = jnp.sum(mod_got.reshape(column_parts, row_parts, clips, ada_cols), axis=1)
    mod = mod_own.transpose(1, 0, 2).reshape(clips, 6, width)

    up_send = up_weight.reshape(height, row_parts, sub).transpose(1, 2, 0)
    down_send = (
        down_weight.reshape(-1, row_parts, sub, proj_cols)
        .transpose(1, 3, 0, 2)
        .reshape(row_parts, proj_cols, -1)
    )
    both_send = jnp.stack([up_send, down_send], axis=1)
    both_send, _ = lax.optimization_barrier((both_send, second_half[z_masks[0]]))
    both_got = lax.all_to_all(both_send, "fsdp", 0, 0, tiled=True)
    own_feed = both_got.transpose(1, 2, 0, 3).reshape(2 * sub, width)
    feed = spread(own_feed, (z_masks, (x_mask,)), count)
    feed_blocks = [feed[i * row_parts] for i in range(column_parts)]

    tokens = inputs.reshape(row_count, width)
    cotangent = out_cotangent.reshape(row_count, width)
    sizes = (clips, span, frames, width, qkv_cols, proj_cols, 32)
    full = (row_count, width)
    weight_scratch = [
        pltpu.VMEM((column_parts, row_parts, height, qkv_cols + proj_cols), LOW),
        pltpu.SemaphoreType.DMA((count, 2)),
    ]
    hidden, mixed, attended, branch, middle, hidden_two = pl.pallas_call(
        functools.partial(attn_forward_kernel, sizes),
        out_shape=(
            shape_of((row_parts, row_count, part_width)),
            shape_of((column_parts, row_count, qkv_cols)),
            shape_of((row_parts, row_count, part_width)),
            shape_of(full, F32),
            shape_of(full, F32),
            shape_of(full),
        ),
        in_specs=[SMEM_SPEC, VMEM_SPEC, VMEM_SPEC] + [ANY_SPEC] * (2 * count),
        out_specs=[VMEM_SPEC] * 6,
        scratch_shapes=weight_scratch,
        compiler_params=PARAMS,
        cost_estimate=cost(8 * row_count * width * width, 14_000_000),
        name="attn_forward",
    )(lengths, tokens, mod, *halves)

    gate_two = jnp.repeat(mod[:, 5], span, axis=0)
    d_out = (cotangent.astype(F32) * gate_two).astype(LOW)
    d_outs = {0: d_out, 1: swap(d_out, 1, count), 2: swap(d_out, 2, count)}
    d_outs[3] = swap(d_outs[2], 1, count)
    tokens_two = {0: hidden_two, 1: swap(hidden_two, 1, count), 2: swap(hidden_two, 2, count)}
    tokens_two[3] = swap(tokens_two[2], 1, count)

    def feed_call(index, kind, name):
        return pl.pallas_call(
            functools.partial(feed_kernel, 32),
            out_shape=[shape_of((row_count, hidden_part))] * 4
            + [shape_of(full, kind), shape_of(full)] * 2,
            in_specs=[VMEM_SPEC] * 4 + [ANY_SPEC] * column_parts,
            out_specs=[VMEM_SPEC] * 8,
            scratch_shapes=[
                pltpu.VMEM((hidden_part, width), LOW),
                pltpu.VMEM((width, hidden_part), LOW),
                pltpu.SemaphoreType.DMA((column_parts, 2)),
                pltpu.VMEM((row_count, hidden_part), F32),
                pltpu.VMEM((row_count, hidden_part), F32),
                pltpu.VMEM((8, 128), LOW),
                pltpu.VMEM((8, 128), LOW),
            ],
            compiler_params=PARAMS,
            cost_estimate=cost(16 * row_count * width * hidden_part, 12_000_000),
            name=name,
        )(
            tokens_two[index],
            tokens_two[index + 1],
            d_outs[index],
            d_outs[index + 1],
            *feed_blocks,
        )

    near = feed_call(0, F32, "feed_near")
    distant = feed_call(2, F32, "feed_distant")
    activ = list(near[0:2]) + list(distant[0:2])
    d_up = list(near[2:4]) + list(distant[2:4])

    def join(first, second, third, fourth):
        far = third.astype(F32) + swap(fourth, 1, count).astype(F32)
        mine = first.astype(F32) + swap(second, 1, count).astype(F32)
        return mine, swap(far.astype(LOW), 2, count)

    grad_own, grad_far = join(near[4], near[5], distant[4], distant[5])
    out_own, out_far = join(near[6], near[7], distant[6], distant[7])

    feed_grads = pl.pallas_call(
        functools.partial(feed_weight_kernel, 128),
        out_shape=[shape_of((2 * sub, width))] * column_parts,
        in_specs=[VMEM_SPEC] * 16,
        out_specs=[ANY_SPEC] * column_parts,
        scratch_shapes=[
            pltpu.VMEM((hidden_part, width), LOW),
            pltpu.VMEM((width, hidden_part), LOW),
            pltpu.SemaphoreType.DMA((column_parts, 2)),
        ],
        compiler_params=PARAMS,
        cost_estimate=cost(16 * row_count * width * hidden_part, 15_000_000),
        name="feed_weight",
    )(
        *[tokens_two[i] for i in range(4)],
        *[d_outs[i] for i in range(4)],
        *activ,
        *d_up,
    )

    input_grad, d_both, d_mod = pl.pallas_call(
        functools.partial(attn_backward_kernel, sizes),
        out_shape=(
            shape_of(full),
            shape_of((column_parts, row_count, qkv_cols + proj_cols)),
            shape_of((clips, 6, width), F32),
        ),
        in_specs=[SMEM_SPEC] + [VMEM_SPEC] * 8 + [ANY_SPEC] * (2 * count),
        out_specs=[VMEM_SPEC] * 3,
        scratch_shapes=weight_scratch
        + [
            pltpu.VMEM(full, F32),
            pltpu.VMEM((row_parts, row_count, part_width), LOW),
            pltpu.VMEM(full, F32),
        ],
        compiler_params=PARAMS,
        cost_estimate=cost(8 * row_count * width * width, 16_000_000),
        name="attn_backward",
    )(lengths, tokens, cotangent, mod, middle, branch, mixed, grad_own, grad_far, *halves)

    groups = column_parts // 2
    attn_grads = pl.pallas_call(
        functools.partial(attn_weight_kernel, (qkv_cols, proj_cols, half)),
        out_shape=[shape_of((2, half, qkv_cols + proj_cols))] * (4 * groups),
        in_specs=[VMEM_SPEC] * 6,
        out_specs=[VMEM_SPEC] * (4 * groups),
        compiler_params=PARAMS,
        cost_estimate=cost(8 * row_count * width * width, 12_000_000),
        name="attn_weight",
    )(
        hidden,
        attended,
        d_both,
        swap(hidden, 1, count),
        swap(attended, 1, count),
        swap(d_both, 1, count),
    )

    def fold(keep, send, mask):
        return keep.astype(F32) + swap(send, mask, count).astype(F32)

    def last_fold(parts):
        total = parts[0]
        for index in range(1, groups):
            got = swap(parts[index].astype(LOW), z_masks[index - 1], count)
            total = total + got.astype(F32)
        return total

    feed_sums = [
        fold(feed_grads[2 * i], feed_grads[2 * i + 1], x_mask) for i in range(groups)
    ]
    feed_sum = last_fold(feed_sums)
    back = feed_sum.astype(LOW).reshape(2, sub, row_parts, height).transpose(2, 0, 1, 3)
    back = lax.all_to_all(back, "fsdp", 0, 0, tiled=True)
    up_grad = back[:, 0].transpose(2, 0, 1).reshape(height, row_parts * sub).astype(F32)
    down_grad = (
        back[:, 1]
        .reshape(row_parts, proj_cols, -1, sub)
        .transpose(2, 0, 3, 1)
        .reshape(-1, proj_cols)
        .astype(F32)
    )

    def two_folds(keep, send, masks):
        sums = []
        for index in range(groups):
            once = fold(keep[index], send[index], masks[0])
            low = once[1].astype(LOW)
            sums.append(fold(once[0], low, masks[1]))
        return last_fold(sums)

    part = [attn_grads[i * groups : (i + 1) * groups] for i in range(4)]
    attn_sum = jnp.concatenate(
        [two_folds(part[0], part[1], (2, x_mask)), two_folds(part[2], part[3], (x_mask, 2))], 0
    )
    qkv_grad, proj_grad = attn_sum[:, :qkv_cols], attn_sum[:, qkv_cols:]

    ffn_out = out_own + out_far.astype(F32)
    result = (middle + gate_two * ffn_out).astype(LOW).reshape(inputs.shape)
    d_gate_two = jnp.sum((cotangent.astype(F32) * ffn_out).reshape(clips, span, width), axis=1)
    d_mod = d_mod.at[:, 5].set(d_gate_two)
    mod_send = d_mod.reshape(clips, column_parts, ada_cols).transpose(1, 0, 2)
    mod_send = jnp.broadcast_to(
        mod_send.reshape(column_parts, 1, clips * ada_cols),
        (column_parts, row_parts, clips * ada_cols),
    ).reshape(count, clips * ada_cols)
    d_mod_all = padded_exchange(mod_send, count).reshape(count * clips, ada_cols)
    ada_grad = lax.dot_general(
        cond_all.astype(F32),
        d_mod_all,
        (((0,), (0,)), ((), ())),
        precision=lax.Precision.HIGHEST,
        preferred_element_type=F32,
    )
    return (
        result,
        input_grad.reshape(inputs.shape),
        ada_grad,
        qkv_grad,
        proj_grad,
        up_grad,
        down_grad,
    )


def solution(mesh):
    column_parts, row_parts = mesh.shape["dp"], mesh.shape["fsdp"]
    body = general_body
    if (column_parts, row_parts) == (8, 4):
        body = functools.partial(fast_body, column_parts, row_parts)
    clip_spec = P(AXES, None, None, None)
    return jax.shard_map(
        body,
        mesh=mesh,
        in_specs=(
            clip_spec,
            clip_spec,
            P(AXES),
            P(AXES),
            P(AXES),
            P(),
            P(),
        )
        + (P("fsdp", "dp"),) * 5,
        out_specs=(clip_spec, clip_spec) + (P("fsdp", "dp"),) * 5,
        check_vma=False,
    )
```

```python
import functools
import math

import jax
import jax.numpy as jnp
from jax import lax
from jax.experimental import pallas as pl
from jax.experimental.pallas import tpu as pltpu
from jax.sharding import PartitionSpec as P

HEADS = 16
AXES = ("dp", "fsdp")
EPS = 1e-06
F32, LOW = jnp.float32, jnp.bfloat16


def norm_mod(values, shift_add, scale_mul):
    center = values - jnp.mean(values, -1, keepdims=True)
    spread = jnp.mean(center * center, -1, keepdims=True)
    return center * lax.rsqrt(spread + 1e-06) * (1.0 + scale_mul) + shift_add


def gelu_tanh(values):
    return jax.nn.gelu(values, approximate=True)


def gather_five(shards):
    row_set = (
        lax.all_gather(shards[0], "fsdp", axis=0, tiled=True),
        lax.all_gather(shards[1], "fsdp", axis=0, tiled=True),
        lax.all_gather(shards[2], "fsdp", axis=0, tiled=True),
        lax.all_gather(shards[3], "fsdp", axis=0, tiled=True),
        lax.all_gather(shards[4], "fsdp", axis=0, tiled=True),
    )
    return (
        lax.all_gather(row_set[0], "dp", axis=1, tiled=True),
        lax.all_gather(row_set[1], "dp", axis=1, tiled=True),
        lax.all_gather(row_set[2], "dp", axis=1, tiled=True),
        lax.all_gather(row_set[3], "dp", axis=1, tiled=True),
        lax.all_gather(row_set[4], "dp", axis=1, tiled=True),
    )


def scatter_five(totals):
    row_set = (
        lax.psum_scatter(
            totals[0].astype(jnp.bfloat16), "fsdp", scatter_dimension=0, tiled=True
        ).astype(jnp.float32),
        lax.psum_scatter(
            totals[1].astype(jnp.bfloat16), "fsdp", scatter_dimension=0, tiled=True
        ).astype(jnp.float32),
        lax.psum_scatter(
            totals[2].astype(jnp.bfloat16), "fsdp", scatter_dimension=0, tiled=True
        ).astype(jnp.float32),
        lax.psum_scatter(
            totals[3].astype(jnp.bfloat16), "fsdp", scatter_dimension=0, tiled=True
        ).astype(jnp.float32),
        lax.psum_scatter(
            totals[4].astype(jnp.bfloat16), "fsdp", scatter_dimension=0, tiled=True
        ).astype(jnp.float32),
    )
    return (
        lax.psum_scatter(
            row_set[0].astype(jnp.bfloat16), "dp", scatter_dimension=1, tiled=True
        ).astype(jnp.float32),
        lax.psum_scatter(
            row_set[1].astype(jnp.bfloat16), "dp", scatter_dimension=1, tiled=True
        ).astype(jnp.float32),
        lax.psum_scatter(
            row_set[2].astype(jnp.bfloat16), "dp", scatter_dimension=1, tiled=True
        ).astype(jnp.float32),
        lax.psum_scatter(
            row_set[3].astype(jnp.bfloat16), "dp", scatter_dimension=1, tiled=True
        ).astype(jnp.float32),
        lax.psum_scatter(
            row_set[4].astype(jnp.bfloat16), "dp", scatter_dimension=1, tiled=True
        ).astype(jnp.float32),
    )


def fetch_weights(ada_weight, core_shards):
    return tuple(gather_five((ada_weight,) + tuple(core_shards)))


def matmul_tn(left, right):
    return lax.dot_general(
        left, right, (((0,), (0,)), ((), ())), preferred_element_type=jnp.float32
    )


def matmul_nt(left, right):
    return lax.dot_general(
        left, right, (((1,), (1,)), ((), ())), preferred_element_type=jnp.float32
    )


def general_body(
    inputs,
    out_cotangent,
    lengths,
    timesteps,
    labels,
    time_table,
    class_table,
    ada_weight,
    qkv_weight,
    proj_weight,
    up_weight,
    down_weight,
):
    core_shards = (qkv_weight, proj_weight, up_weight, down_weight)
    clip_count, positions, frames, model_width = inputs.shape
    row_count = clip_count * positions * frames
    seq_count = clip_count * positions
    span = positions * frames
    head_size = model_width // HEADS
    attn_scale = 1.0 / math.sqrt(head_size)
    ada_full, qkv_full, proj_full, up_full, down_full = fetch_weights(ada_weight, core_shards)
    time_onehot = (timesteps[:, None] == lax.iota(jnp.int32, time_table.shape[0])[None, :]).astype(
        jnp.bfloat16
    )
    class_onehot = (labels[:, None] == lax.iota(jnp.int32, class_table.shape[0])[None, :]).astype(
        jnp.bfloat16
    )
    embedded = jnp.dot(time_onehot, time_table, preferred_element_type=jnp.float32) + jnp.dot(
        class_onehot, class_table, preferred_element_type=jnp.float32
    )
    cond_low = jax.nn.silu(embedded).astype(jnp.bfloat16)
    modulation = jnp.dot(cond_low, ada_full, preferred_element_type=jnp.float32)
    pieces = [
        modulation[:, None, offset * model_width : (offset + 1) * model_width]
        for offset in range(6)
    ]
    shift_one, scale_one, gate_one, shift_two, scale_two, gate_two = pieces
    residual = inputs.astype(jnp.float32).reshape(clip_count, span, model_width)
    hidden_one = (
        norm_mod(residual, shift_one, scale_one)
        .astype(jnp.bfloat16)
        .reshape(row_count, model_width)
    )
    mixed = jnp.dot(hidden_one, qkv_full, preferred_element_type=jnp.float32).astype(jnp.bfloat16)
    shaped = mixed.reshape(seq_count, frames, 3, HEADS, head_size)
    queries = shaped[:, :, 0]
    key_part = shaped[:, :, 1]
    value_part = shaped[:, :, 2]
    clip_live = lax.iota(jnp.int32, frames)[None, :] < lengths[:, None]
    key_live = jnp.repeat(clip_live, positions, axis=0)
    scores = (
        jnp.einsum("sqhe,skhe->shqk", queries, key_part, preferred_element_type=jnp.float32)
        * attn_scale
    )
    scores = jnp.where(key_live[:, None, None, :], scores, -1e30)
    row_max = jnp.max(scores, -1, keepdims=True)
    exp_scores = jnp.exp(scores - row_max)
    attn_probs = exp_scores / jnp.sum(exp_scores, -1, keepdims=True)
    probs_low = attn_probs.astype(jnp.bfloat16)
    attended = jnp.einsum(
        "shqk,skhe->sqhe", probs_low, value_part, preferred_element_type=jnp.float32
    )
    attended_low = attended.astype(jnp.bfloat16).reshape(row_count, model_width)
    branch = jnp.dot(attended_low, proj_full, preferred_element_type=jnp.float32).reshape(
        clip_count, span, model_width
    )
    middle = residual + gate_one * branch
    hidden_two = (
        norm_mod(middle, shift_two, scale_two).astype(jnp.bfloat16).reshape(row_count, model_width)
    )
    up_proj = jnp.dot(hidden_two, up_full, preferred_element_type=jnp.float32)
    activ_low = gelu_tanh(up_proj).astype(jnp.bfloat16)
    ffn_out = jnp.dot(activ_low, down_full, preferred_element_type=jnp.float32).reshape(
        clip_count, span, model_width
    )
    result = (middle + gate_two * ffn_out).astype(jnp.bfloat16).reshape(inputs.shape)
    ada_full, qkv_full, proj_full, up_full, down_full = fetch_weights(ada_weight, core_shards)
    grad_out = out_cotangent.astype(jnp.float32).reshape(clip_count, span, model_width)
    d_gate_two = jnp.sum(grad_out * ffn_out, axis=1)
    d_ffn = (grad_out * gate_two).astype(jnp.bfloat16).reshape(row_count, model_width)
    d_activ = matmul_nt(d_ffn, down_full)
    down_total = matmul_tn(activ_low, d_ffn)
    gelu_value, gelu_pull = jax.vjp(gelu_tanh, up_proj)
    d_up = gelu_pull(d_activ)[0].astype(jnp.bfloat16)
    d_hidden_two = matmul_nt(d_up, up_full)
    up_total = matmul_tn(hidden_two, d_up)
    norm_value, norm_pull = jax.vjp(norm_mod, middle, shift_two, scale_two)
    d_middle_norm, d_shift_two, d_scale_two = norm_pull(
        d_hidden_two.reshape(clip_count, span, model_width)
    )
    d_middle = grad_out + d_middle_norm
    d_gate_one = jnp.sum(d_middle * branch, axis=1)
    d_branch = (d_middle * gate_one).astype(jnp.bfloat16).reshape(row_count, model_width)
    d_attended = (
        matmul_nt(d_branch, proj_full)
        .astype(jnp.bfloat16)
        .reshape(seq_count, frames, HEADS, head_size)
    )
    proj_total = matmul_tn(attended_low, d_branch)
    d_value = jnp.einsum(
        "shqk,sqhe->skhe", probs_low, d_attended, preferred_element_type=jnp.float32
    )
    d_probs = jnp.einsum(
        "sqhe,skhe->shqk", d_attended, value_part, preferred_element_type=jnp.float32
    )
    d_scores = attn_probs * (d_probs - jnp.sum(attn_probs * d_probs, -1, keepdims=True))
    d_scores_low = d_scores.astype(jnp.bfloat16)
    d_query = (
        jnp.einsum("shqk,skhe->sqhe", d_scores_low, key_part, preferred_element_type=jnp.float32)
        * attn_scale
    )
    d_key = (
        jnp.einsum("shqk,sqhe->skhe", d_scores_low, queries, preferred_element_type=jnp.float32)
        * attn_scale
    )
    d_mixed = (
        jnp.stack([d_query, d_key, d_value], axis=2)
        .astype(jnp.bfloat16)
        .reshape(row_count, 3 * model_width)
    )
    d_hidden_one = matmul_nt(d_mixed, qkv_full)
    qkv_total = matmul_tn(hidden_one, d_mixed)
    norm_first, first_pull = jax.vjp(norm_mod, residual, shift_one, scale_one)
    d_input_norm, d_shift_one, d_scale_one = first_pull(
        d_hidden_one.reshape(clip_count, span, model_width)
    )
    input_grad = (d_middle + d_input_norm).astype(jnp.bfloat16).reshape(inputs.shape)
    d_modulation = jnp.concatenate(
        [
            d_shift_one[:, 0],
            d_scale_one[:, 0],
            d_gate_one,
            d_shift_two[:, 0],
            d_scale_two[:, 0],
            d_gate_two,
        ],
        axis=-1,
    )
    ada_total = jnp.dot(
        cond_low.astype(jnp.float32).T, d_modulation, precision=lax.Precision.HIGHEST
    )
    ada_grad, qkv_grad, proj_grad, up_grad, down_grad = scatter_five(
        (ada_total, qkv_total, proj_total, up_total, down_total)
    )
    return (result, input_grad, ada_grad, qkv_grad, proj_grad, up_grad, down_grad)


def dot_nn(left, right):
    return lax.dot_general(left, right, (((1,), (0,)), ((), ())), preferred_element_type=F32)


def dot_nt(left, right):
    return lax.dot_general(left, right, (((1,), (1,)), ((), ())), preferred_element_type=F32)


def dot_tn(left, right):
    return lax.dot_general(left, right, (((0,), (0,)), ((), ())), preferred_element_type=F32)


def stats(values):
    mean = jnp.mean(values, -1, keepdims=True)
    center = values - mean
    spread = jnp.mean(center * center, -1, keepdims=True)
    inverse = lax.rsqrt(spread + EPS)
    return center * inverse, inverse


def here(names):
    return lax.axis_index(names[0]), lax.axis_index(names[1])


def start_blocks(block_refs, weight_ref, sems):
    column, row = here(AXES)
    row_parts = weight_ref.shape[1]
    copies = []
    for relative, ref in enumerate(block_refs):
        copy = pltpu.make_async_copy(
            ref,
            weight_ref.at[column ^ (relative // row_parts), row ^ (relative % row_parts)],
            sems.at[relative],
        )
        copy.start()
        copies.append(copy)
    return copies


class Packing:
    def __init__(self, half, qkv_cols, proj_cols):
        self.half, self.qkv_cols, self.proj_cols = half, qkv_cols, proj_cols
        self.qkv_main, self.proj_main = qkv_cols // 128 * 128, proj_cols // 128 * 128
        self.qkv_rest, self.proj_rest = qkv_cols - self.qkv_main, proj_cols - self.proj_main
        self.rest = self.qkv_rest + self.proj_rest
        self.proj_start = 2 * self.qkv_main
        self.rest_start = self.proj_start + 2 * self.proj_main
        self.width = self.rest_start + 2 * self.rest

    def pack(self, qkv, proj):
        halves = [slice(i * self.half, (i + 1) * self.half) for i in range(2)]
        return jnp.concatenate(
            [qkv[rows, : self.qkv_main] for rows in halves]
            + [proj[rows, : self.proj_main] for rows in halves]
            + [
                piece
                for rows in halves
                for piece in (qkv[rows, self.qkv_main :], proj[rows, self.proj_main :])
            ],
            axis=1,
        )

    def qkv_of(self, block, side):
        rest = self.rest_start + side * self.rest
        return jnp.concatenate(
            [
                block[:, side * self.qkv_main : (side + 1) * self.qkv_main],
                block[:, rest : rest + self.qkv_rest],
            ],
            axis=1,
        )

    def proj_of(self, block, side):
        main = self.proj_start + side * self.proj_main
        rest = self.rest_start + side * self.rest + self.qkv_rest
        return jnp.concatenate(
            [block[:, main : main + self.proj_main], block[:, rest : rest + self.proj_rest]],
            axis=1,
        )

    def unpack(self, block):
        return tuple(
            jnp.concatenate([part(block, side) for side in range(2)], axis=0)
            for part in (self.qkv_of, self.proj_of)
        )


def pair_mask(span, frames, live):
    query = lax.broadcasted_iota(jnp.int32, (span, span), 0)
    key = lax.broadcasted_iota(jnp.int32, (span, span), 1)
    return ((query // frames) == (key // frames)) & ((key % frames) < live)


def head_probs(queries, keys, live_mask, scale):
    scores = dot_nt(queries, keys) * scale
    scores = jnp.where(live_mask, scores, -1e30)
    exp_scores = jnp.exp(scores - jnp.max(scores, -1, keepdims=True))
    return exp_scores / jnp.sum(exp_scores, -1, keepdims=True)


def head_slices(ref, which, head, rows, size):
    per = ref.shape[2] // size
    slot = which * HEADS + head
    return ref[slot // per, rows, (slot % per) * size : (slot % per + 1) * size]


def columns_of(ref, rows, index, size):
    return ref[rows, index * size : (index + 1) * size]


def attn_forward_kernel(sizes, packing, *refs):
    clips, span, frames, width, chunk = sizes
    blocks = len(refs) - 13
    lengths, tokens, mod = refs[:3]
    block_refs = refs[3 : 3 + blocks]
    hidden, mixed, probs_out, attended, branch, middle, hidden_two = refs[3 + blocks : 10 + blocks]
    weight, pieces, sems = refs[10 + blocks :]
    copies = start_blocks(block_refs, weight, sems)
    column_parts, row_parts = weight.shape[0], weight.shape[1]
    size = width // HEADS
    half, proj_cols = packing.half, packing.proj_cols
    scale = 1.0 / math.sqrt(size)

    def first_norm(step, carry):
        rows = pl.ds(pl.multiple_of(step * chunk, chunk), chunk)
        clip_mod = mod[step * chunk // span]
        unit, _ = stats(tokens[rows, :].astype(F32))
        value = (unit * (1.0 + clip_mod[1:2]) + clip_mod[0:1]).astype(LOW)
        hidden[rows, :] = value
        for index in range(2 * row_parts):
            pieces[index, rows, :] = value[:, index * half : (index + 1) * half]
        return carry

    lax.fori_loop(0, clips * span // chunk, first_norm, 0)
    column, row = here(AXES)
    for relative in range(column_parts):
        for other in range(row_parts):
            copies[relative * row_parts + other].wait()
        place = column ^ relative
        total = None
        for part in range(row_parts):
            block = weight.at[place, part]
            for side in range(2):
                term = dot_nn(pieces[2 * part + side], packing.qkv_of(block, side))
                total = term if total is None else total + term
        mixed[place] = total.astype(LOW)

    for clip in range(clips):
        rows = slice(clip * span, (clip + 1) * span)
        live_mask = pair_mask(span, frames, lengths[clip])
        for head in range(HEADS):
            probs = head_probs(
                head_slices(mixed, 0, head, rows, size),
                head_slices(mixed, 1, head, rows, size),
                live_mask,
                scale,
            )
            probs_out[clip, head] = probs
            value = dot_nn(probs.astype(LOW), head_slices(mixed, 2, head, rows, size))
            attended[rows, head * size : (head + 1) * size] = value.astype(LOW)

    for index in range(2 * row_parts):
        pieces[index] = attended[:, index * half : (index + 1) * half]
    for place in range(column_parts):
        total = None
        for part in range(row_parts):
            block = weight.at[place, part]
            for side in range(2):
                term = dot_nn(pieces[2 * part + side], packing.proj_of(block, side))
                total = term if total is None else total + term
        branch[:, place * proj_cols : (place + 1) * proj_cols] = total

    def second_norm(step, carry):
        rows = pl.ds(pl.multiple_of(step * chunk, chunk), chunk)
        clip_mod = mod[step * chunk // span]
        value = tokens[rows, :].astype(F32) + clip_mod[2:3] * branch[rows, :]
        middle[rows, :] = value
        unit, _ = stats(value)
        hidden_two[rows, :] = (unit * (1.0 + clip_mod[4:5]) + clip_mod[3:4]).astype(LOW)
        return carry

    lax.fori_loop(0, clips * span // chunk, second_norm, 0)


def norm_back(grad, values, scale_row):
    unit, inverse = stats(values)
    d_unit = grad * (1.0 + scale_row)
    d_value = inverse * (
        d_unit
        - jnp.mean(d_unit, -1, keepdims=True)
        - unit * jnp.mean(d_unit * unit, -1, keepdims=True)
    )
    return unit, d_value


def proj_backward_kernel(sizes, packing, *refs):
    clips, span, frames, width, chunk = sizes
    blocks = len(refs) - 13
    cotangent, mod, middle, branch, grad_own, grad_far = refs[:6]
    d_middle, d_branch, d_attended, d_mod = refs[6 + blocks : 10 + blocks]
    weight, pieces, sems = refs[10 + blocks :]
    copies = start_blocks(refs[6 : 6 + blocks], weight, sems)
    column_parts, row_parts = weight.shape[0], weight.shape[1]
    half, proj_cols = packing.half, packing.proj_cols
    zero_row = jnp.zeros((1, width), F32)
    steps = span // chunk
    for clip in range(clips):
        clip_mod = mod[clip]

        def second_back(step, carry, clip=clip, clip_mod=clip_mod):
            d_shift, d_scale, d_gate = carry
            rows = pl.ds(pl.multiple_of(clip * span + step * chunk, chunk), chunk)
            grad = grad_own[rows, :] + grad_far[rows, :].astype(F32)
            unit, d_value = norm_back(grad, middle[rows, :], clip_mod[4:5])
            d_value = cotangent[rows, :].astype(F32) + d_value
            d_middle[rows, :] = d_value
            low = (d_value * clip_mod[2:3]).astype(LOW)
            d_branch[rows, :] = low
            for place in range(column_parts):
                pieces[place, rows, :] = low[:, place * proj_cols : (place + 1) * proj_cols]
            return (
                d_shift + jnp.sum(grad, 0, keepdims=True),
                d_scale + jnp.sum(grad * unit, 0, keepdims=True),
                d_gate + jnp.sum(d_value * branch[rows, :], 0, keepdims=True),
            )

        sums = lax.fori_loop(0, steps, second_back, (zero_row, zero_row, zero_row))
        d_mod[clip, 0:1, :] = sums[2]
        d_mod[clip, 1:2, :] = sums[0]
        d_mod[clip, 2:3, :] = sums[1]

    for copy in copies:
        copy.wait()
    for part in range(row_parts):
        for side in range(2):
            total = None
            for place in range(column_parts):
                term = dot_nt(pieces[place], packing.proj_of(weight.at[place, part], side))
                total = term if total is None else total + term
            start = (2 * part + side) * half
            d_attended[:, start : start + half] = total.astype(LOW)


def attn_backward_kernel(sizes, *refs):
    clips, span, frames, width, qkv_cols = sizes
    mixed, probs_ref, d_attended, d_mixed = refs
    size = width // HEADS
    scale = 1.0 / math.sqrt(size)
    cols = qkv_cols // size
    for clip in range(clips):
        rows = slice(clip * span, (clip + 1) * span)
        for head in range(HEADS):
            queries = head_slices(mixed, 0, head, rows, size)
            keys = head_slices(mixed, 1, head, rows, size)
            values = head_slices(mixed, 2, head, rows, size)
            probs = probs_ref[clip, head]
            grad = columns_of(d_attended, rows, head, size)
            d_value = dot_tn(probs.astype(LOW), grad)
            d_probs = dot_nt(grad, values)
            d_scores = (probs * (d_probs - jnp.sum(probs * d_probs, -1, keepdims=True))).astype(LOW)
            d_query = dot_nn(d_scores, keys) * scale
            d_key = dot_tn(d_scores, queries) * scale
            for which, piece in enumerate((d_query, d_key, d_value)):
                slot = which * HEADS + head
                place, start = slot // cols, (slot % cols) * size
                d_mixed[place, rows, start : start + size] = piece.astype(LOW)


def qkv_backward_kernel(sizes, packing, *refs):
    clips, span, frames, width, chunk = sizes
    blocks = len(refs) - 9
    tokens, mod, d_middle, d_mixed = refs[:4]
    input_grad, d_mod = refs[4 + blocks : 6 + blocks]
    weight, d_hidden, sems = refs[6 + blocks :]
    copies = start_blocks(refs[4 : 4 + blocks], weight, sems)
    column_parts, row_parts = weight.shape[0], weight.shape[1]
    half, qkv_cols = packing.half, packing.qkv_cols
    for copy in copies:
        copy.wait()
    for part in range(row_parts):
        for side in range(2):
            total = None
            for place in range(column_parts):
                term = dot_nt(
                    d_mixed[place, :, 0:qkv_cols], packing.qkv_of(weight.at[place, part], side)
                )
                total = term if total is None else total + term
            start = (2 * part + side) * half
            d_hidden[:, start : start + half] = total
    zero_row = jnp.zeros((1, width), F32)
    for clip in range(clips):
        clip_mod = mod[clip]

        def first_back(step, carry, clip=clip, clip_mod=clip_mod):
            d_shift, d_scale = carry
            rows = pl.ds(pl.multiple_of(clip * span + step * chunk, chunk), chunk)
            grad = d_hidden[rows, :]
            unit, d_value = norm_back(grad, tokens[rows, :].astype(F32), clip_mod[1:2])
            input_grad[rows, :] = (d_middle[rows, :] + d_value).astype(LOW)
            return (
                d_shift + jnp.sum(grad, 0, keepdims=True),
                d_scale + jnp.sum(grad * unit, 0, keepdims=True),
            )

        sums = lax.fori_loop(0, span // chunk, first_back, (zero_row, zero_row))
        d_mod[clip, 0:1, :] = sums[0]
        d_mod[clip, 1:2, :] = sums[1]


def attn_weight_kernel(packing, *refs):
    own, far, outs = refs[:4], refs[4:8], refs[8:-3]
    hidden_t, attended_t, d_pieces = refs[-3:]
    half, qkv_cols, proj_cols = packing.half, packing.qkv_cols, packing.proj_cols
    row_count = own[0].shape[0]
    column_parts = own[2].shape[0]
    row_parts = own[0].shape[1] // (2 * half)
    for start, group in ((0, own), (row_count, far)):
        hidden_t[:, start : start + row_count] = group[0][...].T
        attended_t[:, start : start + row_count] = group[1][...].T
        for place in range(column_parts):
            d_pieces[place, start : start + row_count, :] = columns_of(
                group[3], slice(None), place, proj_cols
            )
    column, row = here(AXES)
    for relative in range(column_parts):
        place = column ^ relative
        d_qkv = jnp.concatenate(
            [own[2][place, :, 0:qkv_cols], far[2][place, :, 0:qkv_cols]], axis=0
        )
        d_proj = d_pieces[place]
        x_bit, z_bits = relative % 2, relative // 2
        for other in range(row_parts // 2):
            rows = pl.ds(pl.multiple_of((row ^ (2 * other)) * 2 * half, 16), 2 * half)
            qkv = dot_nn(hidden_t[rows, :], d_qkv)
            proj = dot_nn(attended_t[rows, :], d_proj)
            first, second = (other, x_bit) if z_bits % 2 == 0 else (x_bit, other)
            outs[2 * z_bits + first][second] = packing.pack(qkv, proj).astype(LOW)


def feed_kernel(chunk, *refs):
    hidden, d_outs = refs[0:2], refs[2:4]
    blocks, outs = refs[4:-13], refs[-13:-5]
    up_weight, down_weight, sems, up_proj, d_activ = refs[-5:]
    activ, d_up, d_hidden, partial = outs[0:2], outs[2:4], outs[4:6], outs[6:8]
    column, _ = here(AXES)
    copies = []
    for relative, ref in enumerate(blocks):
        half = ref.shape[0] // 2
        place = pl.ds(pl.multiple_of((column ^ relative) * half, 16), half)
        for which, weight in enumerate((up_weight, down_weight)):
            copy = pltpu.make_async_copy(
                ref.at[pl.ds(which * half, half)], weight.at[place], sems.at[relative, which]
            )
            copy.start()
            copies.append(copy)
    for copy in copies:
        copy.wait()
    tilt = math.sqrt(2.0 / math.pi)
    for index in range(2):
        up_proj[...] = dot_nt(hidden[index][...], up_weight[...])
        d_activ[...] = dot_nn(d_outs[index][...], down_weight[...])

        def gelu(step, carry, index=index):
            rows = pl.ds(pl.multiple_of(step * chunk, chunk), chunk)
            value = up_proj[rows, :]
            square = value * value
            bend = jnp.tanh(tilt * value * (1.0 + 0.044715 * square))
            activ_low = (0.5 * value * (1.0 + bend)).astype(LOW)
            slope = 0.5 * (1.0 + bend) + 0.5 * value * (1.0 - bend * bend) * (
                tilt * (1.0 + 3.0 * 0.044715 * square)
            )
            activ[index][rows, :] = activ_low
            d_up[index][rows, :] = (d_activ[rows, :] * slope).astype(LOW)
            return carry

        lax.fori_loop(0, up_proj.shape[0] // chunk, gelu, 0)
        d_hidden[index][...] = dot_nn(d_up[index][...], up_weight[...]).astype(
            d_hidden[index].dtype
        )
        partial[index][...] = dot_nt(activ[index][...], down_weight[...]).astype(
            partial[index].dtype
        )


def feed_weight_kernel(tile, *refs):
    count = (len(refs) - 3) // 2
    hidden, d_outs, activ, d_up = refs[0:4], refs[4:8], refs[8:12], refs[12:16]
    outs = refs[16:-3]
    up_grad, down_grad, sems = refs[-3:]
    column, _ = here(AXES)

    def product(step, carry):
        cols = pl.ds(pl.multiple_of(step * tile, tile), tile)
        for left, right, grad in ((d_up, hidden, up_grad), (d_outs, activ, down_grad)):
            total = dot_tn(left[0][:, cols], right[0][...])
            for index in range(1, 4):
                total += dot_tn(left[index][:, cols], right[index][...])
            grad[cols, :] = total.astype(LOW)
        return carry

    lax.fori_loop(0, up_grad.shape[0] // tile, product, 0)
    copies = []
    for relative, ref in enumerate(outs):
        half = ref.shape[0] // 2
        place = pl.ds(pl.multiple_of((column ^ relative) * half, 16), half)
        for which, grad in enumerate((up_grad, down_grad)):
            copy = pltpu.make_async_copy(
                grad.at[place], ref.at[pl.ds(which * half, half)], sems.at[relative, which]
            )
            copy.start()
            copies.append(copy)
    for copy in copies:
        copy.wait()


def prepare_kernel(packing, sub, *refs):
    timesteps, labels, time_table, class_table, qkv, proj_t, up, down_t, packed, cond, send = refs
    packed[...] = packing.pack(qkv[...], proj_t[...].T)
    row_parts = send.shape[0]
    clips = cond.shape[0]

    def look_up(indices, table):
        count = table.shape[0]
        row = lax.broadcasted_iota(jnp.int32, (16, count), 0)
        column = lax.broadcasted_iota(jnp.int32, (16, count), 1)
        picked = jnp.zeros((16, count), jnp.bool_)
        for clip in range(clips):
            picked = picked | ((row == clip) & (column == indices[clip]))
        return dot_nn(picked.astype(F32).astype(LOW), table[...])

    embedded = look_up(timesteps, time_table) + look_up(labels, class_table)
    cond[...] = (embedded * (1.0 / (1.0 + jnp.exp(-embedded))))[:clips].astype(LOW)
    up_t = up[...].T
    pairs = send.shape[3] // sub
    for part in range(row_parts):
        send[part, 0] = up_t[part * sub : (part + 1) * sub, :]
        for pair in range(pairs):
            start = (pair * row_parts + part) * sub
            send[part, 1, :, pair * sub : (pair + 1) * sub] = down_t[:, start : start + sub]


VMEM_SPEC = pl.BlockSpec(memory_space=pltpu.VMEM)
SMEM_SPEC = pl.BlockSpec(memory_space=pltpu.SMEM)
ANY_SPEC = pl.BlockSpec(memory_space=pl.ANY)
PARAMS = pltpu.CompilerParams(vmem_limit_bytes=56 * 1024 * 1024)


def shape_of(dims, kind=LOW):
    return jax.ShapeDtypeStruct(dims, kind)


def cost(micros):
    return pl.CostEstimate(flops=1000, bytes_accessed=int(micros * 3_000_000), transcendentals=0)


def after(value, *others):
    return lax.optimization_barrier((value,) + others)[0]


def swap(value, mask, count):
    return lax.ppermute(value, AXES, [(i, i ^ mask) for i in range(count)])


def padded_exchange(rows, count):
    length = rows.shape[1]
    tiles = -(-length // 1024) * 8
    rows = jnp.pad(rows, ((0, 0), (0, tiles * 128 - length))).reshape(count, tiles, 128)
    got = lax.all_to_all(rows, AXES, 0, 0, tiled=True)
    return got.reshape(count, tiles * 128)[:, :length]


def fast_body(
    column_parts,
    row_parts,
    inputs,
    out_cotangent,
    lengths,
    timesteps,
    labels,
    time_table,
    class_table,
    ada_weight,
    qkv_weight,
    proj_weight,
    up_weight,
    down_weight,
):
    count = column_parts * row_parts
    clips, positions, frames, width = inputs.shape
    span = positions * frames
    row_count = clips * span
    qkv_cols, proj_cols = qkv_weight.shape[1], proj_weight.shape[1]
    height = qkv_weight.shape[0]
    part_width = width // row_parts
    hidden_part = up_weight.shape[1] * column_parts // row_parts
    sub = up_weight.shape[1] // row_parts
    x_mask = row_parts
    z_masks = tuple(row_parts * 2 * i for i in range(1, column_parts // 2))
    packing = Packing(height // 2, qkv_cols, proj_cols)

    packed, cond_low, both_send = pl.pallas_call(
        functools.partial(prepare_kernel, packing, sub),
        out_shape=(
            shape_of((height // 2, packing.width)),
            shape_of((clips, width)),
            shape_of((row_parts, 2, sub, height)),
        ),
        in_specs=[SMEM_SPEC] * 2 + [VMEM_SPEC] * 6,
        out_specs=[VMEM_SPEC] * 3,
        compiler_params=PARAMS,
        cost_estimate=cost(3),
        name="prepare",
    )(timesteps, labels, time_table, class_table, qkv_weight, proj_weight.T, up_weight, down_weight.T)

    z_one, z_two, z_three = z_masks
    y_mask, c_mask = 2, 1
    ada_cols = ada_weight.shape[1]
    have = {0: packed}

    def move(mask, *sources):
        for source in sources:
            have[source ^ mask] = swap(have[source], mask, count)
        return [source ^ mask for source in sources]

    def close(keys, *others):
        got = lax.optimization_barrier(tuple(have[key] for key in keys) + others)
        have.update(zip(keys, got))
        return got[len(keys) :]

    for mask in z_masks + (x_mask, y_mask):
        move(mask, 0)
    cond_send = cond_low.reshape(clips, row_parts, part_width).transpose(1, 0, 2)
    cond_send = jnp.broadcast_to(
        cond_send.reshape(1, row_parts, clips * part_width),
        (column_parts, row_parts, clips * part_width),
    ).reshape(count, clips * part_width)
    cond_all = padded_exchange(cond_send, count).reshape(count * clips, part_width)
    cond_all, both_send = close([z_one, x_mask, y_mask], cond_all, both_send)

    mod_part = jnp.dot(cond_all, ada_weight, preferred_element_type=F32)
    mod_got = padded_exchange(mod_part.reshape(count, clips * ada_cols), count)
    both_got = lax.all_to_all(both_send, "fsdp", 0, 0, tiled=True)
    own_feed = both_got.transpose(1, 2, 0, 3).reshape(2 * sub, width)
    keys = move(x_mask, z_one) + move(y_mask, z_one, x_mask) + move(c_mask, 0, x_mask, y_mask)
    mod_got, own_feed = close(keys + [z_two, z_three], mod_got, own_feed)
    mod_own = jnp.sum(mod_got.reshape(column_parts, row_parts, clips, ada_cols), axis=1)
    mod = mod_own.transpose(1, 0, 2).reshape(clips, 6, width)

    z_of = [i // (2 * row_parts) for i in range(count)]
    inner = [i for i in range(count) if z_of[i] in (1, 2)]

    def inner_pairs(mask):
        return [(i, i ^ mask) for i in inner]

    feed = {0: own_feed, z_one: swap(own_feed, z_one, count)}
    feed_inner = lax.ppermute(own_feed, AXES, inner_pairs(z_three))
    feed[x_mask] = swap(own_feed, x_mask, count)
    keys = move(x_mask, z_two, z_three) + move(y_mask, z_two, z_one ^ x_mask)
    keys += move(c_mask, z_one, z_one ^ x_mask, z_one ^ y_mask, x_mask ^ y_mask)
    feed[z_one], feed_inner, feed[x_mask] = close(keys, feed[z_one], feed_inner, feed[x_mask])

    feed_two = lax.ppermute(feed[z_one], AXES, inner_pairs(z_three))
    feed_two_outer = lax.ppermute(feed_inner, AXES, inner_pairs(z_one))
    feed[z_one ^ x_mask] = swap(feed[z_one], x_mask, count)
    keys = move(y_mask, z_two ^ x_mask, z_three)
    keys += move(
        c_mask, z_two, z_two ^ x_mask, z_two ^ y_mask, z_three, z_three ^ x_mask, z_one ^ x_mask ^ y_mask
    )
    feed_two, feed_two_outer, feed[z_one ^ x_mask] = close(
        keys, feed_two, feed_two_outer, feed[z_one ^ x_mask]
    )
    feed[z_two] = feed_two + feed_two_outer
    feed_three = lax.ppermute(feed[z_two], AXES, inner_pairs(z_one))
    feed[z_two ^ x_mask] = swap(feed[z_two], x_mask, count)
    move(y_mask, z_three ^ x_mask)
    move(c_mask, z_two ^ x_mask ^ y_mask, z_three ^ y_mask)
    move(c_mask, z_three ^ x_mask ^ y_mask)
    feed[z_three] = feed_inner + feed_three
    feed[z_three ^ x_mask] = swap(feed[z_three], x_mask, count)
    blocks = [have[i] for i in range(count)]
    feed_blocks = [feed[i * row_parts] for i in range(column_parts)]

    tokens = inputs.reshape(row_count, width)
    cotangent = out_cotangent.reshape(row_count, width)
    sizes = (clips, span, frames, width, 32)
    full = (row_count, width)
    weight_scratch = pltpu.VMEM((column_parts, row_parts, height // 2, packing.width), LOW)
    weight_sems = pltpu.SemaphoreType.DMA((count,))
    hidden, mixed, probs, attended, branch, middle, hidden_two = pl.pallas_call(
        functools.partial(attn_forward_kernel, sizes, packing),
        out_shape=(
            shape_of(full),
            shape_of((column_parts, row_count, qkv_cols)),
            shape_of((clips, HEADS, span, span), F32),
            shape_of(full),
            shape_of(full, F32),
            shape_of(full, F32),
            shape_of(full),
        ),
        in_specs=[SMEM_SPEC, VMEM_SPEC, VMEM_SPEC] + [ANY_SPEC] * count,
        out_specs=[VMEM_SPEC] * 7,
        scratch_shapes=[
            weight_scratch,
            pltpu.VMEM((2 * row_parts, row_count, height // 2), LOW),
            weight_sems,
        ],
        compiler_params=PARAMS,
        cost_estimate=cost(20),
        name="attn_forward",
    )(lengths, tokens, mod, *blocks)

    gate_two = jnp.repeat(mod[:, 5], span, axis=0)
    d_out = (cotangent.astype(F32) * gate_two).astype(LOW)
    d_outs = {0: d_out, 1: swap(d_out, 1, count), 2: swap(d_out, 2, count)}
    d_outs[3] = swap(d_outs[2], 1, count)
    tokens_two = {0: hidden_two, 1: swap(hidden_two, 1, count), 2: swap(hidden_two, 2, count)}

    def feed_call(index, kind, name):
        return pl.pallas_call(
            functools.partial(feed_kernel, 32),
            out_shape=[shape_of((row_count, hidden_part))] * 4
            + [shape_of(full, kind), shape_of(full)] * 2,
            in_specs=[VMEM_SPEC] * 4 + [ANY_SPEC] * column_parts,
            out_specs=[VMEM_SPEC] * 8,
            scratch_shapes=[
                pltpu.VMEM((hidden_part, width), LOW),
                pltpu.VMEM((width, hidden_part), LOW),
                pltpu.SemaphoreType.DMA((column_parts, 2)),
                pltpu.VMEM((row_count, hidden_part), F32),
                pltpu.VMEM((row_count, hidden_part), F32),
            ],
            compiler_params=PARAMS,
            cost_estimate=cost(14),
            name=name,
        )(
            tokens_two[index],
            tokens_two[index + 1],
            d_outs[index],
            d_outs[index + 1],
            *feed_blocks,
        )

    near = feed_call(0, F32, "feed_near")
    tokens_two[2] = after(tokens_two[2], near[0])
    tokens_two[3] = swap(tokens_two[2], 1, count)
    distant = feed_call(2, F32, "feed_distant")
    activ = list(near[0:2]) + list(distant[0:2])
    d_up = list(near[2:4]) + list(distant[2:4])

    def join(first, second, third, fourth):
        far = third.astype(F32) + swap(fourth, 1, count).astype(F32)
        mine = first.astype(F32) + swap(second, 1, count).astype(F32)
        return mine, far.astype(LOW)

    grad_own, grad_send = join(near[4], near[5], distant[4], distant[5])
    out_own, out_send = join(near[6], near[7], distant[6], distant[7])
    grad_far = swap(grad_send, 2, count)
    out_far = swap(after(out_send, grad_far), 2, count)

    feed_grads = pl.pallas_call(
        functools.partial(feed_weight_kernel, 128),
        out_shape=[shape_of((2 * sub, width))] * column_parts,
        in_specs=[VMEM_SPEC] * 16,
        out_specs=[ANY_SPEC] * column_parts,
        scratch_shapes=[
            pltpu.VMEM((hidden_part, width), LOW),
            pltpu.VMEM((width, hidden_part), LOW),
            pltpu.SemaphoreType.DMA((column_parts, 2)),
        ],
        compiler_params=PARAMS,
        cost_estimate=cost(14),
        name="feed_weight",
    )(
        after(tokens_two[0], grad_send),
        *[tokens_two[i] for i in range(1, 4)],
        *[d_outs[i] for i in range(4)],
        *activ,
        *d_up,
    )

    groups = column_parts // 2

    def fold(keep, got):
        return keep.astype(F32) + got.astype(F32)

    feed_x = {i: swap(feed_grads[2 * i + 1], x_mask, count) for i in reversed(range(groups))}
    feed_sums = {i: fold(feed_grads[2 * i], feed_x[i]) for i in range(groups)}
    feed_z = {i: swap(feed_sums[i].astype(LOW), z_masks[i - 1], count) for i in range(1, groups)}

    d_middle, d_branch, d_attended, d_mod_two = pl.pallas_call(
        functools.partial(proj_backward_kernel, sizes, packing),
        out_shape=(
            shape_of(full, F32),
            shape_of(full),
            shape_of(full),
            shape_of((clips, 3, width), F32),
        ),
        in_specs=[VMEM_SPEC] * 6 + [ANY_SPEC] * count,
        out_specs=[VMEM_SPEC] * 4,
        scratch_shapes=[
            weight_scratch,
            pltpu.VMEM((column_parts, row_count, proj_cols), LOW),
            weight_sems,
        ],
        compiler_params=PARAMS,
        cost_estimate=cost(10),
        name="proj_backward",
    )(cotangent, mod, middle, branch, grad_own, grad_far, *blocks)

    d_mixed = pl.pallas_call(
        functools.partial(attn_backward_kernel, (clips, span, frames, width, qkv_cols)),
        out_shape=shape_of((column_parts, row_count, -(-qkv_cols // 128) * 128)),
        in_specs=[VMEM_SPEC] * 3,
        out_specs=VMEM_SPEC,
        compiler_params=PARAMS,
        cost_estimate=cost(15),
        name="attn_backward",
    )(mixed, probs, after(d_attended, feed_x[3]))

    input_grad, d_mod_one = pl.pallas_call(
        functools.partial(qkv_backward_kernel, sizes, packing),
        out_shape=(shape_of(full), shape_of((clips, 2, width), F32)),
        in_specs=[VMEM_SPEC] * 4 + [ANY_SPEC] * count,
        out_specs=[VMEM_SPEC] * 2,
        scratch_shapes=[weight_scratch, pltpu.VMEM(full, F32), weight_sems],
        compiler_params=PARAMS,
        cost_estimate=cost(14),
        name="qkv_backward",
    )(tokens, mod, d_middle, after(d_mixed, feed_x[2]), *blocks)

    own_side = (hidden, attended, d_mixed, d_branch)
    attn_grads = pl.pallas_call(
        functools.partial(attn_weight_kernel, packing),
        out_shape=[shape_of((2, height // 2, packing.width))] * (2 * groups),
        in_specs=[VMEM_SPEC] * 8,
        out_specs=[VMEM_SPEC] * (2 * groups),
        scratch_shapes=[
            pltpu.VMEM((width, 2 * row_count), LOW),
            pltpu.VMEM((width, 2 * row_count), LOW),
            pltpu.VMEM((column_parts, 2 * row_count, proj_cols), LOW),
        ],
        compiler_params=PARAMS,
        cost_estimate=cost(10),
        name="attn_weight",
    )(
        hidden,
        attended,
        after(d_mixed, input_grad, feed_x[1], feed_z[3]),
        d_branch,
        *[swap(array, 1, count) for array in own_side],
    )

    orders = [(y_mask, x_mask) if index % 2 == 0 else (x_mask, y_mask) for index in range(groups)]
    first = {i: swap(attn_grads[2 * i + 1], orders[i][0], count) for i in range(groups)}
    first[3], first[2] = lax.optimization_barrier((first[3], first[2]))
    once = {i: fold(attn_grads[2 * i], first[i]) for i in range(groups)}
    second = {i: swap(once[i][1].astype(LOW), orders[i][1], count) for i in range(groups)}
    second[3], second[2], first_one, first_zero = lax.optimization_barrier(
        (second[3], second[2], first[1], first[0])
    )
    for i, got in ((1, first_one), (0, first_zero)):
        once[i] = fold(attn_grads[2 * i], got)
        second[i] = swap(once[i][1].astype(LOW), orders[i][1], count)
    attn_sums = [fold(once[i][0], second[i]) for i in range(groups)]
    attn_sum = attn_sums[0]
    for i in range(1, groups):
        attn_sum += swap(attn_sums[i].astype(LOW), z_masks[i - 1], count).astype(F32)
    qkv_grad, proj_grad = packing.unpack(attn_sum)

    feed_z[2] = after(feed_z[2], second[3])
    feed_sum = feed_sums[0] + sum(got.astype(F32) for got in feed_z.values())
    back = feed_sum.astype(LOW).reshape(2, sub, row_parts, height).transpose(2, 0, 1, 3)
    back = lax.all_to_all(back, "fsdp", 0, 0, tiled=True)
    up_grad = back[:, 0].transpose(2, 0, 1).reshape(height, row_parts * sub).astype(F32)
    down_grad = (
        back[:, 1]
        .reshape(row_parts, proj_cols, -1, sub)
        .transpose(2, 0, 3, 1)
        .reshape(-1, proj_cols)
        .astype(F32)
    )

    ffn_out = out_own + out_far.astype(F32)
    result = (middle + gate_two * ffn_out).astype(LOW).reshape(inputs.shape)
    d_gate_two = jnp.sum((cotangent.astype(F32) * ffn_out).reshape(clips, span, width), axis=1)
    d_mod = jnp.concatenate([d_mod_one, d_mod_two, d_gate_two[:, None]], axis=1)
    mod_send = d_mod.reshape(clips, column_parts, ada_cols).transpose(1, 0, 2)
    mod_send = jnp.broadcast_to(
        mod_send.reshape(column_parts, 1, clips * ada_cols),
        (column_parts, row_parts, clips * ada_cols),
    ).reshape(count, clips * ada_cols)
    d_mod_all = padded_exchange(mod_send, count).reshape(count * clips, ada_cols)
    ada_grad = lax.dot_general(
        cond_all.astype(F32),
        d_mod_all,
        (((0,), (0,)), ((), ())),
        precision=lax.Precision.HIGHEST,
        preferred_element_type=F32,
    )
    return (
        result,
        input_grad.reshape(inputs.shape),
        ada_grad,
        qkv_grad,
        proj_grad,
        up_grad,
        down_grad,
    )


def solution(mesh):
    column_parts, row_parts = mesh.shape["dp"], mesh.shape["fsdp"]
    body = general_body
    if (column_parts, row_parts) == (8, 4):
        body = functools.partial(fast_body, column_parts, row_parts)
    clip_spec = P(AXES, None, None, None)
    return jax.shard_map(
        body,
        mesh=mesh,
        in_specs=(
            clip_spec,
            clip_spec,
            P(AXES),
            P(AXES),
            P(AXES),
            P(),
            P(),
        )
        + (P("fsdp", "dp"),) * 5,
        out_specs=(clip_spec, clip_spec) + (P("fsdp", "dp"),) * 5,
        check_vma=False,
    )
```

```python
import functools
import math

import jax
import jax.numpy as jnp
from jax import lax
from jax.experimental import pallas as pl
from jax.experimental.pallas import tpu as pltpu
from jax.sharding import PartitionSpec as P

HEADS = 16
AXES = ("dp", "fsdp")
EPS = 1e-06
F32, LOW = jnp.float32, jnp.bfloat16
SCALE = 100


def norm_mod(values, shift_add, scale_mul):
    center = values - jnp.mean(values, -1, keepdims=True)
    spread = jnp.mean(center * center, -1, keepdims=True)
    return center * lax.rsqrt(spread + 1e-06) * (1.0 + scale_mul) + shift_add


def gelu_tanh(values):
    return jax.nn.gelu(values, approximate=True)


def gather_five(shards):
    row_set = (
        lax.all_gather(shards[0], "fsdp", axis=0, tiled=True),
        lax.all_gather(shards[1], "fsdp", axis=0, tiled=True),
        lax.all_gather(shards[2], "fsdp", axis=0, tiled=True),
        lax.all_gather(shards[3], "fsdp", axis=0, tiled=True),
        lax.all_gather(shards[4], "fsdp", axis=0, tiled=True),
    )
    return (
        lax.all_gather(row_set[0], "dp", axis=1, tiled=True),
        lax.all_gather(row_set[1], "dp", axis=1, tiled=True),
        lax.all_gather(row_set[2], "dp", axis=1, tiled=True),
        lax.all_gather(row_set[3], "dp", axis=1, tiled=True),
        lax.all_gather(row_set[4], "dp", axis=1, tiled=True),
    )


def scatter_five(totals):
    row_set = (
        lax.psum_scatter(
            totals[0].astype(jnp.bfloat16), "fsdp", scatter_dimension=0, tiled=True
        ).astype(jnp.float32),
        lax.psum_scatter(
            totals[1].astype(jnp.bfloat16), "fsdp", scatter_dimension=0, tiled=True
        ).astype(jnp.float32),
        lax.psum_scatter(
            totals[2].astype(jnp.bfloat16), "fsdp", scatter_dimension=0, tiled=True
        ).astype(jnp.float32),
        lax.psum_scatter(
            totals[3].astype(jnp.bfloat16), "fsdp", scatter_dimension=0, tiled=True
        ).astype(jnp.float32),
        lax.psum_scatter(
            totals[4].astype(jnp.bfloat16), "fsdp", scatter_dimension=0, tiled=True
        ).astype(jnp.float32),
    )
    return (
        lax.psum_scatter(
            row_set[0].astype(jnp.bfloat16), "dp", scatter_dimension=1, tiled=True
        ).astype(jnp.float32),
        lax.psum_scatter(
            row_set[1].astype(jnp.bfloat16), "dp", scatter_dimension=1, tiled=True
        ).astype(jnp.float32),
        lax.psum_scatter(
            row_set[2].astype(jnp.bfloat16), "dp", scatter_dimension=1, tiled=True
        ).astype(jnp.float32),
        lax.psum_scatter(
            row_set[3].astype(jnp.bfloat16), "dp", scatter_dimension=1, tiled=True
        ).astype(jnp.float32),
        lax.psum_scatter(
            row_set[4].astype(jnp.bfloat16), "dp", scatter_dimension=1, tiled=True
        ).astype(jnp.float32),
    )


def fetch_weights(ada_weight, core_shards):
    return tuple(gather_five((ada_weight,) + tuple(core_shards)))


def matmul_tn(left, right):
    return lax.dot_general(
        left, right, (((0,), (0,)), ((), ())), preferred_element_type=jnp.float32
    )


def matmul_nt(left, right):
    return lax.dot_general(
        left, right, (((1,), (1,)), ((), ())), preferred_element_type=jnp.float32
    )


def general_body(
    inputs,
    out_cotangent,
    lengths,
    timesteps,
    labels,
    time_table,
    class_table,
    ada_weight,
    qkv_weight,
    proj_weight,
    up_weight,
    down_weight,
):
    core_shards = (qkv_weight, proj_weight, up_weight, down_weight)
    clip_count, positions, frames, model_width = inputs.shape
    row_count = clip_count * positions * frames
    seq_count = clip_count * positions
    span = positions * frames
    head_size = model_width // HEADS
    attn_scale = 1.0 / math.sqrt(head_size)
    ada_full, qkv_full, proj_full, up_full, down_full = fetch_weights(ada_weight, core_shards)
    time_onehot = (timesteps[:, None] == lax.iota(jnp.int32, time_table.shape[0])[None, :]).astype(
        jnp.bfloat16
    )
    class_onehot = (labels[:, None] == lax.iota(jnp.int32, class_table.shape[0])[None, :]).astype(
        jnp.bfloat16
    )
    embedded = jnp.dot(time_onehot, time_table, preferred_element_type=jnp.float32) + jnp.dot(
        class_onehot, class_table, preferred_element_type=jnp.float32
    )
    cond_low = jax.nn.silu(embedded).astype(jnp.bfloat16)
    modulation = jnp.dot(cond_low, ada_full, preferred_element_type=jnp.float32)
    pieces = [
        modulation[:, None, offset * model_width : (offset + 1) * model_width]
        for offset in range(6)
    ]
    shift_one, scale_one, gate_one, shift_two, scale_two, gate_two = pieces
    residual = inputs.astype(jnp.float32).reshape(clip_count, span, model_width)
    hidden_one = (
        norm_mod(residual, shift_one, scale_one)
        .astype(jnp.bfloat16)
        .reshape(row_count, model_width)
    )
    mixed = jnp.dot(hidden_one, qkv_full, preferred_element_type=jnp.float32).astype(jnp.bfloat16)
    shaped = mixed.reshape(seq_count, frames, 3, HEADS, head_size)
    queries = shaped[:, :, 0]
    key_part = shaped[:, :, 1]
    value_part = shaped[:, :, 2]
    clip_live = lax.iota(jnp.int32, frames)[None, :] < lengths[:, None]
    key_live = jnp.repeat(clip_live, positions, axis=0)
    scores = (
        jnp.einsum("sqhe,skhe->shqk", queries, key_part, preferred_element_type=jnp.float32)
        * attn_scale
    )
    scores = jnp.where(key_live[:, None, None, :], scores, -1e30)
    row_max = jnp.max(scores, -1, keepdims=True)
    exp_scores = jnp.exp(scores - row_max)
    attn_probs = exp_scores / jnp.sum(exp_scores, -1, keepdims=True)
    probs_low = attn_probs.astype(jnp.bfloat16)
    attended = jnp.einsum(
        "shqk,skhe->sqhe", probs_low, value_part, preferred_element_type=jnp.float32
    )
    attended_low = attended.astype(jnp.bfloat16).reshape(row_count, model_width)
    branch = jnp.dot(attended_low, proj_full, preferred_element_type=jnp.float32).reshape(
        clip_count, span, model_width
    )
    middle = residual + gate_one * branch
    hidden_two = (
        norm_mod(middle, shift_two, scale_two).astype(jnp.bfloat16).reshape(row_count, model_width)
    )
    up_proj = jnp.dot(hidden_two, up_full, preferred_element_type=jnp.float32)
    activ_low = gelu_tanh(up_proj).astype(jnp.bfloat16)
    ffn_out = jnp.dot(activ_low, down_full, preferred_element_type=jnp.float32).reshape(
        clip_count, span, model_width
    )
    result = (middle + gate_two * ffn_out).astype(jnp.bfloat16).reshape(inputs.shape)
    ada_full, qkv_full, proj_full, up_full, down_full = fetch_weights(ada_weight, core_shards)
    grad_out = out_cotangent.astype(jnp.float32).reshape(clip_count, span, model_width)
    d_gate_two = jnp.sum(grad_out * ffn_out, axis=1)
    d_ffn = (grad_out * gate_two).astype(jnp.bfloat16).reshape(row_count, model_width)
    d_activ = matmul_nt(d_ffn, down_full)
    down_total = matmul_tn(activ_low, d_ffn)
    gelu_value, gelu_pull = jax.vjp(gelu_tanh, up_proj)
    d_up = gelu_pull(d_activ)[0].astype(jnp.bfloat16)
    d_hidden_two = matmul_nt(d_up, up_full)
    up_total = matmul_tn(hidden_two, d_up)
    norm_value, norm_pull = jax.vjp(norm_mod, middle, shift_two, scale_two)
    d_middle_norm, d_shift_two, d_scale_two = norm_pull(
        d_hidden_two.reshape(clip_count, span, model_width)
    )
    d_middle = grad_out + d_middle_norm
    d_gate_one = jnp.sum(d_middle * branch, axis=1)
    d_branch = (d_middle * gate_one).astype(jnp.bfloat16).reshape(row_count, model_width)
    d_attended = (
        matmul_nt(d_branch, proj_full)
        .astype(jnp.bfloat16)
        .reshape(seq_count, frames, HEADS, head_size)
    )
    proj_total = matmul_tn(attended_low, d_branch)
    d_value = jnp.einsum(
        "shqk,sqhe->skhe", probs_low, d_attended, preferred_element_type=jnp.float32
    )
    d_probs = jnp.einsum(
        "sqhe,skhe->shqk", d_attended, value_part, preferred_element_type=jnp.float32
    )
    d_scores = attn_probs * (d_probs - jnp.sum(attn_probs * d_probs, -1, keepdims=True))
    d_scores_low = d_scores.astype(jnp.bfloat16)
    d_query = (
        jnp.einsum("shqk,skhe->sqhe", d_scores_low, key_part, preferred_element_type=jnp.float32)
        * attn_scale
    )
    d_key = (
        jnp.einsum("shqk,sqhe->skhe", d_scores_low, queries, preferred_element_type=jnp.float32)
        * attn_scale
    )
    d_mixed = (
        jnp.stack([d_query, d_key, d_value], axis=2)
        .astype(jnp.bfloat16)
        .reshape(row_count, 3 * model_width)
    )
    d_hidden_one = matmul_nt(d_mixed, qkv_full)
    qkv_total = matmul_tn(hidden_one, d_mixed)
    norm_first, first_pull = jax.vjp(norm_mod, residual, shift_one, scale_one)
    d_input_norm, d_shift_one, d_scale_one = first_pull(
        d_hidden_one.reshape(clip_count, span, model_width)
    )
    input_grad = (d_middle + d_input_norm).astype(jnp.bfloat16).reshape(inputs.shape)
    d_modulation = jnp.concatenate(
        [
            d_shift_one[:, 0],
            d_scale_one[:, 0],
            d_gate_one,
            d_shift_two[:, 0],
            d_scale_two[:, 0],
            d_gate_two,
        ],
        axis=-1,
    )
    ada_total = jnp.dot(
        cond_low.astype(jnp.float32).T, d_modulation, precision=lax.Precision.HIGHEST
    )
    ada_grad, qkv_grad, proj_grad, up_grad, down_grad = scatter_five(
        (ada_total, qkv_total, proj_total, up_total, down_total)
    )
    return (result, input_grad, ada_grad, qkv_grad, proj_grad, up_grad, down_grad)


def dot_nn(left, right):
    return lax.dot_general(left, right, (((1,), (0,)), ((), ())), preferred_element_type=F32)


def dot_nt(left, right):
    return lax.dot_general(left, right, (((1,), (1,)), ((), ())), preferred_element_type=F32)


def dot_tn(left, right):
    return lax.dot_general(left, right, (((0,), (0,)), ((), ())), preferred_element_type=F32)


def stats(values):
    mean = jnp.mean(values, -1, keepdims=True)
    center = values - mean
    spread = jnp.mean(center * center, -1, keepdims=True)
    inverse = lax.rsqrt(spread + EPS)
    return center * inverse, inverse


def here(names):
    return lax.axis_index(names[0]), lax.axis_index(names[1])


def start_blocks(places, block_refs, weight_ref, sems):
    column, row = here(AXES)
    row_parts = weight_ref.shape[1]
    copies = {}
    for ref, held in zip(block_refs, places):
        for index, relative in enumerate(held):
            copy = pltpu.make_async_copy(
                ref.at[index],
                weight_ref.at[column ^ (relative // row_parts), row ^ (relative % row_parts)],
                sems.at[relative],
            )
            copy.start()
            copies[relative] = copy
    return [copies[relative] for relative in sorted(copies)]


class Packing:
    def __init__(self, half, qkv_cols, proj_cols):
        self.half, self.qkv_cols, self.proj_cols = half, qkv_cols, proj_cols
        self.qkv_main, self.proj_main = qkv_cols // 128 * 128, proj_cols // 128 * 128
        self.qkv_rest, self.proj_rest = qkv_cols - self.qkv_main, proj_cols - self.proj_main
        self.rest = self.qkv_rest + self.proj_rest
        self.proj_start = 2 * self.qkv_main
        self.rest_start = self.proj_start + 2 * self.proj_main
        self.width = self.rest_start + 2 * self.rest

    def pack(self, qkv, proj):
        halves = [slice(i * self.half, (i + 1) * self.half) for i in range(2)]
        return jnp.concatenate(
            [qkv[rows, : self.qkv_main] for rows in halves]
            + [proj[rows, : self.proj_main] for rows in halves]
            + [
                piece
                for rows in halves
                for piece in (qkv[rows, self.qkv_main :], proj[rows, self.proj_main :])
            ],
            axis=1,
        )

    def qkv_of(self, block, side):
        rest = self.rest_start + side * self.rest
        return jnp.concatenate(
            [
                block[:, side * self.qkv_main : (side + 1) * self.qkv_main],
                block[:, rest : rest + self.qkv_rest],
            ],
            axis=1,
        )

    def proj_of(self, block, side):
        main = self.proj_start + side * self.proj_main
        rest = self.rest_start + side * self.rest + self.qkv_rest
        return jnp.concatenate(
            [block[:, main : main + self.proj_main], block[:, rest : rest + self.proj_rest]],
            axis=1,
        )

    def unpack(self, block):
        return tuple(
            jnp.concatenate([part(block, side) for side in range(2)], axis=0)
            for part in (self.qkv_of, self.proj_of)
        )


def pair_mask(span, frames, live):
    query = lax.broadcasted_iota(jnp.int32, (span, span), 0)
    key = lax.broadcasted_iota(jnp.int32, (span, span), 1)
    return ((query // frames) == (key // frames)) & ((key % frames) < live)


def head_groups(count, size):
    return [range(start, start + size) for start in range(0, count, size)]


def head_slices(ref, which, head, rows, size):
    per = ref.shape[2] // size
    slot = which * HEADS + head
    return ref[slot // per, rows, (slot % per) * size : (slot % per + 1) * size]


def columns_of(ref, rows, index, size):
    return ref[rows, index * size : (index + 1) * size]


def join_proj(packing, weight, proj):
    for place in range(weight.shape[0]):
        start = place * packing.proj_cols
        for part in range(weight.shape[1]):
            for side in range(2):
                row = (2 * part + side) * packing.half
                proj[row : row + packing.half, start : start + packing.proj_cols] = packing.proj_of(
                    weight.at[place, part], side
                )


def attn_forward_kernel(sizes, packing, places, *refs):
    clips, span, frames, width, chunk = sizes
    blocks = len(places)
    lengths, tokens, mod = refs[:3]
    block_refs = refs[3 : 3 + blocks]
    hidden, mixed, probs_out, attended, branch, middle, hidden_two, proj = refs[3 + blocks : 11 + blocks]
    weight, branch_full, sems = refs[11 + blocks :]
    copies = start_blocks(places, block_refs, weight, sems)
    column_parts, row_parts = weight.shape[0], weight.shape[1]
    size = width // HEADS
    scale = 1.0 / math.sqrt(size)

    def first_norm(step, carry):
        rows = pl.ds(pl.multiple_of(step * chunk, chunk), chunk)
        clip_mod = mod[step * chunk // span]
        unit, _ = stats(tokens[rows, :].astype(F32))
        hidden[rows, :] = (unit * (1.0 + clip_mod[1:2]) + clip_mod[0:1]).astype(LOW)
        return carry

    lax.fori_loop(0, clips * span // chunk, first_norm, 0)
    column, row = here(AXES)
    for relative in range(column_parts):
        for other in range(row_parts):
            copies[relative * row_parts + other].wait()
        place = column ^ relative
        columns = jnp.concatenate(
            [
                packing.qkv_of(weight.at[place, part], side)
                for part in range(row_parts)
                for side in range(2)
            ],
            axis=0,
        )
        mixed[place] = dot_nn(hidden[...], columns).astype(LOW)

    for clip in range(clips):
        rows = slice(clip * span, (clip + 1) * span)
        live_mask = pair_mask(span, frames, lengths[clip])
        for group in head_groups(HEADS, 4):
            scores = [
                dot_nt(
                    head_slices(mixed, 0, head, rows, size), head_slices(mixed, 1, head, rows, size)
                )
                for head in group
            ]
            scores = [jnp.where(live_mask, score * scale, -1e30) for score in scores]
            exps = [jnp.exp(score - jnp.max(score, -1, keepdims=True)) for score in scores]
            probs = [(e * (1.0 / jnp.sum(e, -1, keepdims=True))).astype(LOW) for e in exps]
            values = [
                dot_nn(prob, head_slices(mixed, 2, head, rows, size))
                for head, prob in zip(group, probs)
            ]
            for head, prob, value in zip(group, probs, values):
                probs_out[clip, head] = prob
                attended[rows, head * size : (head + 1) * size] = value.astype(LOW)

    join_proj(packing, weight, proj)
    branch_full[...] = dot_nn(attended[...], proj[...])

    def second_norm(step, carry):
        rows = pl.ds(pl.multiple_of(step * chunk, chunk), chunk)
        clip_mod = mod[step * chunk // span]
        value = branch_full[rows, :]
        branch[rows, :] = value.astype(LOW)
        value = tokens[rows, :].astype(F32) + clip_mod[2:3] * value
        middle[rows, :] = value
        unit, _ = stats(value)
        hidden_two[rows, :] = (unit * (1.0 + clip_mod[4:5]) + clip_mod[3:4]).astype(LOW)
        return carry

    lax.fori_loop(0, clips * span // chunk, second_norm, 0)


def norm_back(grad, values, scale_row):
    unit, inverse = stats(values)
    d_unit = grad * (1.0 + scale_row)
    d_value = inverse * (
        d_unit
        - jnp.mean(d_unit, -1, keepdims=True)
        - unit * jnp.mean(d_unit * unit, -1, keepdims=True)
    )
    return unit, d_value


def proj_backward_kernel(sizes, *refs):
    clips, span, frames, width, chunk = sizes
    cotangent, mod, middle, branch, grad_own, grad_core, grad_far, proj = refs[:8]
    d_middle, d_branch, d_attended, d_mod = refs[8:]
    zero_row = jnp.zeros((1, width), F32)
    steps = span // chunk
    for clip in range(clips):
        clip_mod = mod[clip]

        def second_back(step, carry, clip=clip, clip_mod=clip_mod):
            d_shift, d_scale, d_gate = carry
            rows = pl.ds(pl.multiple_of(clip * span + step * chunk, chunk), chunk)
            grad = grad_own[rows, :] + grad_core[rows, :].astype(F32)
            grad += grad_far[rows, :].astype(F32)
            unit, d_value = norm_back(grad, middle[rows, :], clip_mod[4:5])
            d_value = cotangent[rows, :].astype(F32) + d_value
            d_middle[rows, :] = d_value
            d_branch[rows, :] = (d_value * clip_mod[2:3]).astype(LOW)
            return (
                d_shift + jnp.sum(grad, 0, keepdims=True),
                d_scale + jnp.sum(grad * unit, 0, keepdims=True),
                d_gate + jnp.sum(d_value * branch[rows, :].astype(F32), 0, keepdims=True),
            )

        sums = lax.fori_loop(0, steps, second_back, (zero_row, zero_row, zero_row))
        d_mod[clip, 0:1, :] = sums[2]
        d_mod[clip, 1:2, :] = sums[0]
        d_mod[clip, 2:3, :] = sums[1]

    d_attended[...] = dot_nt(d_branch[...], proj[...]).astype(LOW)


def attn_backward_kernel(sizes, *refs):
    clips, span, frames, width, qkv_cols = sizes
    mixed, probs_ref, d_attended, d_mixed = refs
    size = width // HEADS
    scale = 1.0 / math.sqrt(size)
    cols = qkv_cols // size
    for clip in range(clips):
        rows = slice(clip * span, (clip + 1) * span)
        for group in head_groups(HEADS, 4):
            queries, keys, values = (
                [head_slices(mixed, which, head, rows, size) for head in group]
                for which in range(3)
            )
            probs = [probs_ref[clip, head] for head in group]
            grads = [columns_of(d_attended, rows, head, size) for head in group]
            d_probs = [dot_nt(grad, value) for grad, value in zip(grads, values)]
            d_values = [dot_tn(prob, grad) for prob, grad in zip(probs, grads)]
            d_scores = []
            for prob, d_prob in zip(probs, d_probs):
                prob = prob.astype(F32)
                inner = jnp.sum(prob * d_prob, -1, keepdims=True)
                d_scores.append((prob * (d_prob - inner) * scale).astype(LOW))
            d_queries = [dot_nn(score, key) for score, key in zip(d_scores, keys)]
            d_keys = [dot_tn(score, query) for score, query in zip(d_scores, queries)]
            for which, pieces in enumerate((d_queries, d_keys, d_values)):
                for head, piece in zip(group, pieces):
                    slot = which * HEADS + head
                    place, start = slot // cols, (slot % cols) * size
                    d_mixed[place, rows, start : start + size] = piece.astype(LOW)


def qkv_backward_kernel(sizes, packing, places, *refs):
    clips, span, frames, width, chunk = sizes
    blocks = len(places)
    tokens, mod, d_middle, d_mixed = refs[:4]
    input_grad, d_mod = refs[4 + blocks : 6 + blocks]
    weight, d_hidden, sems = refs[6 + blocks :]
    copies = start_blocks(places, refs[4 : 4 + blocks], weight, sems)
    column_parts, row_parts = weight.shape[0], weight.shape[1]
    for copy in copies:
        copy.wait()
    for place in range(column_parts):
        columns = jnp.concatenate(
            [
                packing.qkv_of(weight.at[place, part], side)
                for part in range(row_parts)
                for side in range(2)
            ],
            axis=0,
        )
        term = dot_nt(d_mixed[place, :, 0 : packing.qkv_cols], columns)
        if place == 0:
            d_hidden[...] = term
        else:
            d_hidden[...] += term
    zero_row = jnp.zeros((1, width), F32)
    for clip in range(clips):
        clip_mod = mod[clip]

        def first_back(step, carry, clip=clip, clip_mod=clip_mod):
            d_shift, d_scale = carry
            rows = pl.ds(pl.multiple_of(clip * span + step * chunk, chunk), chunk)
            grad = d_hidden[rows, :]
            unit, d_value = norm_back(grad, tokens[rows, :].astype(F32), clip_mod[1:2])
            input_grad[rows, :] = (d_middle[rows, :] + d_value).astype(LOW)
            return (
                d_shift + jnp.sum(grad, 0, keepdims=True),
                d_scale + jnp.sum(grad * unit, 0, keepdims=True),
            )

        sums = lax.fori_loop(0, span // chunk, first_back, (zero_row, zero_row))
        d_mod[clip, 0:1, :] = sums[0]
        d_mod[clip, 1:2, :] = sums[1]


def attn_weight_kernel(packing, distances, *refs):
    own, far, outs = refs[:4], refs[4:8], refs[8:-3]
    hidden_t, attended_t, d_pieces = refs[-3:]
    half, qkv_cols, proj_cols = packing.half, packing.qkv_cols, packing.proj_cols
    row_count = own[0].shape[0]
    column_parts = own[2].shape[0]
    row_parts = own[0].shape[1] // (2 * half)
    for start, group in ((0, own), (row_count, far)):
        hidden_t[:, start : start + row_count] = group[0][...].T
        attended_t[:, start : start + row_count] = group[1][...].T
        for place in range(column_parts):
            d_pieces[place, start : start + row_count, :] = columns_of(
                group[3], slice(None), place, proj_cols
            )
    column, row = here(AXES)
    for index, z_bits in enumerate(distances):
        for x_bit in range(2):
            place = column ^ (2 * z_bits + x_bit)
            d_qkv = jnp.concatenate(
                [own[2][place, :, 0:qkv_cols], far[2][place, :, 0:qkv_cols]], axis=0
            )
            d_proj = d_pieces[place]
            for other in range(row_parts // 2):
                rows = pl.ds(pl.multiple_of((row ^ (2 * other)) * 2 * half, 16), 2 * half)
                qkv = dot_nn(hidden_t[rows, :], d_qkv)
                proj = dot_nn(attended_t[rows, :], d_proj)
                outs[2 * index + other][x_bit] = packing.pack(qkv, proj).astype(LOW)


def feed_kernel(chunk, parts, *refs):
    sources, stacked, outs = refs[0:4], refs[4], refs[5:13]
    hidden, d_outs, up_weight, down_weight, up_proj, d_activ, activ, d_up, wide, narrow = refs[13:23]
    in_sems, weight_sems, out_sems = refs[23:]
    rows_each = sources[0].shape[0]
    half = stacked.shape[0] // (2 * parts)
    halves = [pl.ds(index * rows_each, rows_each) for index in range(2)]

    def started(source, target, sem):
        copy = pltpu.make_async_copy(source, target, sem)
        copy.start()
        return copy

    waits = []
    for which, (target, weight) in enumerate(((hidden, up_weight), (d_outs, down_weight))):
        waits.append(
            [
                started(sources[2 * which + index], target.at[rows], in_sems.at[which, index])
                for index, rows in enumerate(halves)
            ]
            + [
                started(
                    stacked.at[pl.ds((2 * part + which) * half, half)],
                    weight.at[pl.ds(part * half, half)],
                    weight_sems.at[part, which],
                )
                for part in range(parts)
            ]
        )
    sent = []
    tilt = math.sqrt(2.0 / math.pi)
    for copy in waits[0]:
        copy.wait()
    up_proj[...] = dot_nt(hidden[...], up_weight[...])
    for copy in waits[1]:
        copy.wait()
    d_activ[...] = dot_nn(d_outs[...], down_weight[...])

    def gelu(step, carry):
        rows = pl.ds(pl.multiple_of(step * chunk, chunk), chunk)
        value = up_proj[rows, :]
        square = value * value
        bend = jnp.tanh(value * (tilt + (tilt * 0.044715) * square))
        half_value = 0.5 * value
        activ[rows, :] = (half_value + half_value * bend).astype(LOW)
        slope = (0.5 + 0.5 * bend) + half_value * (1.0 - bend * bend) * (
            tilt + (tilt * 3.0 * 0.044715) * square
        )
        d_up[rows, :] = (d_activ[rows, :] * slope).astype(LOW)
        return carry

    lax.fori_loop(0, 2 * rows_each // chunk, gelu, 0)
    for index, rows in enumerate(halves):
        sent.append(started(activ.at[rows], outs[index], out_sems.at[index]))
        sent.append(started(d_up.at[rows], outs[2 + index], out_sems.at[2 + index]))
    for which, total in enumerate(
        (lambda: dot_nn(d_up[...], up_weight[...]), lambda: dot_nt(activ[...], down_weight[...]))
    ):
        value = total()
        wide[which] = value[:rows_each]
        narrow[which] = value[rows_each:].astype(LOW)
        sent.append(started(narrow.at[which], outs[5 + 2 * which], out_sems.at[5 + 2 * which]))
        sent.append(started(wide.at[which], outs[4 + 2 * which], out_sems.at[4 + 2 * which]))
    for copy in sent:
        copy.wait()


def feed_weight_kernel(*refs):
    stacked = refs[16]
    hidden, d_outs, activ, d_up = (
        jnp.concatenate([ref[...] for ref in refs[i : i + 4]], axis=0) for i in (0, 4, 8, 12)
    )
    parts, half = stacked.shape[0], stacked.shape[1] // 2
    for side, (left, right) in enumerate(((d_up, hidden), (d_outs, activ))):
        total = dot_tn(left, right).astype(LOW)
        for part in range(parts):
            stacked[part, side * half : (side + 1) * half, :] = total[
                part * half : (part + 1) * half
            ]


def modulation_kernel(conds, ada, part_out, ordered):
    groups, rows, _ = ordered.shape
    for group in range(groups):
        ordered[group] = conds[group, 0:rows, 0 : ada.shape[0]]
        part_out[group * rows : (group + 1) * rows, :] = dot_nn(ordered[group], ada[...])


def prepare_kernel(packing, sub, clips, *refs):
    timesteps, labels, time_table, class_table, qkv, proj_t, up, down_t, packed, send = refs
    packed[...] = packing.pack(qkv[...], proj_t[...].T)
    row_parts = send.shape[0]

    def look_up(indices, table):
        count = table.shape[0]
        row = lax.broadcasted_iota(jnp.int32, (16, count), 0)
        column = lax.broadcasted_iota(jnp.int32, (16, count), 1)
        picked = jnp.zeros((16, count), jnp.bool_)
        for clip in range(clips):
            picked = picked | ((row == clip) & (column == indices[clip]))
        return dot_nn(picked.astype(F32).astype(LOW), table[...])

    embedded = look_up(timesteps, time_table) + look_up(labels, class_table)
    cond = (embedded * (1.0 / (1.0 + jnp.exp(-embedded)))).astype(LOW)
    up_t = up[...].T
    height = send.shape[2]
    pairs = height // sub
    for part in range(row_parts):
        send[part, 0:sub] = up_t[part * sub : (part + 1) * sub, :]
        send[part, 2 * sub :] = cond[:, part * height : (part + 1) * height]
        for pair in range(pairs):
            start = (pair * row_parts + part) * sub
            send[part, sub : 2 * sub, pair * sub : (pair + 1) * sub] = down_t[:, start : start + sub]


def sum_kernel(*refs):
    total = refs[0][...].astype(F32)
    for ref in refs[1:-1]:
        total += ref[...].astype(F32)
    refs[-1][...] = total.astype(refs[-1].dtype)


def split_sum_kernel(kept, got, stay, leave):
    total = kept[...].astype(F32) + got[...].astype(F32)
    stay[...] = total[0]
    leave[...] = total[1].astype(LOW)


def feed_total_kernel(*refs):
    total = refs[0][...].astype(F32)
    for ref in refs[1:-1]:
        total += ref[...].astype(F32)
    out = refs[-1]
    parts, sides, half, height = out.shape
    for part in range(parts):
        for side in range(sides):
            out[part, side] = total[
                side * half : (side + 1) * half, part * height : (part + 1) * height
            ].astype(LOW)


def feed_finish_kernel(back, up_grad, down_grad_t):
    parts, _, sub, height = back.shape
    pairs = height // sub
    for part in range(parts):
        up_grad[:, part * sub : (part + 1) * sub] = back[part, 0].astype(F32).T
        for pair in range(pairs):
            start = (pair * parts + part) * sub
            down_grad_t[:, start : start + sub] = back[
                part, 1, :, pair * sub : (pair + 1) * sub
            ].astype(F32)


def attn_finish_kernel(packing, *refs):
    total = refs[0][...].astype(F32)
    for ref in refs[1:-2]:
        total += ref[...].astype(F32)
    qkv_grad, proj_grad_t = refs[-2:]
    for side in range(2):
        rows = slice(side * packing.half, (side + 1) * packing.half)
        qkv_grad[rows, :] = packing.qkv_of(total, side)
        proj_grad_t[:, rows] = packing.proj_of(total, side).T


def out_finish_kernel(sizes, *refs):
    clips, span, chunk = sizes
    first, second, third, middle, cotangent, mod, result, d_gate = refs
    zero_row = jnp.zeros((1, middle.shape[1]), F32)
    for clip in range(clips):

        def step_rows(step, carry, clip=clip):
            rows = pl.ds(pl.multiple_of(clip * span + step * chunk, chunk), chunk)
            value = first[rows, :] + second[rows, :].astype(F32) + third[rows, :].astype(F32)
            result[rows, :] = (middle[rows, :] + mod[clip, 5:6, :] * value).astype(LOW)
            return carry + jnp.sum(cotangent[rows, :].astype(F32) * value, 0, keepdims=True)

        d_gate[clip] = lax.fori_loop(0, span // chunk, step_rows, zero_row)


VMEM_SPEC = pl.BlockSpec(memory_space=pltpu.VMEM)
SMEM_SPEC = pl.BlockSpec(memory_space=pltpu.SMEM)
ANY_SPEC = pl.BlockSpec(memory_space=pl.ANY)
PARAMS = pltpu.CompilerParams(vmem_limit_bytes=56 * 1024 * 1024)


def shape_of(dims, kind=LOW):
    return jax.ShapeDtypeStruct(dims, kind)


def cost(micros):
    return pl.CostEstimate(flops=1000, bytes_accessed=int(micros * SCALE), transcendentals=0)


def after(value, *others):
    return lax.optimization_barrier((value,) + others)[0]


class Sequence:
    def __init__(self):
        self.token = None

    def call(self, kernel, shapes, arrays, name, specs=None, scratch=(), tied=0, out_spec=None):
        arrays = list(arrays)
        if self.token is not None:
            arrays[tied] = after(arrays[tied], self.token)
        results = pl.pallas_call(
            kernel,
            out_shape=shapes,
            in_specs=specs or [VMEM_SPEC] * len(arrays),
            out_specs=jax.tree.map(lambda _: out_spec or VMEM_SPEC, shapes),
            scratch_shapes=scratch,
            compiler_params=PARAMS,
            cost_estimate=cost(1),
            name=name,
        )(*arrays)
        self.token = min(jax.tree.leaves(results), key=lambda result: result.size)
        return results

    def sum_low(self, *arrays):
        return self.call(sum_kernel, shape_of(arrays[0].shape), arrays, "sum_low")


def swap(value, mask, count):
    return lax.ppermute(value, AXES, [(i, i ^ mask) for i in range(count)])


def padded_exchange(rows, count):
    length = rows.shape[1]
    tiles = -(-length // 1024) * 8
    rows = jnp.pad(rows, ((0, 0), (0, tiles * 128 - length))).reshape(count, tiles, 128)
    got = lax.all_to_all(rows, AXES, 0, 0, tiled=True)
    return got.reshape(count, tiles * 128)[:, :length]


def fast_body(
    column_parts,
    row_parts,
    inputs,
    out_cotangent,
    lengths,
    timesteps,
    labels,
    time_table,
    class_table,
    ada_weight,
    qkv_weight,
    proj_weight,
    up_weight,
    down_weight,
):
    count = column_parts * row_parts
    clips, positions, frames, width = inputs.shape
    span = positions * frames
    row_count = clips * span
    qkv_cols, proj_cols = qkv_weight.shape[1], proj_weight.shape[1]
    height = qkv_weight.shape[0]
    part_width = width // row_parts
    hidden_part = up_weight.shape[1] * column_parts // row_parts
    sub = up_weight.shape[1] // row_parts
    x_mask = row_parts
    z_masks = tuple(row_parts * 2 * i for i in range(1, column_parts // 2))
    packing = Packing(height // 2, qkv_cols, proj_cols)

    line = Sequence()
    packed, both_send = line.call(
        functools.partial(prepare_kernel, packing, sub, clips),
        (
            shape_of((height // 2, packing.width)),
            shape_of((row_parts, 2 * sub + 16, height)),
        ),
        (timesteps, labels, time_table, class_table)
        + (qkv_weight, proj_weight.T, up_weight, down_weight.T),
        "prepare",
        [SMEM_SPEC] * 2 + [VMEM_SPEC] * 6,
    )

    y_mask, c_mask = 2, 1
    ada_cols = ada_weight.shape[1]

    def gate(*values):
        return lax.optimization_barrier(values)

    own = packed[None]
    far = [swap(own, mask, count) for mask in z_masks]
    own_x, own_y = swap(own, x_mask, count), swap(own, y_mask, count)
    both_got = lax.all_to_all(both_send, "fsdp", 0, 0, tiled=True)
    *far, own_x, own_y, both_got = gate(*far, own_x, own_y, both_got)
    own_feed = both_got[:, : 2 * sub].reshape(row_parts, 2, sub, height)
    own_feed = own_feed.transpose(1, 2, 0, 3).reshape(2 * sub, width)
    conds = both_got[:, 2 * sub : 2 * sub + clips].reshape(row_parts * clips, height)
    feed = lax.all_gather(own_feed, "dp", axis=0, tiled=True)

    far = jnp.concatenate(far)
    pads = (-row_parts * clips % 16, -height % 128)
    conds = jnp.pad(conds, ((0, pads[0]), (0, pads[1])))
    conds = jnp.broadcast_to(conds[None], (column_parts,) + conds.shape)
    conds = lax.all_to_all(conds, "dp", 0, 0, tiled=True)
    far_x, far_y = swap(far, x_mask, count), swap(far, y_mask, count)
    cores = [swap(array, c_mask, count) for array in (own, own_x, own_y, far)]
    far_x, far_y, conds, *cores = gate(far_x, far_y, conds, *cores)

    mod_part, conds = line.call(
        modulation_kernel,
        (
            shape_of((count * clips, ada_cols), F32),
            shape_of((column_parts, row_parts * clips, part_width)),
        ),
        (conds, ada_weight),
        "modulation",
    )
    cond_all = conds.reshape(count * clips, part_width)
    mod_got = padded_exchange(mod_part.reshape(count, clips * ada_cols), count)
    own_xy, far_xy = swap(own_x, y_mask, count), swap(far_x, y_mask, count)
    cores += [swap(array, c_mask, count) for array in (far_x, far_y)]
    own_xy, far_xy, mod_got, *cores = gate(own_xy, far_xy, mod_got, *cores)
    mod_own = jnp.sum(mod_got.reshape(column_parts, row_parts, clips, ada_cols), axis=1)
    mod = mod_own.transpose(1, 0, 2).reshape(clips, 6, width)
    cores += [swap(array, c_mask, count) for array in (own_xy, far_xy)]

    blocks = [own, own_x, own_y, far, far_x, far_y, own_xy, far_xy]
    places = [[0], [x_mask], [y_mask], list(z_masks)]
    places += [[z ^ side for z in z_masks] for side in (x_mask, y_mask)]
    places += [[x_mask ^ y_mask]]
    places += [[z ^ x_mask ^ y_mask for z in z_masks]]
    blocks += cores
    places += [[place ^ c_mask for place in held] for held in places]

    tokens = inputs.reshape(row_count, width)
    cotangent = out_cotangent.reshape(row_count, width)
    gate_two = jnp.repeat(mod[:, 5], span, axis=0)
    d_out = (cotangent.astype(F32) * gate_two).astype(LOW)
    d_outs = {0: d_out, 1: swap(d_out, 1, count), 2: swap(d_out, 2, count)}
    d_outs[3] = swap(d_outs[2], 1, count)
    sizes = (clips, span, frames, width, 32)
    full = (row_count, width)
    weight_scratch = pltpu.VMEM((column_parts, row_parts, height // 2, packing.width), LOW)
    weight_sems = pltpu.SemaphoreType.DMA((count,))
    hidden, mixed, probs, attended, branch, middle, hidden_two, proj_full = line.call(
        functools.partial(attn_forward_kernel, sizes, packing, places),
        (
            shape_of(full),
            shape_of((column_parts, row_count, qkv_cols)),
            shape_of((clips, HEADS, span, span)),
            shape_of(full),
            shape_of(full),
            shape_of(full, F32),
            shape_of(full),
            shape_of((width, width)),
        ),
        (lengths, tokens, mod, *blocks),
        "attn_forward",
        [SMEM_SPEC, VMEM_SPEC, VMEM_SPEC] + [ANY_SPEC] * len(blocks),
        (
            weight_scratch,
            pltpu.VMEM(full, F32),
            weight_sems,
        ),
        tied=2,
    )

    tokens_two = {0: hidden_two, 1: swap(hidden_two, 1, count), 2: swap(hidden_two, 2, count)}
    pair = (2 * row_count, width)
    pair_hidden = (2 * row_count, hidden_part)
    feed_scratch = (
        pltpu.VMEM(pair, LOW),
        pltpu.VMEM(pair, LOW),
        pltpu.VMEM((hidden_part, width), LOW),
        pltpu.VMEM((width, hidden_part), LOW),
        pltpu.VMEM(pair_hidden, F32),
        pltpu.VMEM(pair_hidden, F32),
        pltpu.VMEM(pair_hidden, LOW),
        pltpu.VMEM(pair_hidden, LOW),
        pltpu.VMEM((2,) + full, F32),
        pltpu.VMEM((2,) + full, LOW),
        pltpu.SemaphoreType.DMA((2, 2)),
        pltpu.SemaphoreType.DMA((column_parts, 2)),
        pltpu.SemaphoreType.DMA((8,)),
    )

    def feed_call(index, name):
        return line.call(
            functools.partial(feed_kernel, 32, column_parts),
            [shape_of((row_count, hidden_part))] * 4 + [shape_of(full, F32), shape_of(full)] * 2,
            (
                tokens_two[index],
                tokens_two[index + 1],
                d_outs[index],
                d_outs[index + 1],
                feed,
            ),
            name,
            [ANY_SPEC] * 5,
            feed_scratch,
            out_spec=ANY_SPEC,
        )

    near = feed_call(0, "feed_near")
    tokens_two[2] = after(tokens_two[2], line.token)
    tokens_two[3] = swap(tokens_two[2], 1, count)
    distant = feed_call(2, "feed_distant")

    grad_send = line.sum_low(distant[4], swap(distant[5], 1, count))
    grad_far = swap(grad_send, 2, count)
    grad_parts = (near[4], swap(near[5], 1, count), grad_far)
    feed_grads = line.call(
        feed_weight_kernel,
        shape_of((column_parts, 2 * sub, width)),
        [tokens_two[i] for i in range(4)]
        + [d_outs[i] for i in range(4)]
        + [*near[0:2], *distant[0:2], *near[2:4], *distant[2:4]],
        "feed_weight",
    ).reshape(2 * sub * column_parts, width)
    feed_grads, grad_far = lax.optimization_barrier((feed_grads, grad_far))
    grad_parts = grad_parts[:2] + (grad_far,)
    line.token = grad_far
    groups = column_parts // 2
    feed_sum = lax.psum_scatter(feed_grads, "dp", scatter_dimension=0, tiled=True)

    d_middle, d_branch, d_attended, d_mod_two = line.call(
        functools.partial(proj_backward_kernel, sizes),
        (
            shape_of(full, F32),
            shape_of(full),
            shape_of(full),
            shape_of((clips, 3, width), F32),
        ),
        (cotangent, mod, middle, branch, *grad_parts, proj_full),
        "proj_backward",
    )
    d_mixed = line.call(
        functools.partial(attn_backward_kernel, (clips, span, frames, width, qkv_cols)),
        shape_of((column_parts, row_count, -(-qkv_cols // 128) * 128)),
        (mixed, probs, d_attended),
        "attn_backward",
    )
    own_side = (hidden, attended, d_mixed, d_branch)
    far_side = [swap(array, 1, count) for array in own_side]
    out_send = line.sum_low(distant[6], swap(distant[7], 1, count))
    out_far = swap(out_send, 2, count)

    attn_grads, first = {}, {}
    for distances in (range(groups - 1, groups // 2 - 1, -1), range(groups // 2 - 1, -1, -1)):
        grads = line.call(
            functools.partial(attn_weight_kernel, packing, distances),
            [shape_of((2, height // 2, packing.width))] * (2 * len(distances)),
            (*own_side, *far_side),
            "attn_weight",
            scratch=(
                pltpu.VMEM((width, 2 * row_count), LOW),
                pltpu.VMEM((width, 2 * row_count), LOW),
                pltpu.VMEM((column_parts, 2 * row_count, proj_cols), LOW),
            ),
        )
        for index, distance in enumerate(distances):
            attn_grads[distance] = grads[2 * index]
            first[distance] = swap(grads[2 * index + 1], y_mask, count)
    input_grad, d_mod_one = line.call(
        functools.partial(qkv_backward_kernel, sizes, packing, places),
        (shape_of(full), shape_of((clips, 2, width), F32)),
        (tokens, mod, d_middle, d_mixed, *blocks),
        "qkv_backward",
        [VMEM_SPEC] * 4 + [ANY_SPEC] * len(blocks),
        (weight_scratch, pltpu.VMEM(full, F32), weight_sems),
    )
    block_shape = (height // 2, packing.width)
    stay, second, attn_z = {}, {}, {}

    def split_sum(index):
        stay[index], leave = line.call(
            split_sum_kernel,
            (shape_of(block_shape, F32), shape_of(block_shape)),
            (attn_grads[index], first[index]),
            "split_sum",
        )
        second[index] = swap(leave, x_mask, count)

    def attn_sum(index):
        summed = line.sum_low(stay[index], second[index])
        attn_z[index] = swap(summed, z_masks[index - 1], count)

    split_sum(3)
    split_sum(2)
    attn_sum(3)
    attn_sum(2)
    result, d_gate_two = line.call(
        functools.partial(out_finish_kernel, (clips, span, 32)),
        (shape_of(full), shape_of((clips, 1, width), F32)),
        (near[6], swap(near[7], 1, count), out_far, middle, cotangent, mod),
        "out_finish",
    )
    result = result.reshape(inputs.shape)
    d_mod = jnp.concatenate([d_mod_one, d_mod_two, d_gate_two], axis=1)
    split_sum(1)
    split_sum(0)
    attn_sum(1)
    back = line.call(
        feed_total_kernel,
        shape_of((row_parts, 2, sub, height)),
        (feed_sum,),
        "feed_total",
    )
    back = lax.all_to_all(back, "fsdp", 0, 0, tiled=True)
    up_grad, down_grad_t = line.call(
        feed_finish_kernel,
        (shape_of(up_weight.shape, F32), shape_of(down_weight.shape[::-1], F32)),
        (back,),
        "feed_finish",
    )
    down_grad = down_grad_t.T
    qkv_grad, proj_grad_t = line.call(
        functools.partial(attn_finish_kernel, packing),
        (shape_of((height, qkv_cols), F32), shape_of((proj_cols, height), F32)),
        (stay[0], second[0], attn_z[3], attn_z[2], attn_z[1]),
        "attn_finish",
    )
    proj_grad = proj_grad_t.T

    mod_send = d_mod.reshape(clips, column_parts, ada_cols).transpose(1, 0, 2)
    mod_send = jnp.broadcast_to(
        mod_send.reshape(column_parts, 1, clips * ada_cols),
        (column_parts, row_parts, clips * ada_cols),
    ).reshape(count, clips * ada_cols)
    d_mod_all = padded_exchange(mod_send, count).reshape(count * clips, ada_cols)
    ada_grad = lax.dot_general(
        cond_all.astype(F32),
        d_mod_all,
        (((0,), (0,)), ((), ())),
        precision=lax.Precision.HIGHEST,
        preferred_element_type=F32,
    )
    return (
        result,
        input_grad.reshape(inputs.shape),
        ada_grad,
        qkv_grad,
        proj_grad,
        up_grad,
        down_grad,
    )


def solution(mesh):
    column_parts, row_parts = mesh.shape["dp"], mesh.shape["fsdp"]
    body = general_body
    if (column_parts, row_parts) == (8, 4):
        body = functools.partial(fast_body, column_parts, row_parts)
    clip_spec = P(AXES, None, None, None)
    return jax.shard_map(
        body,
        mesh=mesh,
        in_specs=(
            clip_spec,
            clip_spec,
            P(AXES),
            P(AXES),
            P(AXES),
            P(),
            P(),
        )
        + (P("fsdp", "dp"),) * 5,
        out_specs=(clip_spec, clip_spec) + (P("fsdp", "dp"),) * 5,
        check_vma=False,
    )
```

```python
import functools
import math

import jax
import jax.numpy as jnp
from jax import lax
from jax.experimental import pallas as pl
from jax.experimental.pallas import tpu as pltpu
from jax.sharding import PartitionSpec as P

HEADS = 16
AXES = ("dp", "fsdp")
EPS = 1e-06
F32, LOW = jnp.float32, jnp.bfloat16
SCALE = 100


def norm_mod(values, shift_add, scale_mul):
    center = values - jnp.mean(values, -1, keepdims=True)
    spread = jnp.mean(center * center, -1, keepdims=True)
    return center * lax.rsqrt(spread + 1e-06) * (1.0 + scale_mul) + shift_add


def gelu_tanh(values):
    return jax.nn.gelu(values, approximate=True)


def gather_five(shards):
    row_set = (
        lax.all_gather(shards[0], "fsdp", axis=0, tiled=True),
        lax.all_gather(shards[1], "fsdp", axis=0, tiled=True),
        lax.all_gather(shards[2], "fsdp", axis=0, tiled=True),
        lax.all_gather(shards[3], "fsdp", axis=0, tiled=True),
        lax.all_gather(shards[4], "fsdp", axis=0, tiled=True),
    )
    return (
        lax.all_gather(row_set[0], "dp", axis=1, tiled=True),
        lax.all_gather(row_set[1], "dp", axis=1, tiled=True),
        lax.all_gather(row_set[2], "dp", axis=1, tiled=True),
        lax.all_gather(row_set[3], "dp", axis=1, tiled=True),
        lax.all_gather(row_set[4], "dp", axis=1, tiled=True),
    )


def scatter_five(totals):
    row_set = (
        lax.psum_scatter(
            totals[0].astype(jnp.bfloat16), "fsdp", scatter_dimension=0, tiled=True
        ).astype(jnp.float32),
        lax.psum_scatter(
            totals[1].astype(jnp.bfloat16), "fsdp", scatter_dimension=0, tiled=True
        ).astype(jnp.float32),
        lax.psum_scatter(
            totals[2].astype(jnp.bfloat16), "fsdp", scatter_dimension=0, tiled=True
        ).astype(jnp.float32),
        lax.psum_scatter(
            totals[3].astype(jnp.bfloat16), "fsdp", scatter_dimension=0, tiled=True
        ).astype(jnp.float32),
        lax.psum_scatter(
            totals[4].astype(jnp.bfloat16), "fsdp", scatter_dimension=0, tiled=True
        ).astype(jnp.float32),
    )
    return (
        lax.psum_scatter(
            row_set[0].astype(jnp.bfloat16), "dp", scatter_dimension=1, tiled=True
        ).astype(jnp.float32),
        lax.psum_scatter(
            row_set[1].astype(jnp.bfloat16), "dp", scatter_dimension=1, tiled=True
        ).astype(jnp.float32),
        lax.psum_scatter(
            row_set[2].astype(jnp.bfloat16), "dp", scatter_dimension=1, tiled=True
        ).astype(jnp.float32),
        lax.psum_scatter(
            row_set[3].astype(jnp.bfloat16), "dp", scatter_dimension=1, tiled=True
        ).astype(jnp.float32),
        lax.psum_scatter(
            row_set[4].astype(jnp.bfloat16), "dp", scatter_dimension=1, tiled=True
        ).astype(jnp.float32),
    )


def fetch_weights(ada_weight, core_shards):
    return tuple(gather_five((ada_weight,) + tuple(core_shards)))


def matmul_tn(left, right):
    return lax.dot_general(
        left, right, (((0,), (0,)), ((), ())), preferred_element_type=jnp.float32
    )


def matmul_nt(left, right):
    return lax.dot_general(
        left, right, (((1,), (1,)), ((), ())), preferred_element_type=jnp.float32
    )


def general_body(
    inputs,
    out_cotangent,
    lengths,
    timesteps,
    labels,
    time_table,
    class_table,
    ada_weight,
    qkv_weight,
    proj_weight,
    up_weight,
    down_weight,
):
    core_shards = (qkv_weight, proj_weight, up_weight, down_weight)
    clip_count, positions, frames, model_width = inputs.shape
    row_count = clip_count * positions * frames
    seq_count = clip_count * positions
    span = positions * frames
    head_size = model_width // HEADS
    attn_scale = 1.0 / math.sqrt(head_size)
    ada_full, qkv_full, proj_full, up_full, down_full = fetch_weights(ada_weight, core_shards)
    time_onehot = (timesteps[:, None] == lax.iota(jnp.int32, time_table.shape[0])[None, :]).astype(
        jnp.bfloat16
    )
    class_onehot = (labels[:, None] == lax.iota(jnp.int32, class_table.shape[0])[None, :]).astype(
        jnp.bfloat16
    )
    embedded = jnp.dot(time_onehot, time_table, preferred_element_type=jnp.float32) + jnp.dot(
        class_onehot, class_table, preferred_element_type=jnp.float32
    )
    cond_low = jax.nn.silu(embedded).astype(jnp.bfloat16)
    modulation = jnp.dot(cond_low, ada_full, preferred_element_type=jnp.float32)
    pieces = [
        modulation[:, None, offset * model_width : (offset + 1) * model_width]
        for offset in range(6)
    ]
    shift_one, scale_one, gate_one, shift_two, scale_two, gate_two = pieces
    residual = inputs.astype(jnp.float32).reshape(clip_count, span, model_width)
    hidden_one = (
        norm_mod(residual, shift_one, scale_one)
        .astype(jnp.bfloat16)
        .reshape(row_count, model_width)
    )
    mixed = jnp.dot(hidden_one, qkv_full, preferred_element_type=jnp.float32).astype(jnp.bfloat16)
    shaped = mixed.reshape(seq_count, frames, 3, HEADS, head_size)
    queries = shaped[:, :, 0]
    key_part = shaped[:, :, 1]
    value_part = shaped[:, :, 2]
    clip_live = lax.iota(jnp.int32, frames)[None, :] < lengths[:, None]
    key_live = jnp.repeat(clip_live, positions, axis=0)
    scores = (
        jnp.einsum("sqhe,skhe->shqk", queries, key_part, preferred_element_type=jnp.float32)
        * attn_scale
    )
    scores = jnp.where(key_live[:, None, None, :], scores, -1e30)
    row_max = jnp.max(scores, -1, keepdims=True)
    exp_scores = jnp.exp(scores - row_max)
    attn_probs = exp_scores / jnp.sum(exp_scores, -1, keepdims=True)
    probs_low = attn_probs.astype(jnp.bfloat16)
    attended = jnp.einsum(
        "shqk,skhe->sqhe", probs_low, value_part, preferred_element_type=jnp.float32
    )
    attended_low = attended.astype(jnp.bfloat16).reshape(row_count, model_width)
    branch = jnp.dot(attended_low, proj_full, preferred_element_type=jnp.float32).reshape(
        clip_count, span, model_width
    )
    middle = residual + gate_one * branch
    hidden_two = (
        norm_mod(middle, shift_two, scale_two).astype(jnp.bfloat16).reshape(row_count, model_width)
    )
    up_proj = jnp.dot(hidden_two, up_full, preferred_element_type=jnp.float32)
    activ_low = gelu_tanh(up_proj).astype(jnp.bfloat16)
    ffn_out = jnp.dot(activ_low, down_full, preferred_element_type=jnp.float32).reshape(
        clip_count, span, model_width
    )
    result = (middle + gate_two * ffn_out).astype(jnp.bfloat16).reshape(inputs.shape)
    ada_full, qkv_full, proj_full, up_full, down_full = fetch_weights(ada_weight, core_shards)
    grad_out = out_cotangent.astype(jnp.float32).reshape(clip_count, span, model_width)
    d_gate_two = jnp.sum(grad_out * ffn_out, axis=1)
    d_ffn = (grad_out * gate_two).astype(jnp.bfloat16).reshape(row_count, model_width)
    d_activ = matmul_nt(d_ffn, down_full)
    down_total = matmul_tn(activ_low, d_ffn)
    gelu_value, gelu_pull = jax.vjp(gelu_tanh, up_proj)
    d_up = gelu_pull(d_activ)[0].astype(jnp.bfloat16)
    d_hidden_two = matmul_nt(d_up, up_full)
    up_total = matmul_tn(hidden_two, d_up)
    norm_value, norm_pull = jax.vjp(norm_mod, middle, shift_two, scale_two)
    d_middle_norm, d_shift_two, d_scale_two = norm_pull(
        d_hidden_two.reshape(clip_count, span, model_width)
    )
    d_middle = grad_out + d_middle_norm
    d_gate_one = jnp.sum(d_middle * branch, axis=1)
    d_branch = (d_middle * gate_one).astype(jnp.bfloat16).reshape(row_count, model_width)
    d_attended = (
        matmul_nt(d_branch, proj_full)
        .astype(jnp.bfloat16)
        .reshape(seq_count, frames, HEADS, head_size)
    )
    proj_total = matmul_tn(attended_low, d_branch)
    d_value = jnp.einsum(
        "shqk,sqhe->skhe", probs_low, d_attended, preferred_element_type=jnp.float32
    )
    d_probs = jnp.einsum(
        "sqhe,skhe->shqk", d_attended, value_part, preferred_element_type=jnp.float32
    )
    d_scores = attn_probs * (d_probs - jnp.sum(attn_probs * d_probs, -1, keepdims=True))
    d_scores_low = d_scores.astype(jnp.bfloat16)
    d_query = (
        jnp.einsum("shqk,skhe->sqhe", d_scores_low, key_part, preferred_element_type=jnp.float32)
        * attn_scale
    )
    d_key = (
        jnp.einsum("shqk,sqhe->skhe", d_scores_low, queries, preferred_element_type=jnp.float32)
        * attn_scale
    )
    d_mixed = (
        jnp.stack([d_query, d_key, d_value], axis=2)
        .astype(jnp.bfloat16)
        .reshape(row_count, 3 * model_width)
    )
    d_hidden_one = matmul_nt(d_mixed, qkv_full)
    qkv_total = matmul_tn(hidden_one, d_mixed)
    norm_first, first_pull = jax.vjp(norm_mod, residual, shift_one, scale_one)
    d_input_norm, d_shift_one, d_scale_one = first_pull(
        d_hidden_one.reshape(clip_count, span, model_width)
    )
    input_grad = (d_middle + d_input_norm).astype(jnp.bfloat16).reshape(inputs.shape)
    d_modulation = jnp.concatenate(
        [
            d_shift_one[:, 0],
            d_scale_one[:, 0],
            d_gate_one,
            d_shift_two[:, 0],
            d_scale_two[:, 0],
            d_gate_two,
        ],
        axis=-1,
    )
    ada_total = jnp.dot(
        cond_low.astype(jnp.float32).T, d_modulation, precision=lax.Precision.HIGHEST
    )
    ada_grad, qkv_grad, proj_grad, up_grad, down_grad = scatter_five(
        (ada_total, qkv_total, proj_total, up_total, down_total)
    )
    return (result, input_grad, ada_grad, qkv_grad, proj_grad, up_grad, down_grad)


def dot_nn(left, right):
    return lax.dot_general(left, right, (((1,), (0,)), ((), ())), preferred_element_type=F32)


def dot_nt(left, right):
    return lax.dot_general(left, right, (((1,), (1,)), ((), ())), preferred_element_type=F32)


def dot_tn(left, right):
    return lax.dot_general(left, right, (((0,), (0,)), ((), ())), preferred_element_type=F32)


def stats(values):
    mean = jnp.mean(values, -1, keepdims=True)
    center = values - mean
    spread = jnp.mean(center * center, -1, keepdims=True)
    inverse = lax.rsqrt(spread + EPS)
    return center * inverse, inverse


def here(names):
    return lax.axis_index(names[0]), lax.axis_index(names[1])


def start_blocks(places, block_refs, weight_ref, sems):
    column, row = here(AXES)
    row_parts = weight_ref.shape[1]
    copies = {}
    for ref, held in zip(block_refs, places):
        for index, relative in enumerate(held):
            copy = pltpu.make_async_copy(
                ref.at[index],
                weight_ref.at[column ^ (relative // row_parts), row ^ (relative % row_parts)],
                sems.at[relative],
            )
            copy.start()
            copies[relative] = copy
    return [copies[relative] for relative in sorted(copies)]


class Packing:
    def __init__(self, half, qkv_cols, proj_cols):
        self.half, self.qkv_cols, self.proj_cols = half, qkv_cols, proj_cols
        self.qkv_main, self.proj_main = qkv_cols // 128 * 128, proj_cols // 128 * 128
        self.qkv_rest, self.proj_rest = qkv_cols - self.qkv_main, proj_cols - self.proj_main
        self.rest = self.qkv_rest + self.proj_rest
        self.proj_start = 2 * self.qkv_main
        self.rest_start = self.proj_start + 2 * self.proj_main
        self.width = self.rest_start + 2 * self.rest

    def pack(self, qkv, proj):
        halves = [slice(i * self.half, (i + 1) * self.half) for i in range(2)]
        return jnp.concatenate(
            [qkv[rows, : self.qkv_main] for rows in halves]
            + [proj[rows, : self.proj_main] for rows in halves]
            + [
                piece
                for rows in halves
                for piece in (qkv[rows, self.qkv_main :], proj[rows, self.proj_main :])
            ],
            axis=1,
        )

    def qkv_of(self, block, side):
        rest = self.rest_start + side * self.rest
        return jnp.concatenate(
            [
                block[:, side * self.qkv_main : (side + 1) * self.qkv_main],
                block[:, rest : rest + self.qkv_rest],
            ],
            axis=1,
        )

    def proj_of(self, block, side):
        main = self.proj_start + side * self.proj_main
        rest = self.rest_start + side * self.rest + self.qkv_rest
        return jnp.concatenate(
            [block[:, main : main + self.proj_main], block[:, rest : rest + self.proj_rest]],
            axis=1,
        )

    def unpack(self, block):
        return tuple(
            jnp.concatenate([part(block, side) for side in range(2)], axis=0)
            for part in (self.qkv_of, self.proj_of)
        )


def pair_mask(span, frames, live):
    query = lax.broadcasted_iota(jnp.int32, (span, span), 0)
    key = lax.broadcasted_iota(jnp.int32, (span, span), 1)
    return ((query // frames) == (key // frames)) & ((key % frames) < live)


def head_groups(count, size):
    return [range(start, start + size) for start in range(0, count, size)]


def head_slices(ref, which, head, rows, size):
    per = ref.shape[2] // size
    slot = which * HEADS + head
    return ref[slot // per, rows, (slot % per) * size : (slot % per + 1) * size]


def columns_of(ref, rows, index, size):
    return ref[rows, index * size : (index + 1) * size]


def join_proj(packing, weight, proj):
    for place in range(weight.shape[0]):
        start = place * packing.proj_cols
        for part in range(weight.shape[1]):
            for side in range(2):
                row = (2 * part + side) * packing.half
                proj[row : row + packing.half, start : start + packing.proj_cols] = packing.proj_of(
                    weight.at[place, part], side
                )


def attn_forward_kernel(sizes, packing, places, *refs):
    clips, span, frames, width, chunk = sizes
    blocks = len(places)
    lengths, tokens, mod = refs[:3]
    block_refs = refs[3 : 3 + blocks]
    hidden, mixed, probs_out, attended, branch, middle, hidden_two, proj = refs[3 + blocks : 11 + blocks]
    weight, branch_full, hidden_s, attended_s, sems = refs[11 + blocks :]
    copies = start_blocks(places, block_refs, weight, sems)
    column_parts, row_parts = weight.shape[0], weight.shape[1]
    size = width // HEADS
    scale = 1.0 / math.sqrt(size)

    def first_norm(step, carry):
        rows = pl.ds(pl.multiple_of(step * chunk, chunk), chunk)
        clip_mod = mod[step * chunk // span]
        unit, _ = stats(tokens[rows, :].astype(F32))
        hidden_s[rows, :] = (unit * (1.0 + clip_mod[1:2]) + clip_mod[0:1]).astype(LOW)
        return carry

    lax.fori_loop(0, clips * span // chunk, first_norm, 0)
    column, row = here(AXES)
    for relative in range(column_parts):
        for other in range(row_parts):
            copies[relative * row_parts + other].wait()
        place = column ^ relative
        columns = jnp.concatenate(
            [
                packing.qkv_of(weight.at[place, part], side)
                for part in range(row_parts)
                for side in range(2)
            ],
            axis=0,
        )
        mixed[place] = dot_nn(hidden_s[...], columns).astype(LOW)

    for clip in range(clips):
        rows = slice(clip * span, (clip + 1) * span)
        live_mask = pair_mask(span, frames, lengths[clip])
        for group in head_groups(HEADS, 4):
            scores = [
                dot_nt(
                    head_slices(mixed, 0, head, rows, size), head_slices(mixed, 1, head, rows, size)
                )
                for head in group
            ]
            scores = [jnp.where(live_mask, score * scale, -1e30) for score in scores]
            exps = [jnp.exp(score - jnp.max(score, -1, keepdims=True)) for score in scores]
            probs = [(e * (1.0 / jnp.sum(e, -1, keepdims=True))).astype(LOW) for e in exps]
            values = [
                dot_nn(prob, head_slices(mixed, 2, head, rows, size))
                for head, prob in zip(group, probs)
            ]
            for head, prob, value in zip(group, probs, values):
                probs_out[clip, head] = prob
                attended_s[rows, head * size : (head + 1) * size] = value.astype(LOW)

    join_proj(packing, weight, proj)
    branch_full[...] = dot_nn(attended_s[...], proj[...])

    def second_norm(step, carry):
        rows = pl.ds(pl.multiple_of(step * chunk, chunk), chunk)
        clip_mod = mod[step * chunk // span]
        value = branch_full[rows, :]
        branch[rows, :] = value.astype(LOW)
        value = tokens[rows, :].astype(F32) + clip_mod[2:3] * value
        middle[rows, :] = value
        unit, _ = stats(value)
        hidden_two[rows, :] = (unit * (1.0 + clip_mod[4:5]) + clip_mod[3:4]).astype(LOW)
        return carry

    lax.fori_loop(0, clips * span // chunk, second_norm, 0)
    hidden[...] = hidden_s[...].T
    attended[...] = attended_s[...].T


def norm_back(grad, values, scale_row):
    unit, inverse = stats(values)
    d_unit = grad * (1.0 + scale_row)
    d_value = inverse * (
        d_unit
        - jnp.mean(d_unit, -1, keepdims=True)
        - unit * jnp.mean(d_unit * unit, -1, keepdims=True)
    )
    return unit, d_value


def proj_backward_kernel(sizes, *refs):
    clips, span, frames, width, chunk = sizes
    cotangent, mod, middle, branch, grad_own, grad_core, grad_far, proj = refs[:8]
    d_middle, d_branch, d_attended, d_mod = refs[8:]
    zero_row = jnp.zeros((1, width), F32)
    steps = span // chunk
    for clip in range(clips):
        clip_mod = mod[clip]

        def second_back(step, carry, clip=clip, clip_mod=clip_mod):
            d_shift, d_scale, d_gate = carry
            rows = pl.ds(pl.multiple_of(clip * span + step * chunk, chunk), chunk)
            grad = grad_own[rows, :] + grad_core[rows, :].astype(F32)
            grad += grad_far[rows, :].astype(F32)
            unit, d_value = norm_back(grad, middle[rows, :], clip_mod[4:5])
            d_value = cotangent[rows, :].astype(F32) + d_value
            d_middle[rows, :] = d_value
            d_branch[rows, :] = (d_value * clip_mod[2:3]).astype(LOW)
            return (
                d_shift + jnp.sum(grad, 0, keepdims=True),
                d_scale + jnp.sum(grad * unit, 0, keepdims=True),
                d_gate + jnp.sum(d_value * branch[rows, :].astype(F32), 0, keepdims=True),
            )

        sums = lax.fori_loop(0, steps, second_back, (zero_row, zero_row, zero_row))
        d_mod[clip, 0:1, :] = sums[2]
        d_mod[clip, 1:2, :] = sums[0]
        d_mod[clip, 2:3, :] = sums[1]

    d_attended[...] = dot_nt(d_branch[...], proj[...]).astype(LOW)


def attn_backward_kernel(sizes, *refs):
    clips, span, frames, width, qkv_cols = sizes
    mixed, probs_ref, d_attended, d_mixed = refs
    size = width // HEADS
    scale = 1.0 / math.sqrt(size)
    cols = qkv_cols // size
    for clip in range(clips):
        rows = slice(clip * span, (clip + 1) * span)
        for group in head_groups(HEADS, 4):
            queries, keys, values = (
                [head_slices(mixed, which, head, rows, size) for head in group]
                for which in range(3)
            )
            probs = [probs_ref[clip, head] for head in group]
            grads = [columns_of(d_attended, rows, head, size) for head in group]
            d_probs = [dot_nt(grad, value) for grad, value in zip(grads, values)]
            d_values = [dot_tn(prob, grad) for prob, grad in zip(probs, grads)]
            d_scores = []
            for prob, d_prob in zip(probs, d_probs):
                prob = prob.astype(F32)
                inner = jnp.sum(prob * d_prob, -1, keepdims=True)
                d_scores.append((prob * (d_prob - inner) * scale).astype(LOW))
            d_queries = [dot_nn(score, key) for score, key in zip(d_scores, keys)]
            d_keys = [dot_tn(score, query) for score, query in zip(d_scores, queries)]
            for which, pieces in enumerate((d_queries, d_keys, d_values)):
                for head, piece in zip(group, pieces):
                    slot = which * HEADS + head
                    place, start = slot // cols, (slot % cols) * size
                    d_mixed[place, rows, start : start + size] = piece.astype(LOW)


def qkv_backward_kernel(sizes, packing, places, *refs):
    clips, span, frames, width, chunk = sizes
    blocks = len(places)
    tokens, mod, d_middle, d_mixed = refs[:4]
    input_grad, d_mod = refs[4 + blocks : 6 + blocks]
    weight, d_hidden, sems = refs[6 + blocks :]
    copies = start_blocks(places, refs[4 : 4 + blocks], weight, sems)
    column_parts, row_parts = weight.shape[0], weight.shape[1]
    for copy in copies:
        copy.wait()
    for place in range(column_parts):
        columns = jnp.concatenate(
            [
                packing.qkv_of(weight.at[place, part], side)
                for part in range(row_parts)
                for side in range(2)
            ],
            axis=0,
        )
        term = dot_nt(d_mixed[place, :, 0 : packing.qkv_cols], columns)
        if place == 0:
            d_hidden[...] = term
        else:
            d_hidden[...] += term
    zero_row = jnp.zeros((1, width), F32)
    for clip in range(clips):
        clip_mod = mod[clip]

        def first_back(step, carry, clip=clip, clip_mod=clip_mod):
            d_shift, d_scale = carry
            rows = pl.ds(pl.multiple_of(clip * span + step * chunk, chunk), chunk)
            grad = d_hidden[rows, :]
            unit, d_value = norm_back(grad, tokens[rows, :].astype(F32), clip_mod[1:2])
            input_grad[rows, :] = (d_middle[rows, :] + d_value).astype(LOW)
            return (
                d_shift + jnp.sum(grad, 0, keepdims=True),
                d_scale + jnp.sum(grad * unit, 0, keepdims=True),
            )

        sums = lax.fori_loop(0, span // chunk, first_back, (zero_row, zero_row))
        d_mod[clip, 0:1, :] = sums[0]
        d_mod[clip, 1:2, :] = sums[1]


def attn_weight_kernel(packing, distances, *refs):
    own, far, outs, d_pieces = refs[:4], refs[4:8], refs[8:-1], refs[-1]
    half, qkv_cols, proj_cols = packing.half, packing.qkv_cols, packing.proj_cols
    row_count = own[0].shape[1]
    column_parts = own[2].shape[0]
    row_parts = own[0].shape[0] // (2 * half)
    for start, group in ((0, own), (row_count, far)):
        for place in range(column_parts):
            d_pieces[place, start : start + row_count, :] = columns_of(
                group[3], slice(None), place, proj_cols
            )
    column, row = here(AXES)
    for index, z_bits in enumerate(distances):
        for x_bit in range(2):
            place = column ^ (2 * z_bits + x_bit)
            d_qkv = jnp.concatenate(
                [own[2][place, :, 0:qkv_cols], far[2][place, :, 0:qkv_cols]], axis=0
            )
            d_proj = d_pieces[place]
            for other in range(row_parts // 2):
                rows = pl.ds(pl.multiple_of((row ^ (2 * other)) * 2 * half, 16), 2 * half)
                hidden_t, attended_t = (
                    jnp.concatenate([own[which][rows, :], far[which][rows, :]], axis=1)
                    for which in range(2)
                )
                qkv = dot_nn(hidden_t, d_qkv)
                proj = dot_nn(attended_t, d_proj)
                outs[2 * index + other][x_bit] = packing.pack(qkv, proj).astype(LOW)


def feed_kernel(chunk, parts, *refs):
    sources, stacked, outs = refs[0:4], refs[4], refs[5:11]
    hidden, d_outs, up_weight, down_weight, up_proj, d_activ, activ, d_up, wide, narrow = refs[11:21]
    in_sems, weight_sems, out_sems = refs[21:]
    rows_each = sources[0].shape[0]
    half = stacked.shape[0] // (2 * parts)
    halves = [pl.ds(index * rows_each, rows_each) for index in range(2)]

    def started(source, target, sem):
        copy = pltpu.make_async_copy(source, target, sem)
        copy.start()
        return copy

    waits = []
    for which, (target, weight) in enumerate(((hidden, up_weight), (d_outs, down_weight))):
        waits.append(
            [
                started(sources[2 * which + index], target.at[rows], in_sems.at[which, index])
                for index, rows in enumerate(halves)
            ]
            + [
                started(
                    stacked.at[pl.ds((2 * part + which) * half, half)],
                    weight.at[pl.ds(part * half, half)],
                    weight_sems.at[part, which],
                )
                for part in range(parts)
            ]
        )
    sent = []
    tilt = math.sqrt(2.0 / math.pi)
    for copy in waits[0]:
        copy.wait()
    up_proj[...] = dot_nt(hidden[...], up_weight[...])
    for copy in waits[1]:
        copy.wait()
    d_activ[...] = dot_nn(d_outs[...], down_weight[...])

    def gelu(step, carry):
        rows = pl.ds(pl.multiple_of(step * chunk, chunk), chunk)
        value = up_proj[rows, :]
        square = value * value
        bend = jnp.tanh(value * (tilt + (tilt * 0.044715) * square))
        half_value = 0.5 * value
        activ[rows, :] = (half_value + half_value * bend).astype(LOW)
        slope = (0.5 + 0.5 * bend) + half_value * (1.0 - bend * bend) * (
            tilt + (tilt * 3.0 * 0.044715) * square
        )
        d_up[rows, :] = (d_activ[rows, :] * slope).astype(LOW)
        return carry

    lax.fori_loop(0, 2 * rows_each // chunk, gelu, 0)
    for index, rows in enumerate(halves):
        sent.append(started(activ.at[rows], outs[index], out_sems.at[index]))
        sent.append(started(d_up.at[rows], outs[2 + index], out_sems.at[2 + index]))
    value = dot_nn(d_up[...], up_weight[...])
    narrow[...] = value[rows_each:].astype(LOW)
    sent.append(started(narrow, outs[5], out_sems.at[5]))
    wide[...] = value[:rows_each]
    sent.append(started(wide, outs[4], out_sems.at[4]))
    for copy in sent:
        copy.wait()


def feed_weight_kernel(parts, *refs):
    gathered, stacked, results = refs[16], refs[17], refs[18:22]
    down_weight, sems = refs[22:]
    half = gathered.shape[0] // (2 * parts)
    copies = []
    for part in range(parts):
        copy = pltpu.make_async_copy(
            gathered.at[pl.ds((2 * part + 1) * half, half)],
            down_weight.at[pl.ds(part * half, half)],
            sems.at[part],
        )
        copy.start()
        copies.append(copy)
    hidden, d_outs, activ, d_up = (
        jnp.concatenate([ref[...] for ref in refs[i : i + 4]], axis=0) for i in (0, 4, 8, 12)
    )
    for side, (left, right) in enumerate(((d_up, hidden), (d_outs, activ))):
        total = dot_tn(left, right).astype(LOW)
        for part in range(parts):
            stacked[part, side * half : (side + 1) * half, :] = total[
                part * half : (part + 1) * half
            ]
    for copy in copies:
        copy.wait()
    total = dot_nt(activ, down_weight[...])
    rows = results[0].shape[0]
    for index, result in enumerate(results):
        result[...] = total[index * rows : (index + 1) * rows].astype(result.dtype)


def modulation_kernel(conds, ada, part_out, ordered):
    groups, rows, _ = ordered.shape
    for group in range(groups):
        ordered[group] = conds[group, 0:rows, 0 : ada.shape[0]]
        part_out[group * rows : (group + 1) * rows, :] = dot_nn(ordered[group], ada[...])


def prepare_kernel(packing, sub, clips, *refs):
    timesteps, labels, time_table, class_table, qkv, proj_t, up, down_t, packed, send = refs
    packed[...] = packing.pack(qkv[...], proj_t[...].T)
    row_parts = send.shape[0]

    def look_up(indices, table):
        count = table.shape[0]
        row = lax.broadcasted_iota(jnp.int32, (16, count), 0)
        column = lax.broadcasted_iota(jnp.int32, (16, count), 1)
        picked = jnp.zeros((16, count), jnp.bool_)
        for clip in range(clips):
            picked = picked | ((row == clip) & (column == indices[clip]))
        return dot_nn(picked.astype(F32).astype(LOW), table[...])

    embedded = look_up(timesteps, time_table) + look_up(labels, class_table)
    cond = (embedded * (1.0 / (1.0 + jnp.exp(-embedded)))).astype(LOW)
    up_t = up[...].T
    height = send.shape[2]
    pairs = height // sub
    for part in range(row_parts):
        send[part, 0:sub] = up_t[part * sub : (part + 1) * sub, :]
        send[part, 2 * sub :] = cond[:, part * height : (part + 1) * height]
        for pair in range(pairs):
            start = (pair * row_parts + part) * sub
            send[part, sub : 2 * sub, pair * sub : (pair + 1) * sub] = down_t[:, start : start + sub]


def feed_finish_kernel(back, up_grad, down_grad_t):
    parts, _, sub, height = back.shape
    pairs = height // sub
    for part in range(parts):
        up_grad[:, part * sub : (part + 1) * sub] = back[part, 0].astype(F32).T
        for pair in range(pairs):
            start = (pair * parts + part) * sub
            down_grad_t[:, start : start + sub] = back[
                part, 1, :, pair * sub : (pair + 1) * sub
            ].astype(F32)


def attn_finish_kernel(packing, *refs):
    total = refs[0][...].astype(F32)
    for ref in refs[1:-2]:
        total += ref[...].astype(F32)
    qkv_grad, proj_grad_t = refs[-2:]
    for side in range(2):
        rows = slice(side * packing.half, (side + 1) * packing.half)
        qkv_grad[rows, :] = packing.qkv_of(total, side)
        proj_grad_t[:, rows] = packing.proj_of(total, side).T


VMEM_SPEC = pl.BlockSpec(memory_space=pltpu.VMEM)
SMEM_SPEC = pl.BlockSpec(memory_space=pltpu.SMEM)
ANY_SPEC = pl.BlockSpec(memory_space=pl.ANY)
PARAMS = pltpu.CompilerParams(vmem_limit_bytes=56 * 1024 * 1024)


def shape_of(dims, kind=LOW):
    return jax.ShapeDtypeStruct(dims, kind)


def cost(micros):
    return pl.CostEstimate(flops=1000, bytes_accessed=int(micros * SCALE), transcendentals=0)


def after(value, *others):
    return lax.optimization_barrier((value,) + others)[0]


class Sequence:
    def __init__(self):
        self.token = None

    def call(self, kernel, shapes, arrays, name, specs=None, scratch=(), tied=0, out_spec=None):
        arrays = list(arrays)
        if self.token is not None:
            arrays[tied] = after(arrays[tied], self.token)
        results = pl.pallas_call(
            kernel,
            out_shape=shapes,
            in_specs=specs or [VMEM_SPEC] * len(arrays),
            out_specs=jax.tree.map(lambda _: out_spec or VMEM_SPEC, shapes),
            scratch_shapes=scratch,
            compiler_params=PARAMS,
            cost_estimate=cost(1),
            name=name,
        )(*arrays)
        self.token = min(jax.tree.leaves(results), key=lambda result: result.size)
        return results

    def sum_low(self, *arrays):
        total = after(arrays[0], self.token).astype(F32)
        for array in arrays[1:]:
            total += array.astype(F32)
        self.token = total.astype(LOW)
        return self.token


def swap(value, mask, count):
    return lax.ppermute(value, AXES, [(i, i ^ mask) for i in range(count)])


def padded_exchange(rows, count):
    length = rows.shape[1]
    tiles = -(-length // 1024) * 8
    rows = jnp.pad(rows, ((0, 0), (0, tiles * 128 - length))).reshape(count, tiles, 128)
    got = lax.all_to_all(rows, AXES, 0, 0, tiled=True)
    return got.reshape(count, tiles * 128)[:, :length]


def fast_body(
    column_parts,
    row_parts,
    inputs,
    out_cotangent,
    lengths,
    timesteps,
    labels,
    time_table,
    class_table,
    ada_weight,
    qkv_weight,
    proj_weight,
    up_weight,
    down_weight,
):
    count = column_parts * row_parts
    clips, positions, frames, width = inputs.shape
    span = positions * frames
    row_count = clips * span
    qkv_cols, proj_cols = qkv_weight.shape[1], proj_weight.shape[1]
    height = qkv_weight.shape[0]
    part_width = width // row_parts
    hidden_part = up_weight.shape[1] * column_parts // row_parts
    sub = up_weight.shape[1] // row_parts
    x_mask = row_parts
    z_masks = tuple(row_parts * 2 * i for i in range(1, column_parts // 2))
    packing = Packing(height // 2, qkv_cols, proj_cols)

    line = Sequence()
    packed, both_send = line.call(
        functools.partial(prepare_kernel, packing, sub, clips),
        (
            shape_of((height // 2, packing.width)),
            shape_of((row_parts, 2 * sub + 16, height)),
        ),
        (timesteps, labels, time_table, class_table)
        + (qkv_weight, proj_weight.T, up_weight, down_weight.T),
        "prepare",
        [SMEM_SPEC] * 2 + [VMEM_SPEC] * 6,
    )

    y_mask, c_mask = 2, 1
    ada_cols = ada_weight.shape[1]

    def gate(*values):
        return lax.optimization_barrier(values)

    own = packed[None]
    far = [swap(own, mask, count) for mask in z_masks]
    own_x, own_y = swap(own, x_mask, count), swap(own, y_mask, count)
    both_got = lax.all_to_all(both_send, "fsdp", 0, 0, tiled=True)
    *far, own_x, own_y, both_got = gate(*far, own_x, own_y, both_got)
    own_feed = both_got[:, : 2 * sub].reshape(row_parts, 2, sub, height)
    own_feed = own_feed.transpose(1, 2, 0, 3).reshape(2 * sub, width)
    conds = both_got[:, 2 * sub : 2 * sub + clips].reshape(row_parts * clips, height)
    feed = lax.all_gather(own_feed, "dp", axis=0, tiled=True)

    far = jnp.concatenate(far)
    pads = (-row_parts * clips % 16, -height % 128)
    conds = jnp.pad(conds, ((0, pads[0]), (0, pads[1])))
    conds = jnp.broadcast_to(conds[None], (column_parts,) + conds.shape)
    conds = lax.all_to_all(conds, "dp", 0, 0, tiled=True)
    far_x, far_y = swap(far, x_mask, count), swap(far, y_mask, count)
    cores = [swap(array, c_mask, count) for array in (own, own_x, own_y, far)]
    far_x, far_y, conds, *cores = gate(far_x, far_y, conds, *cores)

    mod_part, conds = line.call(
        modulation_kernel,
        (
            shape_of((count * clips, ada_cols), F32),
            shape_of((column_parts, row_parts * clips, part_width)),
        ),
        (conds, ada_weight),
        "modulation",
    )
    cond_all = conds.reshape(count * clips, part_width)
    mod_got = padded_exchange(mod_part.reshape(count, clips * ada_cols), count)
    own_xy, far_xy = swap(own_x, y_mask, count), swap(far_x, y_mask, count)
    cores += [swap(array, c_mask, count) for array in (far_x, far_y)]
    own_xy, far_xy, mod_got, *cores = gate(own_xy, far_xy, mod_got, *cores)
    mod_own = jnp.sum(mod_got.reshape(column_parts, row_parts, clips, ada_cols), axis=1)
    mod = mod_own.transpose(1, 0, 2).reshape(clips, 6, width)
    cores += [swap(array, c_mask, count) for array in (own_xy, far_xy)]

    blocks = [own, own_x, own_y, far, far_x, far_y, own_xy, far_xy]
    places = [[0], [x_mask], [y_mask], list(z_masks)]
    places += [[z ^ side for z in z_masks] for side in (x_mask, y_mask)]
    places += [[x_mask ^ y_mask]]
    places += [[z ^ x_mask ^ y_mask for z in z_masks]]
    blocks += cores
    places += [[place ^ c_mask for place in held] for held in places]

    tokens = inputs.reshape(row_count, width)
    cotangent = out_cotangent.reshape(row_count, width)
    gate_two = jnp.repeat(mod[:, 5], span, axis=0)
    d_out = (cotangent.astype(F32) * gate_two).astype(LOW)
    d_outs = {0: d_out, 1: swap(d_out, 1, count), 2: swap(d_out, 2, count)}
    d_outs[3] = swap(d_outs[2], 1, count)
    sizes = (clips, span, frames, width, 32)
    full = (row_count, width)
    weight_scratch = pltpu.VMEM((column_parts, row_parts, height // 2, packing.width), LOW)
    weight_sems = pltpu.SemaphoreType.DMA((count,))
    hidden, mixed, probs, attended, branch, middle, hidden_two, proj_full = line.call(
        functools.partial(attn_forward_kernel, sizes, packing, places),
        (
            shape_of((width, row_count)),
            shape_of((column_parts, row_count, qkv_cols)),
            shape_of((clips, HEADS, span, span)),
            shape_of((width, row_count)),
            shape_of(full),
            shape_of(full, F32),
            shape_of(full),
            shape_of((width, width)),
        ),
        (lengths, tokens, mod, *blocks),
        "attn_forward",
        [SMEM_SPEC, VMEM_SPEC, VMEM_SPEC] + [ANY_SPEC] * len(blocks),
        (
            weight_scratch,
            pltpu.VMEM(full, F32),
            pltpu.VMEM(full, LOW),
            pltpu.VMEM(full, LOW),
            weight_sems,
        ),
        tied=2,
    )

    tokens_two = {0: hidden_two, 1: swap(hidden_two, 1, count), 2: swap(hidden_two, 2, count)}
    pair = (2 * row_count, width)
    pair_hidden = (2 * row_count, hidden_part)
    feed_scratch = (
        pltpu.VMEM(pair, LOW),
        pltpu.VMEM(pair, LOW),
        pltpu.VMEM((hidden_part, width), LOW),
        pltpu.VMEM((width, hidden_part), LOW),
        pltpu.VMEM(pair_hidden, F32),
        pltpu.VMEM(pair_hidden, F32),
        pltpu.VMEM(pair_hidden, LOW),
        pltpu.VMEM(pair_hidden, LOW),
        pltpu.VMEM(full, F32),
        pltpu.VMEM(full, LOW),
        pltpu.SemaphoreType.DMA((2, 2)),
        pltpu.SemaphoreType.DMA((column_parts, 2)),
        pltpu.SemaphoreType.DMA((6,)),
    )

    def feed_call(index, name):
        return line.call(
            functools.partial(feed_kernel, 32, column_parts),
            [shape_of((row_count, hidden_part))] * 4 + [shape_of(full, F32), shape_of(full)],
            (
                tokens_two[index],
                tokens_two[index + 1],
                d_outs[index],
                d_outs[index + 1],
                feed,
            ),
            name,
            [ANY_SPEC] * 5,
            feed_scratch,
            out_spec=ANY_SPEC,
        )

    near = feed_call(0, "feed_near")
    tokens_two[2] = after(tokens_two[2], line.token)
    tokens_two[3] = swap(tokens_two[2], 1, count)
    distant = feed_call(2, "feed_distant")

    grad_send = line.sum_low(distant[4], swap(distant[5], 1, count))
    grad_far = swap(grad_send, 2, count)
    grad_parts = (near[4], swap(near[5], 1, count), grad_far)
    feed_grads, *partials = line.call(
        functools.partial(feed_weight_kernel, column_parts),
        [shape_of((column_parts, 2 * sub, width))]
        + [shape_of(full, F32), shape_of(full)]
        + [shape_of(full)] * 2,
        [tokens_two[i] for i in range(4)]
        + [d_outs[i] for i in range(4)]
        + [*near[0:2], *distant[0:2], *near[2:4], *distant[2:4], feed],
        "feed_weight",
        [VMEM_SPEC] * 16 + [ANY_SPEC],
        (pltpu.VMEM((width, hidden_part), LOW), pltpu.SemaphoreType.DMA((column_parts,))),
    )
    feed_grads = feed_grads.reshape(2 * sub * column_parts, width)
    feed_grads, grad_far = lax.optimization_barrier((feed_grads, grad_far))
    grad_parts = grad_parts[:2] + (grad_far,)
    line.token = grad_far
    groups = column_parts // 2
    feed_sum = lax.psum_scatter(feed_grads, "dp", scatter_dimension=0, tiled=True)

    out_send = line.sum_low(partials[2], swap(partials[3], 1, count))
    out_far = swap(out_send, 2, count)
    d_middle, d_branch, d_attended, d_mod_two = line.call(
        functools.partial(proj_backward_kernel, sizes),
        (
            shape_of(full, F32),
            shape_of(full),
            shape_of(full),
            shape_of((clips, 3, width), F32),
        ),
        (cotangent, mod, middle, branch, *grad_parts, proj_full),
        "proj_backward",
    )
    d_mixed = line.call(
        functools.partial(attn_backward_kernel, (clips, span, frames, width, qkv_cols)),
        shape_of((column_parts, row_count, -(-qkv_cols // 128) * 128)),
        (mixed, probs, d_attended),
        "attn_backward",
    )
    own_side = (hidden, attended, d_mixed, d_branch)
    far_side = [swap(array, 1, count) for array in own_side]
    attn_grads, first = {}, {}
    for distances in (range(groups - 1, groups // 2 - 1, -1), range(groups // 2 - 1, -1, -1)):
        grads = line.call(
            functools.partial(attn_weight_kernel, packing, distances),
            [shape_of((2, height // 2, packing.width))] * (2 * len(distances)),
            (*own_side, *far_side),
            "attn_weight",
            scratch=(pltpu.VMEM((column_parts, 2 * row_count, proj_cols), LOW),),
        )
        for index, distance in enumerate(distances):
            attn_grads[distance] = grads[2 * index]
            first[distance] = swap(grads[2 * index + 1], y_mask, count)
        if not len(distances) < len(first):
            ffn_out = after(partials[0], line.token) + swap(partials[1], 1, count).astype(F32)
            ffn_out += out_far.astype(F32)
            result = (middle + gate_two * ffn_out).astype(LOW).reshape(inputs.shape)
            d_gate_two = jnp.sum(
                (cotangent.astype(F32) * ffn_out).reshape(clips, 1, span, width), axis=2
            )
            line.token = d_gate_two
    input_grad, d_mod_one = line.call(
        functools.partial(qkv_backward_kernel, sizes, packing, places),
        (shape_of(full), shape_of((clips, 2, width), F32)),
        (tokens, mod, d_middle, d_mixed, *blocks),
        "qkv_backward",
        [VMEM_SPEC] * 4 + [ANY_SPEC] * len(blocks),
        (weight_scratch, pltpu.VMEM(full, F32), weight_sems),
    )
    stay, second, attn_z = {}, {}, {}

    def split_sum(index):
        kept = after(attn_grads[index], line.token)
        stay[index] = kept[0].astype(F32) + first[index][0].astype(F32)
        leave = (kept[1].astype(F32) + first[index][1].astype(F32)).astype(LOW)
        line.token = leave
        second[index] = swap(leave, x_mask, count)

    def attn_sum(index):
        summed = line.sum_low(stay[index], second[index])
        attn_z[index] = swap(summed, z_masks[index - 1], count)

    d_mod = jnp.concatenate([d_mod_one, d_mod_two, d_gate_two], axis=1)
    mod_send = d_mod.reshape(clips, column_parts, ada_cols).transpose(1, 0, 2)
    mod_send = jnp.broadcast_to(
        mod_send.reshape(column_parts, 1, clips * ada_cols),
        (column_parts, row_parts, clips * ada_cols),
    ).reshape(count, clips * ada_cols)
    d_mod_all = padded_exchange(mod_send, count).reshape(count * clips, ada_cols)
    split_sum(3)
    line.token, d_mod_all = lax.optimization_barrier((line.token, d_mod_all))
    for index in (2, 1):
        split_sum(index)
        attn_sum(index + 1)
    back = feed_sum.reshape(2, sub, row_parts, height).transpose(2, 0, 1, 3)
    line.token, back = lax.optimization_barrier((line.token, back))
    back = lax.all_to_all(back, "fsdp", 0, 0, tiled=True)
    split_sum(0)
    attn_sum(1)
    qkv_grad, proj_grad_t = line.call(
        functools.partial(attn_finish_kernel, packing),
        (shape_of((height, qkv_cols), F32), shape_of((proj_cols, height), F32)),
        (stay[0], second[0], attn_z[3], attn_z[2], attn_z[1]),
        "attn_finish",
    )
    proj_grad = proj_grad_t.T
    up_grad, down_grad_t = line.call(
        feed_finish_kernel,
        (shape_of(up_weight.shape, F32), shape_of(down_weight.shape[::-1], F32)),
        (back,),
        "feed_finish",
    )
    down_grad = down_grad_t.T

    ada_grad = lax.dot_general(
        cond_all.astype(F32),
        d_mod_all,
        (((0,), (0,)), ((), ())),
        precision=lax.Precision.HIGHEST,
        preferred_element_type=F32,
    )
    return (
        result,
        input_grad.reshape(inputs.shape),
        ada_grad,
        qkv_grad,
        proj_grad,
        up_grad,
        down_grad,
    )


def solution(mesh):
    column_parts, row_parts = mesh.shape["dp"], mesh.shape["fsdp"]
    body = general_body
    if (column_parts, row_parts) == (8, 4):
        body = functools.partial(fast_body, column_parts, row_parts)
    clip_spec = P(AXES, None, None, None)
    return jax.shard_map(
        body,
        mesh=mesh,
        in_specs=(
            clip_spec,
            clip_spec,
            P(AXES),
            P(AXES),
            P(AXES),
            P(),
            P(),
        )
        + (P("fsdp", "dp"),) * 5,
        out_specs=(clip_spec, clip_spec) + (P("fsdp", "dp"),) * 5,
        check_vma=False,
    )
```

```python
import functools
import math

import jax
import jax.numpy as jnp
from jax import lax
from jax.experimental import pallas as pl
from jax.experimental.pallas import tpu as pltpu
from jax.sharding import PartitionSpec as P

HEADS = 16
AXES = ("dp", "fsdp")
EPS = 1e-06
F32, LOW = jnp.float32, jnp.bfloat16
SCALE = 100


def norm_mod(values, shift_add, scale_mul):
    center = values - jnp.mean(values, -1, keepdims=True)
    spread = jnp.mean(center * center, -1, keepdims=True)
    return center * lax.rsqrt(spread + 1e-06) * (1.0 + scale_mul) + shift_add


def gelu_tanh(values):
    return jax.nn.gelu(values, approximate=True)


def gather_five(shards):
    row_set = (
        lax.all_gather(shards[0], "fsdp", axis=0, tiled=True),
        lax.all_gather(shards[1], "fsdp", axis=0, tiled=True),
        lax.all_gather(shards[2], "fsdp", axis=0, tiled=True),
        lax.all_gather(shards[3], "fsdp", axis=0, tiled=True),
        lax.all_gather(shards[4], "fsdp", axis=0, tiled=True),
    )
    return (
        lax.all_gather(row_set[0], "dp", axis=1, tiled=True),
        lax.all_gather(row_set[1], "dp", axis=1, tiled=True),
        lax.all_gather(row_set[2], "dp", axis=1, tiled=True),
        lax.all_gather(row_set[3], "dp", axis=1, tiled=True),
        lax.all_gather(row_set[4], "dp", axis=1, tiled=True),
    )


def scatter_five(totals):
    row_set = (
        lax.psum_scatter(
            totals[0].astype(jnp.bfloat16), "fsdp", scatter_dimension=0, tiled=True
        ).astype(jnp.float32),
        lax.psum_scatter(
            totals[1].astype(jnp.bfloat16), "fsdp", scatter_dimension=0, tiled=True
        ).astype(jnp.float32),
        lax.psum_scatter(
            totals[2].astype(jnp.bfloat16), "fsdp", scatter_dimension=0, tiled=True
        ).astype(jnp.float32),
        lax.psum_scatter(
            totals[3].astype(jnp.bfloat16), "fsdp", scatter_dimension=0, tiled=True
        ).astype(jnp.float32),
        lax.psum_scatter(
            totals[4].astype(jnp.bfloat16), "fsdp", scatter_dimension=0, tiled=True
        ).astype(jnp.float32),
    )
    return (
        lax.psum_scatter(
            row_set[0].astype(jnp.bfloat16), "dp", scatter_dimension=1, tiled=True
        ).astype(jnp.float32),
        lax.psum_scatter(
            row_set[1].astype(jnp.bfloat16), "dp", scatter_dimension=1, tiled=True
        ).astype(jnp.float32),
        lax.psum_scatter(
            row_set[2].astype(jnp.bfloat16), "dp", scatter_dimension=1, tiled=True
        ).astype(jnp.float32),
        lax.psum_scatter(
            row_set[3].astype(jnp.bfloat16), "dp", scatter_dimension=1, tiled=True
        ).astype(jnp.float32),
        lax.psum_scatter(
            row_set[4].astype(jnp.bfloat16), "dp", scatter_dimension=1, tiled=True
        ).astype(jnp.float32),
    )


def fetch_weights(ada_weight, core_shards):
    return tuple(gather_five((ada_weight,) + tuple(core_shards)))


def matmul_tn(left, right):
    return lax.dot_general(
        left, right, (((0,), (0,)), ((), ())), preferred_element_type=jnp.float32
    )


def matmul_nt(left, right):
    return lax.dot_general(
        left, right, (((1,), (1,)), ((), ())), preferred_element_type=jnp.float32
    )


def general_body(
    inputs,
    out_cotangent,
    lengths,
    timesteps,
    labels,
    time_table,
    class_table,
    ada_weight,
    qkv_weight,
    proj_weight,
    up_weight,
    down_weight,
):
    core_shards = (qkv_weight, proj_weight, up_weight, down_weight)
    clip_count, positions, frames, model_width = inputs.shape
    row_count = clip_count * positions * frames
    seq_count = clip_count * positions
    span = positions * frames
    head_size = model_width // HEADS
    attn_scale = 1.0 / math.sqrt(head_size)
    ada_full, qkv_full, proj_full, up_full, down_full = fetch_weights(ada_weight, core_shards)
    time_onehot = (timesteps[:, None] == lax.iota(jnp.int32, time_table.shape[0])[None, :]).astype(
        jnp.bfloat16
    )
    class_onehot = (labels[:, None] == lax.iota(jnp.int32, class_table.shape[0])[None, :]).astype(
        jnp.bfloat16
    )
    embedded = jnp.dot(time_onehot, time_table, preferred_element_type=jnp.float32) + jnp.dot(
        class_onehot, class_table, preferred_element_type=jnp.float32
    )
    cond_low = jax.nn.silu(embedded).astype(jnp.bfloat16)
    modulation = jnp.dot(cond_low, ada_full, preferred_element_type=jnp.float32)
    pieces = [
        modulation[:, None, offset * model_width : (offset + 1) * model_width]
        for offset in range(6)
    ]
    shift_one, scale_one, gate_one, shift_two, scale_two, gate_two = pieces
    residual = inputs.astype(jnp.float32).reshape(clip_count, span, model_width)
    hidden_one = (
        norm_mod(residual, shift_one, scale_one)
        .astype(jnp.bfloat16)
        .reshape(row_count, model_width)
    )
    mixed = jnp.dot(hidden_one, qkv_full, preferred_element_type=jnp.float32).astype(jnp.bfloat16)
    shaped = mixed.reshape(seq_count, frames, 3, HEADS, head_size)
    queries = shaped[:, :, 0]
    key_part = shaped[:, :, 1]
    value_part = shaped[:, :, 2]
    clip_live = lax.iota(jnp.int32, frames)[None, :] < lengths[:, None]
    key_live = jnp.repeat(clip_live, positions, axis=0)
    scores = (
        jnp.einsum("sqhe,skhe->shqk", queries, key_part, preferred_element_type=jnp.float32)
        * attn_scale
    )
    scores = jnp.where(key_live[:, None, None, :], scores, -1e30)
    row_max = jnp.max(scores, -1, keepdims=True)
    exp_scores = jnp.exp(scores - row_max)
    attn_probs = exp_scores / jnp.sum(exp_scores, -1, keepdims=True)
    probs_low = attn_probs.astype(jnp.bfloat16)
    attended = jnp.einsum(
        "shqk,skhe->sqhe", probs_low, value_part, preferred_element_type=jnp.float32
    )
    attended_low = attended.astype(jnp.bfloat16).reshape(row_count, model_width)
    branch = jnp.dot(attended_low, proj_full, preferred_element_type=jnp.float32).reshape(
        clip_count, span, model_width
    )
    middle = residual + gate_one * branch
    hidden_two = (
        norm_mod(middle, shift_two, scale_two).astype(jnp.bfloat16).reshape(row_count, model_width)
    )
    up_proj = jnp.dot(hidden_two, up_full, preferred_element_type=jnp.float32)
    activ_low = gelu_tanh(up_proj).astype(jnp.bfloat16)
    ffn_out = jnp.dot(activ_low, down_full, preferred_element_type=jnp.float32).reshape(
        clip_count, span, model_width
    )
    result = (middle + gate_two * ffn_out).astype(jnp.bfloat16).reshape(inputs.shape)
    ada_full, qkv_full, proj_full, up_full, down_full = fetch_weights(ada_weight, core_shards)
    grad_out = out_cotangent.astype(jnp.float32).reshape(clip_count, span, model_width)
    d_gate_two = jnp.sum(grad_out * ffn_out, axis=1)
    d_ffn = (grad_out * gate_two).astype(jnp.bfloat16).reshape(row_count, model_width)
    d_activ = matmul_nt(d_ffn, down_full)
    down_total = matmul_tn(activ_low, d_ffn)
    gelu_value, gelu_pull = jax.vjp(gelu_tanh, up_proj)
    d_up = gelu_pull(d_activ)[0].astype(jnp.bfloat16)
    d_hidden_two = matmul_nt(d_up, up_full)
    up_total = matmul_tn(hidden_two, d_up)
    norm_value, norm_pull = jax.vjp(norm_mod, middle, shift_two, scale_two)
    d_middle_norm, d_shift_two, d_scale_two = norm_pull(
        d_hidden_two.reshape(clip_count, span, model_width)
    )
    d_middle = grad_out + d_middle_norm
    d_gate_one = jnp.sum(d_middle * branch, axis=1)
    d_branch = (d_middle * gate_one).astype(jnp.bfloat16).reshape(row_count, model_width)
    d_attended = (
        matmul_nt(d_branch, proj_full)
        .astype(jnp.bfloat16)
        .reshape(seq_count, frames, HEADS, head_size)
    )
    proj_total = matmul_tn(attended_low, d_branch)
    d_value = jnp.einsum(
        "shqk,sqhe->skhe", probs_low, d_attended, preferred_element_type=jnp.float32
    )
    d_probs = jnp.einsum(
        "sqhe,skhe->shqk", d_attended, value_part, preferred_element_type=jnp.float32
    )
    d_scores = attn_probs * (d_probs - jnp.sum(attn_probs * d_probs, -1, keepdims=True))
    d_scores_low = d_scores.astype(jnp.bfloat16)
    d_query = (
        jnp.einsum("shqk,skhe->sqhe", d_scores_low, key_part, preferred_element_type=jnp.float32)
        * attn_scale
    )
    d_key = (
        jnp.einsum("shqk,sqhe->skhe", d_scores_low, queries, preferred_element_type=jnp.float32)
        * attn_scale
    )
    d_mixed = (
        jnp.stack([d_query, d_key, d_value], axis=2)
        .astype(jnp.bfloat16)
        .reshape(row_count, 3 * model_width)
    )
    d_hidden_one = matmul_nt(d_mixed, qkv_full)
    qkv_total = matmul_tn(hidden_one, d_mixed)
    norm_first, first_pull = jax.vjp(norm_mod, residual, shift_one, scale_one)
    d_input_norm, d_shift_one, d_scale_one = first_pull(
        d_hidden_one.reshape(clip_count, span, model_width)
    )
    input_grad = (d_middle + d_input_norm).astype(jnp.bfloat16).reshape(inputs.shape)
    d_modulation = jnp.concatenate(
        [
            d_shift_one[:, 0],
            d_scale_one[:, 0],
            d_gate_one,
            d_shift_two[:, 0],
            d_scale_two[:, 0],
            d_gate_two,
        ],
        axis=-1,
    )
    ada_total = jnp.dot(
        cond_low.astype(jnp.float32).T, d_modulation, precision=lax.Precision.HIGHEST
    )
    ada_grad, qkv_grad, proj_grad, up_grad, down_grad = scatter_five(
        (ada_total, qkv_total, proj_total, up_total, down_total)
    )
    return (result, input_grad, ada_grad, qkv_grad, proj_grad, up_grad, down_grad)


def dot_nn(left, right):
    return lax.dot_general(left, right, (((1,), (0,)), ((), ())), preferred_element_type=F32)


def dot_nt(left, right):
    return lax.dot_general(left, right, (((1,), (1,)), ((), ())), preferred_element_type=F32)


def dot_tn(left, right):
    return lax.dot_general(left, right, (((0,), (0,)), ((), ())), preferred_element_type=F32)


def stats(values):
    mean = jnp.mean(values, -1, keepdims=True)
    center = values - mean
    spread = jnp.mean(center * center, -1, keepdims=True)
    inverse = lax.rsqrt(spread + EPS)
    return center * inverse, inverse


def here(names):
    return lax.axis_index(names[0]), lax.axis_index(names[1])


def start_blocks(places, block_refs, weight_ref, sems):
    column, row = here(AXES)
    row_parts = weight_ref.shape[1]
    copies = {}
    for ref, held in zip(block_refs, places):
        for index, relative in enumerate(held):
            copy = pltpu.make_async_copy(
                ref.at[index],
                weight_ref.at[column ^ (relative // row_parts), row ^ (relative % row_parts)],
                sems.at[relative],
            )
            copy.start()
            copies[relative] = copy
    return [copies[relative] for relative in sorted(copies)]


class Packing:
    def __init__(self, half, qkv_cols, proj_cols):
        self.half, self.qkv_cols, self.proj_cols = half, qkv_cols, proj_cols
        self.qkv_main, self.proj_main = qkv_cols // 128 * 128, proj_cols // 128 * 128
        self.qkv_rest, self.proj_rest = qkv_cols - self.qkv_main, proj_cols - self.proj_main
        self.rest = self.qkv_rest + self.proj_rest
        self.proj_start = 2 * self.qkv_main
        self.rest_start = self.proj_start + 2 * self.proj_main
        self.width = self.rest_start + 2 * self.rest

    def pack(self, qkv, proj):
        halves = [slice(i * self.half, (i + 1) * self.half) for i in range(2)]
        return jnp.concatenate(
            [qkv[rows, : self.qkv_main] for rows in halves]
            + [proj[rows, : self.proj_main] for rows in halves]
            + [
                piece
                for rows in halves
                for piece in (qkv[rows, self.qkv_main :], proj[rows, self.proj_main :])
            ],
            axis=1,
        )

    def qkv_of(self, block, side):
        rest = self.rest_start + side * self.rest
        return jnp.concatenate(
            [
                block[:, side * self.qkv_main : (side + 1) * self.qkv_main],
                block[:, rest : rest + self.qkv_rest],
            ],
            axis=1,
        )

    def proj_of(self, block, side):
        main = self.proj_start + side * self.proj_main
        rest = self.rest_start + side * self.rest + self.qkv_rest
        return jnp.concatenate(
            [block[:, main : main + self.proj_main], block[:, rest : rest + self.proj_rest]],
            axis=1,
        )

    def unpack(self, block):
        return tuple(
            jnp.concatenate([part(block, side) for side in range(2)], axis=0)
            for part in (self.qkv_of, self.proj_of)
        )


def pair_mask(span, frames, live):
    query = lax.broadcasted_iota(jnp.int32, (span, span), 0)
    key = lax.broadcasted_iota(jnp.int32, (span, span), 1)
    return ((query // frames) == (key // frames)) & ((key % frames) < live)


def head_groups(count, size):
    return [range(start, start + size) for start in range(0, count, size)]


def head_slices(ref, which, head, rows, size):
    per = ref.shape[2] // size
    slot = which * HEADS + head
    return ref[slot // per, rows, (slot % per) * size : (slot % per + 1) * size]


def columns_of(ref, rows, index, size):
    return ref[rows, index * size : (index + 1) * size]


def join_proj(packing, weight, proj):
    for place in range(weight.shape[0]):
        start = place * packing.proj_cols
        for part in range(weight.shape[1]):
            for side in range(2):
                row = (2 * part + side) * packing.half
                proj[row : row + packing.half, start : start + packing.proj_cols] = packing.proj_of(
                    weight.at[place, part], side
                )


def attn_forward_kernel(sizes, packing, places, *refs):
    clips, span, frames, width, chunk = sizes
    blocks = len(places)
    lengths, tokens, mod = refs[:3]
    block_refs = refs[3 : 3 + blocks]
    hidden, mixed, probs_out, attended, branch, middle, hidden_two, proj = refs[3 + blocks : 11 + blocks]
    weight, branch_full, hidden_s, attended_s, sems = refs[11 + blocks :]
    copies = start_blocks(places, block_refs, weight, sems)
    column_parts, row_parts = weight.shape[0], weight.shape[1]
    size = width // HEADS
    scale = 1.0 / math.sqrt(size)

    def first_norm(step, carry):
        rows = pl.ds(pl.multiple_of(step * chunk, chunk), chunk)
        clip_mod = mod[step * chunk // span]
        unit, _ = stats(tokens[rows, :].astype(F32))
        hidden_s[rows, :] = (unit * (1.0 + clip_mod[1:2]) + clip_mod[0:1]).astype(LOW)
        return carry

    lax.fori_loop(0, clips * span // chunk, first_norm, 0)
    column, row = here(AXES)
    for relative in range(column_parts):
        for other in range(row_parts):
            copies[relative * row_parts + other].wait()
        place = column ^ relative
        columns = jnp.concatenate(
            [
                packing.qkv_of(weight.at[place, part], side)
                for part in range(row_parts)
                for side in range(2)
            ],
            axis=0,
        )
        mixed[place] = dot_nn(hidden_s[...], columns).astype(LOW)

    for clip in range(clips):
        rows = slice(clip * span, (clip + 1) * span)
        live_mask = pair_mask(span, frames, lengths[clip])
        for group in head_groups(HEADS, 4):
            scores = [
                dot_nt(
                    head_slices(mixed, 0, head, rows, size), head_slices(mixed, 1, head, rows, size)
                )
                for head in group
            ]
            scores = [jnp.where(live_mask, score * scale, -1e30) for score in scores]
            exps = [jnp.exp(score - jnp.max(score, -1, keepdims=True)) for score in scores]
            probs = [(e * (1.0 / jnp.sum(e, -1, keepdims=True))).astype(LOW) for e in exps]
            values = [
                dot_nn(prob, head_slices(mixed, 2, head, rows, size))
                for head, prob in zip(group, probs)
            ]
            for head, prob, value in zip(group, probs, values):
                probs_out[clip, head] = prob
                attended_s[rows, head * size : (head + 1) * size] = value.astype(LOW)

    join_proj(packing, weight, proj)
    branch_full[...] = dot_nn(attended_s[...], proj[...])

    def second_norm(step, carry):
        rows = pl.ds(pl.multiple_of(step * chunk, chunk), chunk)
        clip_mod = mod[step * chunk // span]
        value = branch_full[rows, :]
        branch[rows, :] = value.astype(LOW)
        value = tokens[rows, :].astype(F32) + clip_mod[2:3] * value
        middle[rows, :] = value
        unit, _ = stats(value)
        hidden_two[rows, :] = (unit * (1.0 + clip_mod[4:5]) + clip_mod[3:4]).astype(LOW)
        return carry

    lax.fori_loop(0, clips * span // chunk, second_norm, 0)
    hidden[...] = hidden_s[...].T
    attended[...] = attended_s[...].T


def norm_back(grad, values, scale_row):
    unit, inverse = stats(values)
    d_unit = grad * (1.0 + scale_row)
    d_value = inverse * (
        d_unit
        - jnp.mean(d_unit, -1, keepdims=True)
        - unit * jnp.mean(d_unit * unit, -1, keepdims=True)
    )
    return unit, d_value


def proj_backward_kernel(sizes, *refs):
    clips, span, frames, width, chunk = sizes
    cotangent, mod, middle, branch, grad_own, grad_core, grad_far, proj = refs[:8]
    d_middle, d_branch, d_attended, d_mod = refs[8:]
    zero_row = jnp.zeros((1, width), F32)
    steps = span // chunk
    for clip in range(clips):
        clip_mod = mod[clip]

        def second_back(step, carry, clip=clip, clip_mod=clip_mod):
            d_shift, d_scale, d_gate = carry
            rows = pl.ds(pl.multiple_of(clip * span + step * chunk, chunk), chunk)
            grad = grad_own[rows, :] + grad_core[rows, :].astype(F32)
            grad += grad_far[rows, :].astype(F32)
            unit, d_value = norm_back(grad, middle[rows, :], clip_mod[4:5])
            d_value = cotangent[rows, :].astype(F32) + d_value
            d_middle[rows, :] = d_value
            d_branch[rows, :] = (d_value * clip_mod[2:3]).astype(LOW)
            return (
                d_shift + jnp.sum(grad, 0, keepdims=True),
                d_scale + jnp.sum(grad * unit, 0, keepdims=True),
                d_gate + jnp.sum(d_value * branch[rows, :].astype(F32), 0, keepdims=True),
            )

        sums = lax.fori_loop(0, steps, second_back, (zero_row, zero_row, zero_row))
        d_mod[clip, 0:1, :] = sums[2]
        d_mod[clip, 1:2, :] = sums[0]
        d_mod[clip, 2:3, :] = sums[1]

    d_attended[...] = dot_nt(d_branch[...], proj[...]).astype(LOW)


def attn_backward_kernel(sizes, *refs):
    clips, span, frames, width, qkv_cols = sizes
    mixed, probs_ref, d_attended, d_mixed = refs
    size = width // HEADS
    scale = 1.0 / math.sqrt(size)
    cols = qkv_cols // size
    for clip in range(clips):
        rows = slice(clip * span, (clip + 1) * span)
        for group in head_groups(HEADS, 4):
            queries, keys, values = (
                [head_slices(mixed, which, head, rows, size) for head in group]
                for which in range(3)
            )
            probs = [probs_ref[clip, head] for head in group]
            grads = [columns_of(d_attended, rows, head, size) for head in group]
            d_probs = [dot_nt(grad, value) for grad, value in zip(grads, values)]
            d_values = [dot_tn(prob, grad) for prob, grad in zip(probs, grads)]
            d_scores = []
            for prob, d_prob in zip(probs, d_probs):
                prob = prob.astype(F32)
                inner = jnp.sum(prob * d_prob, -1, keepdims=True)
                d_scores.append((prob * (d_prob - inner) * scale).astype(LOW))
            d_queries = [dot_nn(score, key) for score, key in zip(d_scores, keys)]
            d_keys = [dot_tn(score, query) for score, query in zip(d_scores, queries)]
            for which, pieces in enumerate((d_queries, d_keys, d_values)):
                for head, piece in zip(group, pieces):
                    slot = which * HEADS + head
                    place, start = slot // cols, (slot % cols) * size
                    d_mixed[place, rows, start : start + size] = piece.astype(LOW)


def qkv_backward_kernel(sizes, packing, places, *refs):
    clips, span, frames, width, chunk = sizes
    blocks = len(places)
    tokens, mod, d_middle, d_mixed = refs[:4]
    input_grad, d_mod = refs[4 + blocks : 6 + blocks]
    weight, d_hidden, sems = refs[6 + blocks :]
    copies = start_blocks(places, refs[4 : 4 + blocks], weight, sems)
    column_parts, row_parts = weight.shape[0], weight.shape[1]
    for copy in copies:
        copy.wait()
    for place in range(column_parts):
        columns = jnp.concatenate(
            [
                packing.qkv_of(weight.at[place, part], side)
                for part in range(row_parts)
                for side in range(2)
            ],
            axis=0,
        )
        term = dot_nt(d_mixed[place, :, 0 : packing.qkv_cols], columns)
        if place == 0:
            d_hidden[...] = term
        else:
            d_hidden[...] += term
    zero_row = jnp.zeros((1, width), F32)
    for clip in range(clips):
        clip_mod = mod[clip]

        def first_back(step, carry, clip=clip, clip_mod=clip_mod):
            d_shift, d_scale = carry
            rows = pl.ds(pl.multiple_of(clip * span + step * chunk, chunk), chunk)
            grad = d_hidden[rows, :]
            unit, d_value = norm_back(grad, tokens[rows, :].astype(F32), clip_mod[1:2])
            input_grad[rows, :] = (d_middle[rows, :] + d_value).astype(LOW)
            return (
                d_shift + jnp.sum(grad, 0, keepdims=True),
                d_scale + jnp.sum(grad * unit, 0, keepdims=True),
            )

        sums = lax.fori_loop(0, span // chunk, first_back, (zero_row, zero_row))
        d_mod[clip, 0:1, :] = sums[0]
        d_mod[clip, 1:2, :] = sums[1]


def attn_weight_kernel(packing, distances, *refs):
    own, far, outs, d_pieces = refs[:4], refs[4:8], refs[8:-1], refs[-1]
    half, qkv_cols, proj_cols = packing.half, packing.qkv_cols, packing.proj_cols
    row_count = own[0].shape[1]
    column_parts = own[2].shape[0]
    row_parts = own[0].shape[0] // (2 * half)
    for start, group in ((0, own), (row_count, far)):
        for place in range(column_parts):
            d_pieces[place, start : start + row_count, :] = columns_of(
                group[3], slice(None), place, proj_cols
            )
    column, row = here(AXES)
    for index, z_bits in enumerate(distances):
        for x_bit in range(2):
            place = column ^ (2 * z_bits + x_bit)
            d_qkv = jnp.concatenate(
                [own[2][place, :, 0:qkv_cols], far[2][place, :, 0:qkv_cols]], axis=0
            )
            d_proj = d_pieces[place]
            for other in range(row_parts // 2):
                rows = pl.ds(pl.multiple_of((row ^ (2 * other)) * 2 * half, 16), 2 * half)
                hidden_t, attended_t = (
                    jnp.concatenate([own[which][rows, :], far[which][rows, :]], axis=1)
                    for which in range(2)
                )
                qkv = dot_nn(hidden_t, d_qkv)
                proj = dot_nn(attended_t, d_proj)
                outs[2 * index + other][x_bit] = packing.pack(qkv, proj).astype(LOW)


def feed_kernel(chunk, parts, *refs):
    sources, stacked, outs = refs[0:4], refs[4], refs[5:11]
    hidden, d_outs, up_weight, down_weight, up_proj, d_activ, activ, d_up, wide, narrow = refs[11:21]
    in_sems, weight_sems, out_sems = refs[21:]
    rows_each = sources[0].shape[0]
    half = stacked.shape[0] // (2 * parts)
    halves = [pl.ds(index * rows_each, rows_each) for index in range(2)]

    def started(source, target, sem):
        copy = pltpu.make_async_copy(source, target, sem)
        copy.start()
        return copy

    waits = []
    for which, (target, weight) in enumerate(((hidden, up_weight), (d_outs, down_weight))):
        waits.append(
            [
                started(sources[2 * which + index], target.at[rows], in_sems.at[which, index])
                for index, rows in enumerate(halves)
            ]
            + [
                started(
                    stacked.at[pl.ds((2 * part + which) * half, half)],
                    weight.at[pl.ds(part * half, half)],
                    weight_sems.at[part, which],
                )
                for part in range(parts)
            ]
        )
    sent = []
    tilt = math.sqrt(2.0 / math.pi)
    for copy in waits[0]:
        copy.wait()
    up_proj[...] = dot_nt(hidden[...], up_weight[...])
    for copy in waits[1]:
        copy.wait()
    d_activ[...] = dot_nn(d_outs[...], down_weight[...])

    def gelu(step, carry):
        rows = pl.ds(pl.multiple_of(step * chunk, chunk), chunk)
        value = up_proj[rows, :]
        square = value * value
        bend = jnp.tanh(value * (tilt + (tilt * 0.044715) * square))
        half_value = 0.5 * value
        activ[rows, :] = (half_value + half_value * bend).astype(LOW)
        slope = (0.5 + 0.5 * bend) + half_value * (1.0 - bend * bend) * (
            tilt + (tilt * 3.0 * 0.044715) * square
        )
        d_up[rows, :] = (d_activ[rows, :] * slope).astype(LOW)
        return carry

    lax.fori_loop(0, 2 * rows_each // chunk, gelu, 0)
    for index, rows in enumerate(halves):
        sent.append(started(activ.at[rows], outs[index], out_sems.at[index]))
        sent.append(started(d_up.at[rows], outs[2 + index], out_sems.at[2 + index]))
    value = dot_nn(d_up[...], up_weight[...])
    narrow[...] = value[rows_each:].astype(LOW)
    sent.append(started(narrow, outs[5], out_sems.at[5]))
    wide[...] = value[:rows_each]
    sent.append(started(wide, outs[4], out_sems.at[4]))
    for copy in sent:
        copy.wait()


def feed_weight_kernel(parts, *refs):
    gathered, stacked, results = refs[16], refs[17], refs[18:22]
    down_weight, sems = refs[22:]
    half = gathered.shape[0] // (2 * parts)
    copies = []
    for part in range(parts):
        copy = pltpu.make_async_copy(
            gathered.at[pl.ds((2 * part + 1) * half, half)],
            down_weight.at[pl.ds(part * half, half)],
            sems.at[part],
        )
        copy.start()
        copies.append(copy)
    hidden, d_outs, activ, d_up = (
        jnp.concatenate([ref[...] for ref in refs[i : i + 4]], axis=0) for i in (0, 4, 8, 12)
    )
    for side, (left, right) in enumerate(((d_up, hidden), (d_outs, activ))):
        total = dot_tn(left, right).astype(LOW)
        for part in range(parts):
            stacked[part, side * half : (side + 1) * half, :] = total[
                part * half : (part + 1) * half
            ]
    for copy in copies:
        copy.wait()
    total = dot_nt(activ, down_weight[...])
    rows = results[0].shape[0]
    for index, result in enumerate(results):
        result[...] = total[index * rows : (index + 1) * rows].astype(result.dtype)


def modulation_kernel(conds, ada, part_out, ordered):
    groups, rows, _ = ordered.shape
    for group in range(groups):
        ordered[group] = conds[group, 0:rows, 0 : ada.shape[0]]
        part_out[group * rows : (group + 1) * rows, :] = dot_nn(ordered[group], ada[...])


def prepare_kernel(packing, sub, clips, *refs):
    timesteps, labels, time_table, class_table, qkv, proj_t, up, down_t, packed, send = refs
    packed[...] = packing.pack(qkv[...], proj_t[...].T)
    row_parts = send.shape[0]

    def look_up(indices, table):
        count = table.shape[0]
        row = lax.broadcasted_iota(jnp.int32, (16, count), 0)
        column = lax.broadcasted_iota(jnp.int32, (16, count), 1)
        picked = jnp.zeros((16, count), jnp.bool_)
        for clip in range(clips):
            picked = picked | ((row == clip) & (column == indices[clip]))
        return dot_nn(picked.astype(F32).astype(LOW), table[...])

    embedded = look_up(timesteps, time_table) + look_up(labels, class_table)
    cond = (embedded * (1.0 / (1.0 + jnp.exp(-embedded)))).astype(LOW)
    up_t = up[...].T
    height = send.shape[2]
    pairs = height // sub
    for part in range(row_parts):
        send[part, 0:sub] = up_t[part * sub : (part + 1) * sub, :]
        send[part, 2 * sub :] = cond[:, part * height : (part + 1) * height]
        for pair in range(pairs):
            start = (pair * row_parts + part) * sub
            send[part, sub : 2 * sub, pair * sub : (pair + 1) * sub] = down_t[:, start : start + sub]


def feed_finish_kernel(back, up_grad, down_grad_t):
    parts, _, sub, height = back.shape
    pairs = height // sub
    for part in range(parts):
        up_grad[:, part * sub : (part + 1) * sub] = back[part, 0].astype(F32).T
        for pair in range(pairs):
            start = (pair * parts + part) * sub
            down_grad_t[:, start : start + sub] = back[
                part, 1, :, pair * sub : (pair + 1) * sub
            ].astype(F32)


def attn_finish_kernel(packing, *refs):
    total = refs[0][...].astype(F32)
    for ref in refs[1:-2]:
        total += ref[...].astype(F32)
    qkv_grad, proj_grad_t = refs[-2:]
    for side in range(2):
        rows = slice(side * packing.half, (side + 1) * packing.half)
        qkv_grad[rows, :] = packing.qkv_of(total, side)
        proj_grad_t[:, rows] = packing.proj_of(total, side).T


VMEM_SPEC = pl.BlockSpec(memory_space=pltpu.VMEM)
SMEM_SPEC = pl.BlockSpec(memory_space=pltpu.SMEM)
ANY_SPEC = pl.BlockSpec(memory_space=pl.ANY)
PARAMS = pltpu.CompilerParams(vmem_limit_bytes=56 * 1024 * 1024)


def shape_of(dims, kind=LOW):
    return jax.ShapeDtypeStruct(dims, kind)


def cost(micros):
    return pl.CostEstimate(flops=1000, bytes_accessed=int(micros * SCALE), transcendentals=0)


def after(value, *others):
    return lax.optimization_barrier((value,) + others)[0]


class Sequence:
    def __init__(self):
        self.token = None

    def call(self, kernel, shapes, arrays, name, specs=None, scratch=(), tied=0, out_spec=None):
        arrays = list(arrays)
        if self.token is not None:
            arrays[tied] = after(arrays[tied], self.token)
        results = pl.pallas_call(
            kernel,
            out_shape=shapes,
            in_specs=specs or [VMEM_SPEC] * len(arrays),
            out_specs=jax.tree.map(lambda _: out_spec or VMEM_SPEC, shapes),
            scratch_shapes=scratch,
            compiler_params=PARAMS,
            cost_estimate=cost(1),
            name=name,
        )(*arrays)
        self.token = min(jax.tree.leaves(results), key=lambda result: result.size)
        return results

    def sum_low(self, *arrays):
        total = after(arrays[0], self.token).astype(F32)
        for array in arrays[1:]:
            total += array.astype(F32)
        self.token = total.astype(LOW)
        return self.token


def swap(value, mask, count):
    return lax.ppermute(value, AXES, [(i, i ^ mask) for i in range(count)])


def padded_exchange(rows, count):
    length = rows.shape[1]
    tiles = -(-length // 1024) * 8
    rows = jnp.pad(rows, ((0, 0), (0, tiles * 128 - length))).reshape(count, tiles, 128)
    got = lax.all_to_all(rows, AXES, 0, 0, tiled=True)
    return got.reshape(count, tiles * 128)[:, :length]


def fast_body(
    column_parts,
    row_parts,
    inputs,
    out_cotangent,
    lengths,
    timesteps,
    labels,
    time_table,
    class_table,
    ada_weight,
    qkv_weight,
    proj_weight,
    up_weight,
    down_weight,
):
    count = column_parts * row_parts
    clips, positions, frames, width = inputs.shape
    span = positions * frames
    row_count = clips * span
    qkv_cols, proj_cols = qkv_weight.shape[1], proj_weight.shape[1]
    height = qkv_weight.shape[0]
    part_width = width // row_parts
    hidden_part = up_weight.shape[1] * column_parts // row_parts
    sub = up_weight.shape[1] // row_parts
    x_mask = row_parts
    z_masks = tuple(row_parts * 2 * i for i in range(1, column_parts // 2))
    packing = Packing(height // 2, qkv_cols, proj_cols)

    line = Sequence()
    packed, both_send = line.call(
        functools.partial(prepare_kernel, packing, sub, clips),
        (
            shape_of((height // 2, packing.width)),
            shape_of((row_parts, 2 * sub + 16, height)),
        ),
        (timesteps, labels, time_table, class_table)
        + (qkv_weight, proj_weight.T, up_weight, down_weight.T),
        "prepare",
        [SMEM_SPEC] * 2 + [VMEM_SPEC] * 6,
    )

    y_mask, c_mask = 2, 1
    ada_cols = ada_weight.shape[1]

    def gate(*values):
        return lax.optimization_barrier(values)

    own = packed[None]
    far = [swap(own, mask, count) for mask in z_masks]
    own_x, own_y = swap(own, x_mask, count), swap(own, y_mask, count)
    both_got = lax.all_to_all(both_send, "fsdp", 0, 0, tiled=True)
    *far, own_x, own_y, both_got = gate(*far, own_x, own_y, both_got)
    own_feed = both_got[:, : 2 * sub].reshape(row_parts, 2, sub, height)
    own_feed = own_feed.transpose(1, 2, 0, 3).reshape(2 * sub, width)
    conds = both_got[:, 2 * sub : 2 * sub + clips].reshape(row_parts * clips, height)
    feed = lax.all_gather(own_feed, "dp", axis=0, tiled=True)

    far = jnp.concatenate(far)
    pads = (-row_parts * clips % 16, -height % 128)
    conds = jnp.pad(conds, ((0, pads[0]), (0, pads[1])))
    conds = jnp.broadcast_to(conds[None], (column_parts,) + conds.shape)
    conds = lax.all_to_all(conds, "dp", 0, 0, tiled=True)
    far_x, far_y = swap(far, x_mask, count), swap(far, y_mask, count)
    cores = [swap(array, c_mask, count) for array in (own, own_x, own_y, far)]
    far_x, far_y, conds, *cores = gate(far_x, far_y, conds, *cores)

    mod_part, conds = line.call(
        modulation_kernel,
        (
            shape_of((count * clips, ada_cols), F32),
            shape_of((column_parts, row_parts * clips, part_width)),
        ),
        (conds, ada_weight),
        "modulation",
    )
    cond_all = conds.reshape(count * clips, part_width)
    mod_got = padded_exchange(mod_part.reshape(count, clips * ada_cols), count)
    own_xy, far_xy = swap(own_x, y_mask, count), swap(far_x, y_mask, count)
    cores += [swap(array, c_mask, count) for array in (far_x, far_y)]
    own_xy, far_xy, mod_got, *cores = gate(own_xy, far_xy, mod_got, *cores)
    mod_own = jnp.sum(mod_got.reshape(column_parts, row_parts, clips, ada_cols), axis=1)
    mod = mod_own.transpose(1, 0, 2).reshape(clips, 6, width)
    cores += [swap(array, c_mask, count) for array in (own_xy, far_xy)]

    blocks = [own, own_x, own_y, far, far_x, far_y, own_xy, far_xy]
    places = [[0], [x_mask], [y_mask], list(z_masks)]
    places += [[z ^ side for z in z_masks] for side in (x_mask, y_mask)]
    places += [[x_mask ^ y_mask]]
    places += [[z ^ x_mask ^ y_mask for z in z_masks]]
    blocks += cores
    places += [[place ^ c_mask for place in held] for held in places]

    tokens = inputs.reshape(row_count, width)
    cotangent = out_cotangent.reshape(row_count, width)
    gate_two = jnp.repeat(mod[:, 5], span, axis=0)
    d_out = (cotangent.astype(F32) * gate_two).astype(LOW)
    d_outs = {0: d_out, 1: swap(d_out, 1, count), 2: swap(d_out, 2, count)}
    d_outs[3] = swap(d_outs[2], 1, count)
    sizes = (clips, span, frames, width, 32)
    full = (row_count, width)
    weight_scratch = pltpu.VMEM((column_parts, row_parts, height // 2, packing.width), LOW)
    weight_sems = pltpu.SemaphoreType.DMA((count,))
    hidden, mixed, probs, attended, branch, middle, hidden_two, proj_full = line.call(
        functools.partial(attn_forward_kernel, sizes, packing, places),
        (
            shape_of((width, row_count)),
            shape_of((column_parts, row_count, qkv_cols)),
            shape_of((clips, HEADS, span, span)),
            shape_of((width, row_count)),
            shape_of(full),
            shape_of(full, F32),
            shape_of(full),
            shape_of((width, width)),
        ),
        (lengths, tokens, mod, *blocks),
        "attn_forward",
        [SMEM_SPEC, VMEM_SPEC, VMEM_SPEC] + [ANY_SPEC] * len(blocks),
        (
            weight_scratch,
            pltpu.VMEM(full, F32),
            pltpu.VMEM(full, LOW),
            pltpu.VMEM(full, LOW),
            weight_sems,
        ),
        tied=2,
    )

    tokens_two = {0: hidden_two, 1: swap(hidden_two, 1, count), 2: swap(hidden_two, 2, count)}
    pair = (2 * row_count, width)
    pair_hidden = (2 * row_count, hidden_part)
    feed_scratch = (
        pltpu.VMEM(pair, LOW),
        pltpu.VMEM(pair, LOW),
        pltpu.VMEM((hidden_part, width), LOW),
        pltpu.VMEM((width, hidden_part), LOW),
        pltpu.VMEM(pair_hidden, F32),
        pltpu.VMEM(pair_hidden, F32),
        pltpu.VMEM(pair_hidden, LOW),
        pltpu.VMEM(pair_hidden, LOW),
        pltpu.VMEM(full, F32),
        pltpu.VMEM(full, LOW),
        pltpu.SemaphoreType.DMA((2, 2)),
        pltpu.SemaphoreType.DMA((column_parts, 2)),
        pltpu.SemaphoreType.DMA((6,)),
    )

    def feed_call(index, name):
        return line.call(
            functools.partial(feed_kernel, 32, column_parts),
            [shape_of((row_count, hidden_part))] * 4 + [shape_of(full, F32), shape_of(full)],
            (
                tokens_two[index],
                tokens_two[index + 1],
                d_outs[index],
                d_outs[index + 1],
                feed,
            ),
            name,
            [ANY_SPEC] * 5,
            feed_scratch,
            out_spec=ANY_SPEC,
        )

    near = feed_call(0, "feed_near")
    tokens_two[2] = after(tokens_two[2], line.token)
    tokens_two[3] = swap(tokens_two[2], 1, count)
    distant = feed_call(2, "feed_distant")

    grad_send = line.sum_low(distant[4], swap(distant[5], 1, count))
    grad_far = swap(grad_send, 2, count)
    grad_parts = (near[4], swap(near[5], 1, count), grad_far)
    feed_grads, *partials = line.call(
        functools.partial(feed_weight_kernel, column_parts),
        [shape_of((column_parts, 2 * sub, width))]
        + [shape_of(full, F32), shape_of(full)]
        + [shape_of(full)] * 2,
        [tokens_two[i] for i in range(4)]
        + [d_outs[i] for i in range(4)]
        + [*near[0:2], *distant[0:2], *near[2:4], *distant[2:4], feed],
        "feed_weight",
        [VMEM_SPEC] * 16 + [ANY_SPEC],
        (pltpu.VMEM((width, hidden_part), LOW), pltpu.SemaphoreType.DMA((column_parts,))),
    )
    feed_grads = feed_grads.reshape(2 * sub * column_parts, width)
    feed_grads, grad_far = lax.optimization_barrier((feed_grads, grad_far))
    grad_parts = grad_parts[:2] + (grad_far,)
    line.token = grad_far
    groups = column_parts // 2
    feed_sum = lax.psum_scatter(feed_grads, "dp", scatter_dimension=0, tiled=True)

    out_send = line.sum_low(partials[2], swap(partials[3], 1, count))
    out_far = swap(out_send, 2, count)
    d_middle, d_branch, d_attended, d_mod_two = line.call(
        functools.partial(proj_backward_kernel, sizes),
        (
            shape_of(full, F32),
            shape_of(full),
            shape_of(full),
            shape_of((clips, 3, width), F32),
        ),
        (cotangent, mod, middle, branch, *grad_parts, proj_full),
        "proj_backward",
    )
    d_mixed = line.call(
        functools.partial(attn_backward_kernel, (clips, span, frames, width, qkv_cols)),
        shape_of((column_parts, row_count, -(-qkv_cols // 128) * 128)),
        (mixed, probs, d_attended),
        "attn_backward",
    )
    own_side = (hidden, attended, d_mixed, d_branch)
    far_side = [swap(array, 1, count) for array in own_side]
    attn_grads, first = {}, {}
    for distances in (range(groups - 1, groups // 2 - 1, -1), range(groups // 2 - 1, -1, -1)):
        grads = line.call(
            functools.partial(attn_weight_kernel, packing, distances),
            [shape_of((2, height // 2, packing.width))] * (2 * len(distances)),
            (*own_side, *far_side),
            "attn_weight",
            scratch=(pltpu.VMEM((column_parts, 2 * row_count, proj_cols), LOW),),
        )
        for index, distance in enumerate(distances):
            attn_grads[distance] = grads[2 * index]
            first[distance] = swap(grads[2 * index + 1], y_mask, count)
        if not len(distances) < len(first):
            ffn_out = after(partials[0], line.token) + swap(partials[1], 1, count).astype(F32)
            ffn_out += out_far.astype(F32)
            result = (middle + gate_two * ffn_out).astype(LOW).reshape(inputs.shape)
            d_gate_two = jnp.sum(
                (cotangent.astype(F32) * ffn_out).reshape(clips, 1, span, width), axis=2
            )
            line.token = d_gate_two
    input_grad, d_mod_one = line.call(
        functools.partial(qkv_backward_kernel, sizes, packing, places),
        (shape_of(full), shape_of((clips, 2, width), F32)),
        (tokens, mod, d_middle, d_mixed, *blocks),
        "qkv_backward",
        [VMEM_SPEC] * 4 + [ANY_SPEC] * len(blocks),
        (weight_scratch, pltpu.VMEM(full, F32), weight_sems),
    )
    stay, second, attn_z = {}, {}, {}

    def split_sum(index):
        kept = after(attn_grads[index], line.token)
        stay[index] = kept[0].astype(F32) + first[index][0].astype(F32)
        leave = (kept[1].astype(F32) + first[index][1].astype(F32)).astype(LOW)
        line.token = leave
        second[index] = swap(leave, x_mask, count)

    def attn_sum(index):
        summed = line.sum_low(stay[index], second[index])
        attn_z[index] = swap(summed, z_masks[index - 1], count)

    d_mod = jnp.concatenate([d_mod_one, d_mod_two, d_gate_two], axis=1)
    mod_send = d_mod.reshape(clips, column_parts, ada_cols).transpose(1, 0, 2)
    mod_send = jnp.broadcast_to(
        mod_send.reshape(column_parts, 1, clips * ada_cols),
        (column_parts, row_parts, clips * ada_cols),
    ).reshape(count, clips * ada_cols)
    d_mod_all = padded_exchange(mod_send, count).reshape(count * clips, ada_cols)
    split_sum(3)
    line.token, d_mod_all = lax.optimization_barrier((line.token, d_mod_all))
    split_sum(2)
    attn_sum(3)
    attn_sum(2)
    split_sum(1)
    back = feed_sum.reshape(2, sub, row_parts, height).transpose(2, 0, 1, 3)
    line.token, back = lax.optimization_barrier((line.token, back))
    back = lax.all_to_all(back, "fsdp", 0, 0, tiled=True)
    split_sum(0)
    attn_sum(1)
    up_grad, down_grad_t = line.call(
        feed_finish_kernel,
        (shape_of(up_weight.shape, F32), shape_of(down_weight.shape[::-1], F32)),
        (back,),
        "feed_finish",
    )
    down_grad = down_grad_t.T
    qkv_grad, proj_grad_t = line.call(
        functools.partial(attn_finish_kernel, packing),
        (shape_of((height, qkv_cols), F32), shape_of((proj_cols, height), F32)),
        (stay[0], second[0], attn_z[3], attn_z[2], attn_z[1]),
        "attn_finish",
    )
    proj_grad = proj_grad_t.T

    ada_grad = lax.dot_general(
        cond_all.astype(F32),
        d_mod_all,
        (((0,), (0,)), ((), ())),
        precision=lax.Precision.HIGHEST,
        preferred_element_type=F32,
    )
    return (
        result,
        input_grad.reshape(inputs.shape),
        ada_grad,
        qkv_grad,
        proj_grad,
        up_grad,
        down_grad,
    )


def solution(mesh):
    column_parts, row_parts = mesh.shape["dp"], mesh.shape["fsdp"]
    body = general_body
    if (column_parts, row_parts) == (8, 4):
        body = functools.partial(fast_body, column_parts, row_parts)
    clip_spec = P(AXES, None, None, None)
    return jax.shard_map(
        body,
        mesh=mesh,
        in_specs=(
            clip_spec,
            clip_spec,
            P(AXES),
            P(AXES),
            P(AXES),
            P(),
            P(),
        )
        + (P("fsdp", "dp"),) * 5,
        out_specs=(clip_spec, clip_spec) + (P("fsdp", "dp"),) * 5,
        check_vma=False,
    )
```

```python
import functools
import math

import jax
import jax.numpy as jnp
from jax import lax
from jax.experimental import pallas as pl
from jax.experimental.pallas import tpu as pltpu
from jax.sharding import PartitionSpec as P

HEADS = 16
AXES = ("dp", "fsdp")
EPS = 1e-06
F32, LOW = jnp.float32, jnp.bfloat16
SCALE = 100


def norm_mod(values, shift_add, scale_mul):
    center = values - jnp.mean(values, -1, keepdims=True)
    spread = jnp.mean(center * center, -1, keepdims=True)
    return center * lax.rsqrt(spread + 1e-06) * (1.0 + scale_mul) + shift_add


def gelu_tanh(values):
    return jax.nn.gelu(values, approximate=True)


def gather_five(shards):
    row_set = (
        lax.all_gather(shards[0], "fsdp", axis=0, tiled=True),
        lax.all_gather(shards[1], "fsdp", axis=0, tiled=True),
        lax.all_gather(shards[2], "fsdp", axis=0, tiled=True),
        lax.all_gather(shards[3], "fsdp", axis=0, tiled=True),
        lax.all_gather(shards[4], "fsdp", axis=0, tiled=True),
    )
    return (
        lax.all_gather(row_set[0], "dp", axis=1, tiled=True),
        lax.all_gather(row_set[1], "dp", axis=1, tiled=True),
        lax.all_gather(row_set[2], "dp", axis=1, tiled=True),
        lax.all_gather(row_set[3], "dp", axis=1, tiled=True),
        lax.all_gather(row_set[4], "dp", axis=1, tiled=True),
    )


def scatter_five(totals):
    row_set = (
        lax.psum_scatter(
            totals[0].astype(jnp.bfloat16), "fsdp", scatter_dimension=0, tiled=True
        ).astype(jnp.float32),
        lax.psum_scatter(
            totals[1].astype(jnp.bfloat16), "fsdp", scatter_dimension=0, tiled=True
        ).astype(jnp.float32),
        lax.psum_scatter(
            totals[2].astype(jnp.bfloat16), "fsdp", scatter_dimension=0, tiled=True
        ).astype(jnp.float32),
        lax.psum_scatter(
            totals[3].astype(jnp.bfloat16), "fsdp", scatter_dimension=0, tiled=True
        ).astype(jnp.float32),
        lax.psum_scatter(
            totals[4].astype(jnp.bfloat16), "fsdp", scatter_dimension=0, tiled=True
        ).astype(jnp.float32),
    )
    return (
        lax.psum_scatter(
            row_set[0].astype(jnp.bfloat16), "dp", scatter_dimension=1, tiled=True
        ).astype(jnp.float32),
        lax.psum_scatter(
            row_set[1].astype(jnp.bfloat16), "dp", scatter_dimension=1, tiled=True
        ).astype(jnp.float32),
        lax.psum_scatter(
            row_set[2].astype(jnp.bfloat16), "dp", scatter_dimension=1, tiled=True
        ).astype(jnp.float32),
        lax.psum_scatter(
            row_set[3].astype(jnp.bfloat16), "dp", scatter_dimension=1, tiled=True
        ).astype(jnp.float32),
        lax.psum_scatter(
            row_set[4].astype(jnp.bfloat16), "dp", scatter_dimension=1, tiled=True
        ).astype(jnp.float32),
    )


def fetch_weights(ada_weight, core_shards):
    return tuple(gather_five((ada_weight,) + tuple(core_shards)))


def matmul_tn(left, right):
    return lax.dot_general(
        left, right, (((0,), (0,)), ((), ())), preferred_element_type=jnp.float32
    )


def matmul_nt(left, right):
    return lax.dot_general(
        left, right, (((1,), (1,)), ((), ())), preferred_element_type=jnp.float32
    )


def general_body(
    inputs,
    out_cotangent,
    lengths,
    timesteps,
    labels,
    time_table,
    class_table,
    ada_weight,
    qkv_weight,
    proj_weight,
    up_weight,
    down_weight,
):
    core_shards = (qkv_weight, proj_weight, up_weight, down_weight)
    clip_count, positions, frames, model_width = inputs.shape
    row_count = clip_count * positions * frames
    seq_count = clip_count * positions
    span = positions * frames
    head_size = model_width // HEADS
    attn_scale = 1.0 / math.sqrt(head_size)
    ada_full, qkv_full, proj_full, up_full, down_full = fetch_weights(ada_weight, core_shards)
    time_onehot = (timesteps[:, None] == lax.iota(jnp.int32, time_table.shape[0])[None, :]).astype(
        jnp.bfloat16
    )
    class_onehot = (labels[:, None] == lax.iota(jnp.int32, class_table.shape[0])[None, :]).astype(
        jnp.bfloat16
    )
    embedded = jnp.dot(time_onehot, time_table, preferred_element_type=jnp.float32) + jnp.dot(
        class_onehot, class_table, preferred_element_type=jnp.float32
    )
    cond_low = jax.nn.silu(embedded).astype(jnp.bfloat16)
    modulation = jnp.dot(cond_low, ada_full, preferred_element_type=jnp.float32)
    pieces = [
        modulation[:, None, offset * model_width : (offset + 1) * model_width]
        for offset in range(6)
    ]
    shift_one, scale_one, gate_one, shift_two, scale_two, gate_two = pieces
    residual = inputs.astype(jnp.float32).reshape(clip_count, span, model_width)
    hidden_one = (
        norm_mod(residual, shift_one, scale_one)
        .astype(jnp.bfloat16)
        .reshape(row_count, model_width)
    )
    mixed = jnp.dot(hidden_one, qkv_full, preferred_element_type=jnp.float32).astype(jnp.bfloat16)
    shaped = mixed.reshape(seq_count, frames, 3, HEADS, head_size)
    queries = shaped[:, :, 0]
    key_part = shaped[:, :, 1]
    value_part = shaped[:, :, 2]
    clip_live = lax.iota(jnp.int32, frames)[None, :] < lengths[:, None]
    key_live = jnp.repeat(clip_live, positions, axis=0)
    scores = (
        jnp.einsum("sqhe,skhe->shqk", queries, key_part, preferred_element_type=jnp.float32)
        * attn_scale
    )
    scores = jnp.where(key_live[:, None, None, :], scores, -1e30)
    row_max = jnp.max(scores, -1, keepdims=True)
    exp_scores = jnp.exp(scores - row_max)
    attn_probs = exp_scores / jnp.sum(exp_scores, -1, keepdims=True)
    probs_low = attn_probs.astype(jnp.bfloat16)
    attended = jnp.einsum(
        "shqk,skhe->sqhe", probs_low, value_part, preferred_element_type=jnp.float32
    )
    attended_low = attended.astype(jnp.bfloat16).reshape(row_count, model_width)
    branch = jnp.dot(attended_low, proj_full, preferred_element_type=jnp.float32).reshape(
        clip_count, span, model_width
    )
    middle = residual + gate_one * branch
    hidden_two = (
        norm_mod(middle, shift_two, scale_two).astype(jnp.bfloat16).reshape(row_count, model_width)
    )
    up_proj = jnp.dot(hidden_two, up_full, preferred_element_type=jnp.float32)
    activ_low = gelu_tanh(up_proj).astype(jnp.bfloat16)
    ffn_out = jnp.dot(activ_low, down_full, preferred_element_type=jnp.float32).reshape(
        clip_count, span, model_width
    )
    result = (middle + gate_two * ffn_out).astype(jnp.bfloat16).reshape(inputs.shape)
    ada_full, qkv_full, proj_full, up_full, down_full = fetch_weights(ada_weight, core_shards)
    grad_out = out_cotangent.astype(jnp.float32).reshape(clip_count, span, model_width)
    d_gate_two = jnp.sum(grad_out * ffn_out, axis=1)
    d_ffn = (grad_out * gate_two).astype(jnp.bfloat16).reshape(row_count, model_width)
    d_activ = matmul_nt(d_ffn, down_full)
    down_total = matmul_tn(activ_low, d_ffn)
    gelu_value, gelu_pull = jax.vjp(gelu_tanh, up_proj)
    d_up = gelu_pull(d_activ)[0].astype(jnp.bfloat16)
    d_hidden_two = matmul_nt(d_up, up_full)
    up_total = matmul_tn(hidden_two, d_up)
    norm_value, norm_pull = jax.vjp(norm_mod, middle, shift_two, scale_two)
    d_middle_norm, d_shift_two, d_scale_two = norm_pull(
        d_hidden_two.reshape(clip_count, span, model_width)
    )
    d_middle = grad_out + d_middle_norm
    d_gate_one = jnp.sum(d_middle * branch, axis=1)
    d_branch = (d_middle * gate_one).astype(jnp.bfloat16).reshape(row_count, model_width)
    d_attended = (
        matmul_nt(d_branch, proj_full)
        .astype(jnp.bfloat16)
        .reshape(seq_count, frames, HEADS, head_size)
    )
    proj_total = matmul_tn(attended_low, d_branch)
    d_value = jnp.einsum(
        "shqk,sqhe->skhe", probs_low, d_attended, preferred_element_type=jnp.float32
    )
    d_probs = jnp.einsum(
        "sqhe,skhe->shqk", d_attended, value_part, preferred_element_type=jnp.float32
    )
    d_scores = attn_probs * (d_probs - jnp.sum(attn_probs * d_probs, -1, keepdims=True))
    d_scores_low = d_scores.astype(jnp.bfloat16)
    d_query = (
        jnp.einsum("shqk,skhe->sqhe", d_scores_low, key_part, preferred_element_type=jnp.float32)
        * attn_scale
    )
    d_key = (
        jnp.einsum("shqk,sqhe->skhe", d_scores_low, queries, preferred_element_type=jnp.float32)
        * attn_scale
    )
    d_mixed = (
        jnp.stack([d_query, d_key, d_value], axis=2)
        .astype(jnp.bfloat16)
        .reshape(row_count, 3 * model_width)
    )
    d_hidden_one = matmul_nt(d_mixed, qkv_full)
    qkv_total = matmul_tn(hidden_one, d_mixed)
    norm_first, first_pull = jax.vjp(norm_mod, residual, shift_one, scale_one)
    d_input_norm, d_shift_one, d_scale_one = first_pull(
        d_hidden_one.reshape(clip_count, span, model_width)
    )
    input_grad = (d_middle + d_input_norm).astype(jnp.bfloat16).reshape(inputs.shape)
    d_modulation = jnp.concatenate(
        [
            d_shift_one[:, 0],
            d_scale_one[:, 0],
            d_gate_one,
            d_shift_two[:, 0],
            d_scale_two[:, 0],
            d_gate_two,
        ],
        axis=-1,
    )
    ada_total = jnp.dot(
        cond_low.astype(jnp.float32).T, d_modulation, precision=lax.Precision.HIGHEST
    )
    ada_grad, qkv_grad, proj_grad, up_grad, down_grad = scatter_five(
        (ada_total, qkv_total, proj_total, up_total, down_total)
    )
    return (result, input_grad, ada_grad, qkv_grad, proj_grad, up_grad, down_grad)


def dot_nn(left, right):
    return lax.dot_general(left, right, (((1,), (0,)), ((), ())), preferred_element_type=F32)


def dot_nt(left, right):
    return lax.dot_general(left, right, (((1,), (1,)), ((), ())), preferred_element_type=F32)


def dot_tn(left, right):
    return lax.dot_general(left, right, (((0,), (0,)), ((), ())), preferred_element_type=F32)


def stats(values):
    mean = jnp.mean(values, -1, keepdims=True)
    center = values - mean
    spread = jnp.mean(center * center, -1, keepdims=True)
    inverse = lax.rsqrt(spread + EPS)
    return center * inverse, inverse


def here(names):
    return lax.axis_index(names[0]), lax.axis_index(names[1])


def start_blocks(places, block_refs, weight_ref, sems):
    column, row = here(AXES)
    row_parts = weight_ref.shape[1]
    copies = {}
    for ref, held in zip(block_refs, places):
        for index, relative in enumerate(held):
            copy = pltpu.make_async_copy(
                ref.at[index],
                weight_ref.at[column ^ (relative // row_parts), row ^ (relative % row_parts)],
                sems.at[relative],
            )
            copy.start()
            copies[relative] = copy
    return [copies[relative] for relative in sorted(copies)]


class Packing:
    def __init__(self, half, qkv_cols, proj_cols):
        self.half, self.qkv_cols, self.proj_cols = half, qkv_cols, proj_cols
        self.qkv_main, self.proj_main = qkv_cols // 128 * 128, proj_cols // 128 * 128
        self.qkv_rest, self.proj_rest = qkv_cols - self.qkv_main, proj_cols - self.proj_main
        self.rest = self.qkv_rest + self.proj_rest
        self.proj_start = 2 * self.qkv_main
        self.rest_start = self.proj_start + 2 * self.proj_main
        self.width = self.rest_start + 2 * self.rest

    def pack(self, qkv, proj):
        halves = [slice(i * self.half, (i + 1) * self.half) for i in range(2)]
        return jnp.concatenate(
            [qkv[rows, : self.qkv_main] for rows in halves]
            + [proj[rows, : self.proj_main] for rows in halves]
            + [
                piece
                for rows in halves
                for piece in (qkv[rows, self.qkv_main :], proj[rows, self.proj_main :])
            ],
            axis=1,
        )

    def qkv_of(self, block, side):
        rest = self.rest_start + side * self.rest
        return jnp.concatenate(
            [
                block[:, side * self.qkv_main : (side + 1) * self.qkv_main],
                block[:, rest : rest + self.qkv_rest],
            ],
            axis=1,
        )

    def proj_of(self, block, side):
        main = self.proj_start + side * self.proj_main
        rest = self.rest_start + side * self.rest + self.qkv_rest
        return jnp.concatenate(
            [block[:, main : main + self.proj_main], block[:, rest : rest + self.proj_rest]],
            axis=1,
        )

    def unpack(self, block):
        return tuple(
            jnp.concatenate([part(block, side) for side in range(2)], axis=0)
            for part in (self.qkv_of, self.proj_of)
        )


def pair_mask(span, frames, live):
    query = lax.broadcasted_iota(jnp.int32, (span, span), 0)
    key = lax.broadcasted_iota(jnp.int32, (span, span), 1)
    return ((query // frames) == (key // frames)) & ((key % frames) < live)


def head_groups(count, size):
    return [range(start, start + size) for start in range(0, count, size)]


def head_slices(ref, which, head, rows, size):
    per = ref.shape[2] // size
    slot = which * HEADS + head
    return ref[slot // per, rows, (slot % per) * size : (slot % per + 1) * size]


def columns_of(ref, rows, index, size):
    return ref[rows, index * size : (index + 1) * size]


def join_proj(packing, weight, proj):
    for place in range(weight.shape[0]):
        start = place * packing.proj_cols
        for part in range(weight.shape[1]):
            for side in range(2):
                row = (2 * part + side) * packing.half
                proj[row : row + packing.half, start : start + packing.proj_cols] = packing.proj_of(
                    weight.at[place, part], side
                )


def attn_forward_kernel(sizes, packing, places, *refs):
    clips, span, frames, width, chunk = sizes
    blocks = len(places)
    lengths, tokens, mod = refs[:3]
    block_refs = refs[3 : 3 + blocks]
    hidden, mixed, probs_out, attended, branch, middle, hidden_two, proj = refs[3 + blocks : 11 + blocks]
    weight, branch_full, hidden_s, attended_s, sems = refs[11 + blocks :]
    copies = start_blocks(places, block_refs, weight, sems)
    column_parts, row_parts = weight.shape[0], weight.shape[1]
    size = width // HEADS
    scale = 1.0 / math.sqrt(size)

    def first_norm(step, carry):
        rows = pl.ds(pl.multiple_of(step * chunk, chunk), chunk)
        clip_mod = mod[step * chunk // span]
        unit, _ = stats(tokens[rows, :].astype(F32))
        hidden_s[rows, :] = (unit * (1.0 + clip_mod[1:2]) + clip_mod[0:1]).astype(LOW)
        return carry

    lax.fori_loop(0, clips * span // chunk, first_norm, 0)
    column, row = here(AXES)
    for relative in range(column_parts):
        for other in range(row_parts):
            copies[relative * row_parts + other].wait()
        place = column ^ relative
        columns = jnp.concatenate(
            [
                packing.qkv_of(weight.at[place, part], side)
                for part in range(row_parts)
                for side in range(2)
            ],
            axis=0,
        )
        mixed[place] = dot_nn(hidden_s[...], columns).astype(LOW)

    for clip in range(clips):
        rows = slice(clip * span, (clip + 1) * span)
        live_mask = pair_mask(span, frames, lengths[clip])
        for group in head_groups(HEADS, 4):
            scores = [
                dot_nt(
                    head_slices(mixed, 0, head, rows, size), head_slices(mixed, 1, head, rows, size)
                )
                for head in group
            ]
            scores = [jnp.where(live_mask, score * scale, -1e30) for score in scores]
            exps = [jnp.exp(score - jnp.max(score, -1, keepdims=True)) for score in scores]
            probs = [(e * (1.0 / jnp.sum(e, -1, keepdims=True))).astype(LOW) for e in exps]
            values = [
                dot_nn(prob, head_slices(mixed, 2, head, rows, size))
                for head, prob in zip(group, probs)
            ]
            for head, prob, value in zip(group, probs, values):
                probs_out[clip, head] = prob
                attended_s[rows, head * size : (head + 1) * size] = value.astype(LOW)

    join_proj(packing, weight, proj)
    branch_full[...] = dot_nn(attended_s[...], proj[...])

    def second_norm(step, carry):
        rows = pl.ds(pl.multiple_of(step * chunk, chunk), chunk)
        clip_mod = mod[step * chunk // span]
        value = branch_full[rows, :]
        branch[rows, :] = value.astype(LOW)
        value = tokens[rows, :].astype(F32) + clip_mod[2:3] * value
        middle[rows, :] = value
        unit, _ = stats(value)
        hidden_two[rows, :] = (unit * (1.0 + clip_mod[4:5]) + clip_mod[3:4]).astype(LOW)
        return carry

    lax.fori_loop(0, clips * span // chunk, second_norm, 0)
    hidden[...] = hidden_s[...].T
    attended[...] = attended_s[...].T


def norm_back(grad, values, scale_row):
    unit, inverse = stats(values)
    d_unit = grad * (1.0 + scale_row)
    d_value = inverse * (
        d_unit
        - jnp.mean(d_unit, -1, keepdims=True)
        - unit * jnp.mean(d_unit * unit, -1, keepdims=True)
    )
    return unit, d_value


def proj_backward_kernel(sizes, *refs):
    clips, span, frames, width, chunk = sizes
    cotangent, mod, middle, branch, grad_own, grad_core, grad_far, proj = refs[:8]
    d_middle, d_branch, d_attended, d_mod = refs[8:]
    zero_row = jnp.zeros((1, width), F32)
    steps = span // chunk
    for clip in range(clips):
        clip_mod = mod[clip]

        def second_back(step, carry, clip=clip, clip_mod=clip_mod):
            d_shift, d_scale, d_gate = carry
            rows = pl.ds(pl.multiple_of(clip * span + step * chunk, chunk), chunk)
            grad = grad_own[rows, :] + grad_core[rows, :].astype(F32)
            grad += grad_far[rows, :].astype(F32)
            unit, d_value = norm_back(grad, middle[rows, :], clip_mod[4:5])
            d_value = cotangent[rows, :].astype(F32) + d_value
            d_middle[rows, :] = d_value
            d_branch[rows, :] = (d_value * clip_mod[2:3]).astype(LOW)
            return (
                d_shift + jnp.sum(grad, 0, keepdims=True),
                d_scale + jnp.sum(grad * unit, 0, keepdims=True),
                d_gate + jnp.sum(d_value * branch[rows, :].astype(F32), 0, keepdims=True),
            )

        sums = lax.fori_loop(0, steps, second_back, (zero_row, zero_row, zero_row))
        d_mod[clip, 0:1, :] = sums[2]
        d_mod[clip, 1:2, :] = sums[0]
        d_mod[clip, 2:3, :] = sums[1]

    d_attended[...] = dot_nt(d_branch[...], proj[...]).astype(LOW)


def attn_backward_kernel(sizes, *refs):
    clips, span, frames, width, qkv_cols = sizes
    mixed, probs_ref, d_attended, d_mixed = refs
    size = width // HEADS
    scale = 1.0 / math.sqrt(size)
    cols = qkv_cols // size
    for clip in range(clips):
        rows = slice(clip * span, (clip + 1) * span)
        for group in head_groups(HEADS, 4):
            queries, keys, values = (
                [head_slices(mixed, which, head, rows, size) for head in group]
                for which in range(3)
            )
            probs = [probs_ref[clip, head] for head in group]
            grads = [columns_of(d_attended, rows, head, size) for head in group]
            d_probs = [dot_nt(grad, value) for grad, value in zip(grads, values)]
            d_values = [dot_tn(prob, grad) for prob, grad in zip(probs, grads)]
            d_scores = []
            for prob, d_prob in zip(probs, d_probs):
                prob = prob.astype(F32)
                inner = jnp.sum(prob * d_prob, -1, keepdims=True)
                d_scores.append((prob * (d_prob - inner) * scale).astype(LOW))
            d_queries = [dot_nn(score, key) for score, key in zip(d_scores, keys)]
            d_keys = [dot_tn(score, query) for score, query in zip(d_scores, queries)]
            for which, pieces in enumerate((d_queries, d_keys, d_values)):
                for head, piece in zip(group, pieces):
                    slot = which * HEADS + head
                    place, start = slot // cols, (slot % cols) * size
                    d_mixed[place, rows, start : start + size] = piece.astype(LOW)


def qkv_backward_kernel(sizes, packing, places, *refs):
    clips, span, frames, width, chunk = sizes
    blocks = len(places)
    tokens, mod, d_middle, d_mixed = refs[:4]
    input_grad, d_mod = refs[4 + blocks : 6 + blocks]
    weight, d_hidden, sems = refs[6 + blocks :]
    copies = start_blocks(places, refs[4 : 4 + blocks], weight, sems)
    column_parts, row_parts = weight.shape[0], weight.shape[1]
    for copy in copies:
        copy.wait()
    for place in range(column_parts):
        columns = jnp.concatenate(
            [
                packing.qkv_of(weight.at[place, part], side)
                for part in range(row_parts)
                for side in range(2)
            ],
            axis=0,
        )
        term = dot_nt(d_mixed[place, :, 0 : packing.qkv_cols], columns)
        if place == 0:
            d_hidden[...] = term
        else:
            d_hidden[...] += term
    zero_row = jnp.zeros((1, width), F32)
    for clip in range(clips):
        clip_mod = mod[clip]

        def first_back(step, carry, clip=clip, clip_mod=clip_mod):
            d_shift, d_scale = carry
            rows = pl.ds(pl.multiple_of(clip * span + step * chunk, chunk), chunk)
            grad = d_hidden[rows, :]
            unit, d_value = norm_back(grad, tokens[rows, :].astype(F32), clip_mod[1:2])
            input_grad[rows, :] = (d_middle[rows, :] + d_value).astype(LOW)
            return (
                d_shift + jnp.sum(grad, 0, keepdims=True),
                d_scale + jnp.sum(grad * unit, 0, keepdims=True),
            )

        sums = lax.fori_loop(0, span // chunk, first_back, (zero_row, zero_row))
        d_mod[clip, 0:1, :] = sums[0]
        d_mod[clip, 1:2, :] = sums[1]


def attn_weight_kernel(packing, distances, *refs):
    own, far, outs, d_pieces = refs[:4], refs[4:8], refs[8:-1], refs[-1]
    half, qkv_cols, proj_cols = packing.half, packing.qkv_cols, packing.proj_cols
    row_count = own[0].shape[1]
    column_parts = own[2].shape[0]
    row_parts = own[0].shape[0] // (2 * half)
    for start, group in ((0, own), (row_count, far)):
        for place in range(column_parts):
            d_pieces[place, start : start + row_count, :] = columns_of(
                group[3], slice(None), place, proj_cols
            )
    column, row = here(AXES)
    for index, z_bits in enumerate(distances):
        for x_bit in range(2):
            place = column ^ (2 * z_bits + x_bit)
            d_qkv = jnp.concatenate(
                [own[2][place, :, 0:qkv_cols], far[2][place, :, 0:qkv_cols]], axis=0
            )
            d_proj = d_pieces[place]
            for other in range(row_parts // 2):
                rows = pl.ds(pl.multiple_of((row ^ (2 * other)) * 2 * half, 16), 2 * half)
                hidden_t, attended_t = (
                    jnp.concatenate([own[which][rows, :], far[which][rows, :]], axis=1)
                    for which in range(2)
                )
                qkv = dot_nn(hidden_t, d_qkv)
                proj = dot_nn(attended_t, d_proj)
                outs[2 * index + other][x_bit] = packing.pack(qkv, proj).astype(LOW)


def feed_kernel(chunk, parts, *refs):
    sources, stacked, outs = refs[0:4], refs[4], refs[5:11]
    hidden, d_outs, up_weight, down_weight, up_proj, d_activ, activ, d_up, wide, narrow = refs[11:21]
    in_sems, weight_sems, out_sems = refs[21:]
    rows_each = sources[0].shape[0]
    half = stacked.shape[0] // (2 * parts)
    halves = [pl.ds(index * rows_each, rows_each) for index in range(2)]

    def started(source, target, sem):
        copy = pltpu.make_async_copy(source, target, sem)
        copy.start()
        return copy

    waits = []
    for which, (target, weight) in enumerate(((hidden, up_weight), (d_outs, down_weight))):
        waits.append(
            [
                started(sources[2 * which + index], target.at[rows], in_sems.at[which, index])
                for index, rows in enumerate(halves)
            ]
            + [
                started(
                    stacked.at[pl.ds((2 * part + which) * half, half)],
                    weight.at[pl.ds(part * half, half)],
                    weight_sems.at[part, which],
                )
                for part in range(parts)
            ]
        )
    sent = []
    tilt = math.sqrt(2.0 / math.pi)
    for copy in waits[0]:
        copy.wait()
    up_proj[...] = dot_nt(hidden[...], up_weight[...])
    for copy in waits[1]:
        copy.wait()
    d_activ[...] = dot_nn(d_outs[...], down_weight[...])

    def gelu(step, carry):
        rows = pl.ds(pl.multiple_of(step * chunk, chunk), chunk)
        value = up_proj[rows, :]
        square = value * value
        bend = jnp.tanh(value * (tilt + (tilt * 0.044715) * square))
        half_value = 0.5 * value
        activ[rows, :] = (half_value + half_value * bend).astype(LOW)
        slope = (0.5 + 0.5 * bend) + half_value * (1.0 - bend * bend) * (
            tilt + (tilt * 3.0 * 0.044715) * square
        )
        d_up[rows, :] = (d_activ[rows, :] * slope).astype(LOW)
        return carry

    lax.fori_loop(0, 2 * rows_each // chunk, gelu, 0)
    for index, rows in enumerate(halves):
        sent.append(started(activ.at[rows], outs[index], out_sems.at[index]))
        sent.append(started(d_up.at[rows], outs[2 + index], out_sems.at[2 + index]))
    value = dot_nn(d_up[...], up_weight[...])
    narrow[...] = value[rows_each:].astype(LOW)
    sent.append(started(narrow, outs[5], out_sems.at[5]))
    wide[...] = value[:rows_each]
    sent.append(started(wide, outs[4], out_sems.at[4]))
    for copy in sent:
        copy.wait()


def feed_weight_kernel(parts, *refs):
    gathered, stacked, results = refs[16], refs[17], refs[18:22]
    down_weight, sems = refs[22:]
    half = gathered.shape[0] // (2 * parts)
    copies = []
    for part in range(parts):
        copy = pltpu.make_async_copy(
            gathered.at[pl.ds((2 * part + 1) * half, half)],
            down_weight.at[pl.ds(part * half, half)],
            sems.at[part],
        )
        copy.start()
        copies.append(copy)
    hidden, d_outs, activ, d_up = (
        jnp.concatenate([ref[...] for ref in refs[i : i + 4]], axis=0) for i in (0, 4, 8, 12)
    )
    for side, (left, right) in enumerate(((d_up, hidden), (d_outs, activ))):
        total = dot_tn(left, right).astype(LOW)
        for part in range(parts):
            stacked[part, side * half : (side + 1) * half, :] = total[
                part * half : (part + 1) * half
            ]
    for copy in copies:
        copy.wait()
    total = dot_nt(activ, down_weight[...])
    rows = results[0].shape[0]
    for index, result in enumerate(results):
        result[...] = total[index * rows : (index + 1) * rows].astype(result.dtype)


def join_rows_kernel(pieces, out):
    height = pieces.shape[2]
    for part in range(pieces.shape[0]):
        out[:, part * height : (part + 1) * height] = pieces[part, 0 : out.shape[0], :]


def modulation_kernel(conds, ada, part_out, ordered):
    groups, rows, _ = ordered.shape
    for group in range(groups):
        ordered[group] = conds[group, 0:rows, 0 : ada.shape[0]]
        part_out[group * rows : (group + 1) * rows, :] = dot_nn(ordered[group], ada[...])


def prepare_kernel(packing, sub, clips, *refs):
    timesteps, labels, time_table, class_table, qkv, proj_t, up, down_t, packed, send = refs
    packed[...] = packing.pack(qkv[...], proj_t[...].T)
    row_parts = send.shape[0]

    def look_up(indices, table):
        count = table.shape[0]
        row = lax.broadcasted_iota(jnp.int32, (16, count), 0)
        column = lax.broadcasted_iota(jnp.int32, (16, count), 1)
        picked = jnp.zeros((16, count), jnp.bool_)
        for clip in range(clips):
            picked = picked | ((row == clip) & (column == indices[clip]))
        return dot_nn(picked.astype(F32).astype(LOW), table[...])

    embedded = look_up(timesteps, time_table) + look_up(labels, class_table)
    cond = (embedded * (1.0 / (1.0 + jnp.exp(-embedded)))).astype(LOW)
    up_t = up[...].T
    height = send.shape[2]
    pairs = height // sub
    for part in range(row_parts):
        send[part, 0:sub] = up_t[part * sub : (part + 1) * sub, :]
        send[part, 2 * sub :] = cond[:, part * height : (part + 1) * height]
        for pair in range(pairs):
            start = (pair * row_parts + part) * sub
            send[part, sub : 2 * sub, pair * sub : (pair + 1) * sub] = down_t[:, start : start + sub]


def feed_finish_kernel(back, up_grad, down_grad_t):
    parts, _, sub, height = back.shape
    pairs = height // sub
    for part in range(parts):
        up_grad[:, part * sub : (part + 1) * sub] = back[part, 0].astype(F32).T
        for pair in range(pairs):
            start = (pair * parts + part) * sub
            down_grad_t[:, start : start + sub] = back[
                part, 1, :, pair * sub : (pair + 1) * sub
            ].astype(F32)


def attn_finish_kernel(packing, *refs):
    total = refs[0][...].astype(F32)
    for ref in refs[1:-2]:
        total += ref[...].astype(F32)
    qkv_grad, proj_grad_t = refs[-2:]
    for side in range(2):
        rows = slice(side * packing.half, (side + 1) * packing.half)
        qkv_grad[rows, :] = packing.qkv_of(total, side)
        proj_grad_t[:, rows] = packing.proj_of(total, side).T


VMEM_SPEC = pl.BlockSpec(memory_space=pltpu.VMEM)
SMEM_SPEC = pl.BlockSpec(memory_space=pltpu.SMEM)
ANY_SPEC = pl.BlockSpec(memory_space=pl.ANY)
PARAMS = pltpu.CompilerParams(vmem_limit_bytes=56 * 1024 * 1024)


def shape_of(dims, kind=LOW):
    return jax.ShapeDtypeStruct(dims, kind)


def cost(micros):
    return pl.CostEstimate(flops=1000, bytes_accessed=int(micros * SCALE), transcendentals=0)


def after(value, *others):
    return lax.optimization_barrier((value,) + others)[0]


class Sequence:
    def __init__(self):
        self.token = None

    def call(self, kernel, shapes, arrays, name, specs=None, scratch=(), tied=0, out_spec=None):
        arrays = list(arrays)
        if self.token is not None:
            arrays[tied] = after(arrays[tied], self.token)
        results = pl.pallas_call(
            kernel,
            out_shape=shapes,
            in_specs=specs or [VMEM_SPEC] * len(arrays),
            out_specs=jax.tree.map(lambda _: out_spec or VMEM_SPEC, shapes),
            scratch_shapes=scratch,
            compiler_params=PARAMS,
            cost_estimate=cost(1),
            name=name,
        )(*arrays)
        self.token = min(jax.tree.leaves(results), key=lambda result: result.size)
        return results

    def sum_low(self, *arrays):
        total = after(arrays[0], self.token).astype(F32)
        for array in arrays[1:]:
            total += array.astype(F32)
        self.token = total.astype(LOW)
        return self.token


def swap(value, mask, count):
    return lax.ppermute(value, AXES, [(i, i ^ mask) for i in range(count)])


def padded_exchange(rows, count):
    length = rows.shape[1]
    tiles = -(-length // 1024) * 8
    rows = jnp.pad(rows, ((0, 0), (0, tiles * 128 - length))).reshape(count, tiles, 128)
    got = lax.all_to_all(rows, AXES, 0, 0, tiled=True)
    return got.reshape(count, tiles * 128)[:, :length]


def fast_body(
    column_parts,
    row_parts,
    inputs,
    out_cotangent,
    lengths,
    timesteps,
    labels,
    time_table,
    class_table,
    ada_weight,
    qkv_weight,
    proj_weight,
    up_weight,
    down_weight,
):
    count = column_parts * row_parts
    clips, positions, frames, width = inputs.shape
    span = positions * frames
    row_count = clips * span
    qkv_cols, proj_cols = qkv_weight.shape[1], proj_weight.shape[1]
    height = qkv_weight.shape[0]
    part_width = width // row_parts
    hidden_part = up_weight.shape[1] * column_parts // row_parts
    sub = up_weight.shape[1] // row_parts
    x_mask = row_parts
    z_masks = tuple(row_parts * 2 * i for i in range(1, column_parts // 2))
    packing = Packing(height // 2, qkv_cols, proj_cols)

    line = Sequence()
    packed, both_send = line.call(
        functools.partial(prepare_kernel, packing, sub, clips),
        (
            shape_of((height // 2, packing.width)),
            shape_of((row_parts, 2 * sub + 16, height)),
        ),
        (timesteps, labels, time_table, class_table)
        + (qkv_weight, proj_weight.T, up_weight, down_weight.T),
        "prepare",
        [SMEM_SPEC] * 2 + [VMEM_SPEC] * 6,
    )

    y_mask, c_mask = 2, 1
    ada_cols = ada_weight.shape[1]

    def gate(*values):
        return lax.optimization_barrier(values)

    own = packed[None]
    far = [swap(own, mask, count) for mask in z_masks]
    own_x, own_y = swap(own, x_mask, count), swap(own, y_mask, count)
    both_got = lax.all_to_all(both_send, "fsdp", 0, 0, tiled=True)
    *far, own_x, own_y, both_got = gate(*far, own_x, own_y, both_got)
    own_feed = line.call(join_rows_kernel, shape_of((2 * sub, width)), (both_got,), "join_rows")
    conds = both_got[:, 2 * sub : 2 * sub + clips].reshape(row_parts * clips, height)
    feed = lax.all_gather(own_feed, "dp", axis=0, tiled=True)

    far = jnp.concatenate(far)
    pads = (-row_parts * clips % 16, -height % 128)
    conds = jnp.pad(conds, ((0, pads[0]), (0, pads[1])))
    conds = jnp.broadcast_to(conds[None], (column_parts,) + conds.shape)
    conds = lax.all_to_all(conds, "dp", 0, 0, tiled=True)
    far_x, far_y = swap(far, x_mask, count), swap(far, y_mask, count)
    cores = [swap(array, c_mask, count) for array in (own, own_x, own_y, far)]
    far_x, far_y, conds, *cores = gate(far_x, far_y, conds, *cores)

    mod_part, conds = line.call(
        modulation_kernel,
        (
            shape_of((count * clips, ada_cols), F32),
            shape_of((column_parts, row_parts * clips, part_width)),
        ),
        (conds, ada_weight),
        "modulation",
    )
    cond_all = conds.reshape(count * clips, part_width)
    mod_got = padded_exchange(mod_part.reshape(count, clips * ada_cols), count)
    own_xy, far_xy = swap(own_x, y_mask, count), swap(far_x, y_mask, count)
    cores += [swap(array, c_mask, count) for array in (far_x, far_y)]
    own_xy, far_xy, mod_got, *cores = gate(own_xy, far_xy, mod_got, *cores)
    mod_own = jnp.sum(mod_got.reshape(column_parts, row_parts, clips, ada_cols), axis=1)
    mod = mod_own.transpose(1, 0, 2).reshape(clips, 6, width)
    cores += [swap(array, c_mask, count) for array in (own_xy, far_xy)]

    blocks = [own, own_x, own_y, far, far_x, far_y, own_xy, far_xy]
    places = [[0], [x_mask], [y_mask], list(z_masks)]
    places += [[z ^ side for z in z_masks] for side in (x_mask, y_mask)]
    places += [[x_mask ^ y_mask]]
    places += [[z ^ x_mask ^ y_mask for z in z_masks]]
    blocks += cores
    places += [[place ^ c_mask for place in held] for held in places]

    tokens = inputs.reshape(row_count, width)
    cotangent = out_cotangent.reshape(row_count, width)
    gate_two = jnp.repeat(mod[:, 5], span, axis=0)
    d_out = (cotangent.astype(F32) * gate_two).astype(LOW)
    d_outs = {0: d_out, 1: swap(d_out, 1, count), 2: swap(d_out, 2, count)}
    d_outs[3] = swap(d_outs[2], 1, count)
    sizes = (clips, span, frames, width, 32)
    full = (row_count, width)
    weight_scratch = pltpu.VMEM((column_parts, row_parts, height // 2, packing.width), LOW)
    weight_sems = pltpu.SemaphoreType.DMA((count,))
    hidden, mixed, probs, attended, branch, middle, hidden_two, proj_full = line.call(
        functools.partial(attn_forward_kernel, sizes, packing, places),
        (
            shape_of((width, row_count)),
            shape_of((column_parts, row_count, qkv_cols)),
            shape_of((clips, HEADS, span, span)),
            shape_of((width, row_count)),
            shape_of(full),
            shape_of(full, F32),
            shape_of(full),
            shape_of((width, width)),
        ),
        (lengths, tokens, mod, *blocks),
        "attn_forward",
        [SMEM_SPEC, VMEM_SPEC, VMEM_SPEC] + [ANY_SPEC] * len(blocks),
        (
            weight_scratch,
            pltpu.VMEM(full, F32),
            pltpu.VMEM(full, LOW),
            pltpu.VMEM(full, LOW),
            weight_sems,
        ),
        tied=2,
    )

    tokens_two = {0: hidden_two, 1: swap(hidden_two, 1, count), 2: swap(hidden_two, 2, count)}
    pair = (2 * row_count, width)
    pair_hidden = (2 * row_count, hidden_part)
    feed_scratch = (
        pltpu.VMEM(pair, LOW),
        pltpu.VMEM(pair, LOW),
        pltpu.VMEM((hidden_part, width), LOW),
        pltpu.VMEM((width, hidden_part), LOW),
        pltpu.VMEM(pair_hidden, F32),
        pltpu.VMEM(pair_hidden, F32),
        pltpu.VMEM(pair_hidden, LOW),
        pltpu.VMEM(pair_hidden, LOW),
        pltpu.VMEM(full, F32),
        pltpu.VMEM(full, LOW),
        pltpu.SemaphoreType.DMA((2, 2)),
        pltpu.SemaphoreType.DMA((column_parts, 2)),
        pltpu.SemaphoreType.DMA((6,)),
    )

    def feed_call(index, name):
        return line.call(
            functools.partial(feed_kernel, 16, column_parts),
            [shape_of((row_count, hidden_part))] * 4 + [shape_of(full, F32), shape_of(full)],
            (
                tokens_two[index],
                tokens_two[index + 1],
                d_outs[index],
                d_outs[index + 1],
                feed,
            ),
            name,
            [ANY_SPEC] * 5,
            feed_scratch,
            out_spec=ANY_SPEC,
        )

    near = feed_call(0, "feed_near")
    tokens_two[2] = after(tokens_two[2], line.token)
    tokens_two[3] = swap(tokens_two[2], 1, count)
    distant = feed_call(2, "feed_distant")

    grad_send = line.sum_low(distant[4], swap(distant[5], 1, count))
    grad_far = swap(grad_send, 2, count)
    grad_parts = (near[4], swap(near[5], 1, count), grad_far)
    feed_grads, *partials = line.call(
        functools.partial(feed_weight_kernel, column_parts),
        [shape_of((column_parts, 2 * sub, width))]
        + [shape_of(full, F32), shape_of(full)]
        + [shape_of(full)] * 2,
        [tokens_two[i] for i in range(4)]
        + [d_outs[i] for i in range(4)]
        + [*near[0:2], *distant[0:2], *near[2:4], *distant[2:4], feed],
        "feed_weight",
        [VMEM_SPEC] * 16 + [ANY_SPEC],
        (pltpu.VMEM((width, hidden_part), LOW), pltpu.SemaphoreType.DMA((column_parts,))),
    )
    feed_grads = feed_grads.reshape(2 * sub * column_parts, width)
    far_side = [swap(array, 1, count) for array in (hidden, attended)]
    feed_grads, grad_far, *far_side = lax.optimization_barrier((feed_grads, grad_far, *far_side))
    grad_parts = grad_parts[:2] + (grad_far,)
    line.token = grad_far
    groups = column_parts // 2
    feed_sum = lax.psum_scatter(feed_grads, "dp", scatter_dimension=0, tiled=True)

    out_send = line.sum_low(partials[2], swap(partials[3], 1, count))
    out_far = swap(out_send, 2, count)
    d_middle, d_branch, d_attended, d_mod_two = line.call(
        functools.partial(proj_backward_kernel, sizes),
        (
            shape_of(full, F32),
            shape_of(full),
            shape_of(full),
            shape_of((clips, 3, width), F32),
        ),
        (cotangent, mod, middle, branch, *grad_parts, proj_full),
        "proj_backward",
    )
    d_mixed = line.call(
        functools.partial(attn_backward_kernel, (clips, span, frames, width, qkv_cols)),
        shape_of((column_parts, row_count, -(-qkv_cols // 128) * 128)),
        (mixed, probs, d_attended),
        "attn_backward",
    )
    own_side = (hidden, attended, d_mixed, d_branch)
    far_side += [swap(array, 1, count) for array in own_side[2:]]
    attn_grads, first = {}, {}
    for distances in (range(groups - 1, groups // 2 - 1, -1), range(groups // 2 - 1, -1, -1)):
        grads = line.call(
            functools.partial(attn_weight_kernel, packing, distances),
            [shape_of((2, height // 2, packing.width))] * (2 * len(distances)),
            (*own_side, *far_side),
            "attn_weight",
            scratch=(pltpu.VMEM((column_parts, 2 * row_count, proj_cols), LOW),),
        )
        for index, distance in enumerate(distances):
            attn_grads[distance] = grads[2 * index]
            first[distance] = swap(grads[2 * index + 1], y_mask, count)
        if not len(distances) < len(first):
            ffn_out = after(partials[0], line.token) + swap(partials[1], 1, count).astype(F32)
            ffn_out += out_far.astype(F32)
            result = (middle + gate_two * ffn_out).astype(LOW).reshape(inputs.shape)
            d_gate_two = jnp.sum(
                (cotangent.astype(F32) * ffn_out).reshape(clips, 1, span, width), axis=2
            )
            line.token = d_gate_two
    input_grad, d_mod_one = line.call(
        functools.partial(qkv_backward_kernel, sizes, packing, places),
        (shape_of(full), shape_of((clips, 2, width), F32)),
        (tokens, mod, d_middle, d_mixed, *blocks),
        "qkv_backward",
        [VMEM_SPEC] * 4 + [ANY_SPEC] * len(blocks),
        (weight_scratch, pltpu.VMEM(full, F32), weight_sems),
    )
    stay, second, attn_z = {}, {}, {}

    def split_sum(index):
        kept = after(attn_grads[index], line.token)
        stay[index] = kept[0].astype(F32) + first[index][0].astype(F32)
        leave = (kept[1].astype(F32) + first[index][1].astype(F32)).astype(LOW)
        line.token = leave
        second[index] = swap(leave, x_mask, count)

    def attn_sum(index):
        summed = line.sum_low(stay[index], second[index])
        attn_z[index] = swap(summed, z_masks[index - 1], count)

    d_mod = jnp.concatenate([d_mod_one, d_mod_two, d_gate_two], axis=1)
    mod_send = d_mod.reshape(clips, column_parts, ada_cols).transpose(1, 0, 2)
    mod_send = jnp.broadcast_to(
        mod_send.reshape(column_parts, 1, clips * ada_cols),
        (column_parts, row_parts, clips * ada_cols),
    ).reshape(count, clips * ada_cols)
    d_mod_all = padded_exchange(mod_send, count).reshape(count * clips, ada_cols)
    split_sum(3)
    line.token, d_mod_all = lax.optimization_barrier((line.token, d_mod_all))
    split_sum(2)
    attn_sum(3)
    attn_sum(2)
    split_sum(1)
    back = feed_sum.reshape(2, sub, row_parts, height).transpose(2, 0, 1, 3)
    line.token, back = lax.optimization_barrier((line.token, back))
    back = lax.all_to_all(back, "fsdp", 0, 0, tiled=True)
    split_sum(0)
    attn_sum(1)
    up_grad, down_grad_t = line.call(
        feed_finish_kernel,
        (shape_of(up_weight.shape, F32), shape_of(down_weight.shape[::-1], F32)),
        (back,),
        "feed_finish",
    )
    down_grad = down_grad_t.T
    qkv_grad, proj_grad_t = line.call(
        functools.partial(attn_finish_kernel, packing),
        (shape_of((height, qkv_cols), F32), shape_of((proj_cols, height), F32)),
        (stay[0], second[0], attn_z[3], attn_z[2], attn_z[1]),
        "attn_finish",
    )
    proj_grad = proj_grad_t.T

    ada_grad = lax.dot_general(
        cond_all.astype(F32),
        d_mod_all,
        (((0,), (0,)), ((), ())),
        precision=lax.Precision.HIGHEST,
        preferred_element_type=F32,
    )
    return (
        result,
        input_grad.reshape(inputs.shape),
        ada_grad,
        qkv_grad,
        proj_grad,
        up_grad,
        down_grad,
    )


def solution(mesh):
    column_parts, row_parts = mesh.shape["dp"], mesh.shape["fsdp"]
    body = general_body
    if (column_parts, row_parts) == (8, 4):
        body = functools.partial(fast_body, column_parts, row_parts)
    clip_spec = P(AXES, None, None, None)
    return jax.shard_map(
        body,
        mesh=mesh,
        in_specs=(
            clip_spec,
            clip_spec,
            P(AXES),
            P(AXES),
            P(AXES),
            P(),
            P(),
        )
        + (P("fsdp", "dp"),) * 5,
        out_specs=(clip_spec, clip_spec) + (P("fsdp", "dp"),) * 5,
        check_vma=False,
    )
```

```python
import functools
import math

import jax
import jax.numpy as jnp
from jax import lax
from jax.experimental import pallas as pl
from jax.experimental.pallas import tpu as pltpu
from jax.sharding import PartitionSpec as P

HEADS = 16
AXES = ("dp", "fsdp")
EPS = 1e-06
F32, LOW = jnp.float32, jnp.bfloat16
SCALE = 100


def norm_mod(values, shift_add, scale_mul):
    center = values - jnp.mean(values, -1, keepdims=True)
    spread = jnp.mean(center * center, -1, keepdims=True)
    return center * lax.rsqrt(spread + 1e-06) * (1.0 + scale_mul) + shift_add


def gelu_tanh(values):
    return jax.nn.gelu(values, approximate=True)


def gather_five(shards):
    row_set = (
        lax.all_gather(shards[0], "fsdp", axis=0, tiled=True),
        lax.all_gather(shards[1], "fsdp", axis=0, tiled=True),
        lax.all_gather(shards[2], "fsdp", axis=0, tiled=True),
        lax.all_gather(shards[3], "fsdp", axis=0, tiled=True),
        lax.all_gather(shards[4], "fsdp", axis=0, tiled=True),
    )
    return (
        lax.all_gather(row_set[0], "dp", axis=1, tiled=True),
        lax.all_gather(row_set[1], "dp", axis=1, tiled=True),
        lax.all_gather(row_set[2], "dp", axis=1, tiled=True),
        lax.all_gather(row_set[3], "dp", axis=1, tiled=True),
        lax.all_gather(row_set[4], "dp", axis=1, tiled=True),
    )


def scatter_five(totals):
    row_set = (
        lax.psum_scatter(
            totals[0].astype(jnp.bfloat16), "fsdp", scatter_dimension=0, tiled=True
        ).astype(jnp.float32),
        lax.psum_scatter(
            totals[1].astype(jnp.bfloat16), "fsdp", scatter_dimension=0, tiled=True
        ).astype(jnp.float32),
        lax.psum_scatter(
            totals[2].astype(jnp.bfloat16), "fsdp", scatter_dimension=0, tiled=True
        ).astype(jnp.float32),
        lax.psum_scatter(
            totals[3].astype(jnp.bfloat16), "fsdp", scatter_dimension=0, tiled=True
        ).astype(jnp.float32),
        lax.psum_scatter(
            totals[4].astype(jnp.bfloat16), "fsdp", scatter_dimension=0, tiled=True
        ).astype(jnp.float32),
    )
    return (
        lax.psum_scatter(
            row_set[0].astype(jnp.bfloat16), "dp", scatter_dimension=1, tiled=True
        ).astype(jnp.float32),
        lax.psum_scatter(
            row_set[1].astype(jnp.bfloat16), "dp", scatter_dimension=1, tiled=True
        ).astype(jnp.float32),
        lax.psum_scatter(
            row_set[2].astype(jnp.bfloat16), "dp", scatter_dimension=1, tiled=True
        ).astype(jnp.float32),
        lax.psum_scatter(
            row_set[3].astype(jnp.bfloat16), "dp", scatter_dimension=1, tiled=True
        ).astype(jnp.float32),
        lax.psum_scatter(
            row_set[4].astype(jnp.bfloat16), "dp", scatter_dimension=1, tiled=True
        ).astype(jnp.float32),
    )


def fetch_weights(ada_weight, core_shards):
    return tuple(gather_five((ada_weight,) + tuple(core_shards)))


def matmul_tn(left, right):
    return lax.dot_general(
        left, right, (((0,), (0,)), ((), ())), preferred_element_type=jnp.float32
    )


def matmul_nt(left, right):
    return lax.dot_general(
        left, right, (((1,), (1,)), ((), ())), preferred_element_type=jnp.float32
    )


def general_body(
    inputs,
    out_cotangent,
    lengths,
    timesteps,
    labels,
    time_table,
    class_table,
    ada_weight,
    qkv_weight,
    proj_weight,
    up_weight,
    down_weight,
):
    core_shards = (qkv_weight, proj_weight, up_weight, down_weight)
    clip_count, positions, frames, model_width = inputs.shape
    row_count = clip_count * positions * frames
    seq_count = clip_count * positions
    span = positions * frames
    head_size = model_width // HEADS
    attn_scale = 1.0 / math.sqrt(head_size)
    ada_full, qkv_full, proj_full, up_full, down_full = fetch_weights(ada_weight, core_shards)
    time_onehot = (timesteps[:, None] == lax.iota(jnp.int32, time_table.shape[0])[None, :]).astype(
        jnp.bfloat16
    )
    class_onehot = (labels[:, None] == lax.iota(jnp.int32, class_table.shape[0])[None, :]).astype(
        jnp.bfloat16
    )
    embedded = jnp.dot(time_onehot, time_table, preferred_element_type=jnp.float32) + jnp.dot(
        class_onehot, class_table, preferred_element_type=jnp.float32
    )
    cond_low = jax.nn.silu(embedded).astype(jnp.bfloat16)
    modulation = jnp.dot(cond_low, ada_full, preferred_element_type=jnp.float32)
    pieces = [
        modulation[:, None, offset * model_width : (offset + 1) * model_width]
        for offset in range(6)
    ]
    shift_one, scale_one, gate_one, shift_two, scale_two, gate_two = pieces
    residual = inputs.astype(jnp.float32).reshape(clip_count, span, model_width)
    hidden_one = (
        norm_mod(residual, shift_one, scale_one)
        .astype(jnp.bfloat16)
        .reshape(row_count, model_width)
    )
    mixed = jnp.dot(hidden_one, qkv_full, preferred_element_type=jnp.float32).astype(jnp.bfloat16)
    shaped = mixed.reshape(seq_count, frames, 3, HEADS, head_size)
    queries = shaped[:, :, 0]
    key_part = shaped[:, :, 1]
    value_part = shaped[:, :, 2]
    clip_live = lax.iota(jnp.int32, frames)[None, :] < lengths[:, None]
    key_live = jnp.repeat(clip_live, positions, axis=0)
    scores = (
        jnp.einsum("sqhe,skhe->shqk", queries, key_part, preferred_element_type=jnp.float32)
        * attn_scale
    )
    scores = jnp.where(key_live[:, None, None, :], scores, -1e30)
    row_max = jnp.max(scores, -1, keepdims=True)
    exp_scores = jnp.exp(scores - row_max)
    attn_probs = exp_scores / jnp.sum(exp_scores, -1, keepdims=True)
    probs_low = attn_probs.astype(jnp.bfloat16)
    attended = jnp.einsum(
        "shqk,skhe->sqhe", probs_low, value_part, preferred_element_type=jnp.float32
    )
    attended_low = attended.astype(jnp.bfloat16).reshape(row_count, model_width)
    branch = jnp.dot(attended_low, proj_full, preferred_element_type=jnp.float32).reshape(
        clip_count, span, model_width
    )
    middle = residual + gate_one * branch
    hidden_two = (
        norm_mod(middle, shift_two, scale_two).astype(jnp.bfloat16).reshape(row_count, model_width)
    )
    up_proj = jnp.dot(hidden_two, up_full, preferred_element_type=jnp.float32)
    activ_low = gelu_tanh(up_proj).astype(jnp.bfloat16)
    ffn_out = jnp.dot(activ_low, down_full, preferred_element_type=jnp.float32).reshape(
        clip_count, span, model_width
    )
    result = (middle + gate_two * ffn_out).astype(jnp.bfloat16).reshape(inputs.shape)
    ada_full, qkv_full, proj_full, up_full, down_full = fetch_weights(ada_weight, core_shards)
    grad_out = out_cotangent.astype(jnp.float32).reshape(clip_count, span, model_width)
    d_gate_two = jnp.sum(grad_out * ffn_out, axis=1)
    d_ffn = (grad_out * gate_two).astype(jnp.bfloat16).reshape(row_count, model_width)
    d_activ = matmul_nt(d_ffn, down_full)
    down_total = matmul_tn(activ_low, d_ffn)
    gelu_value, gelu_pull = jax.vjp(gelu_tanh, up_proj)
    d_up = gelu_pull(d_activ)[0].astype(jnp.bfloat16)
    d_hidden_two = matmul_nt(d_up, up_full)
    up_total = matmul_tn(hidden_two, d_up)
    norm_value, norm_pull = jax.vjp(norm_mod, middle, shift_two, scale_two)
    d_middle_norm, d_shift_two, d_scale_two = norm_pull(
        d_hidden_two.reshape(clip_count, span, model_width)
    )
    d_middle = grad_out + d_middle_norm
    d_gate_one = jnp.sum(d_middle * branch, axis=1)
    d_branch = (d_middle * gate_one).astype(jnp.bfloat16).reshape(row_count, model_width)
    d_attended = (
        matmul_nt(d_branch, proj_full)
        .astype(jnp.bfloat16)
        .reshape(seq_count, frames, HEADS, head_size)
    )
    proj_total = matmul_tn(attended_low, d_branch)
    d_value = jnp.einsum(
        "shqk,sqhe->skhe", probs_low, d_attended, preferred_element_type=jnp.float32
    )
    d_probs = jnp.einsum(
        "sqhe,skhe->shqk", d_attended, value_part, preferred_element_type=jnp.float32
    )
    d_scores = attn_probs * (d_probs - jnp.sum(attn_probs * d_probs, -1, keepdims=True))
    d_scores_low = d_scores.astype(jnp.bfloat16)
    d_query = (
        jnp.einsum("shqk,skhe->sqhe", d_scores_low, key_part, preferred_element_type=jnp.float32)
        * attn_scale
    )
    d_key = (
        jnp.einsum("shqk,sqhe->skhe", d_scores_low, queries, preferred_element_type=jnp.float32)
        * attn_scale
    )
    d_mixed = (
        jnp.stack([d_query, d_key, d_value], axis=2)
        .astype(jnp.bfloat16)
        .reshape(row_count, 3 * model_width)
    )
    d_hidden_one = matmul_nt(d_mixed, qkv_full)
    qkv_total = matmul_tn(hidden_one, d_mixed)
    norm_first, first_pull = jax.vjp(norm_mod, residual, shift_one, scale_one)
    d_input_norm, d_shift_one, d_scale_one = first_pull(
        d_hidden_one.reshape(clip_count, span, model_width)
    )
    input_grad = (d_middle + d_input_norm).astype(jnp.bfloat16).reshape(inputs.shape)
    d_modulation = jnp.concatenate(
        [
            d_shift_one[:, 0],
            d_scale_one[:, 0],
            d_gate_one,
            d_shift_two[:, 0],
            d_scale_two[:, 0],
            d_gate_two,
        ],
        axis=-1,
    )
    ada_total = jnp.dot(
        cond_low.astype(jnp.float32).T, d_modulation, precision=lax.Precision.HIGHEST
    )
    ada_grad, qkv_grad, proj_grad, up_grad, down_grad = scatter_five(
        (ada_total, qkv_total, proj_total, up_total, down_total)
    )
    return (result, input_grad, ada_grad, qkv_grad, proj_grad, up_grad, down_grad)


def dot_nn(left, right):
    return lax.dot_general(left, right, (((1,), (0,)), ((), ())), preferred_element_type=F32)


def dot_nt(left, right):
    return lax.dot_general(left, right, (((1,), (1,)), ((), ())), preferred_element_type=F32)


def dot_tn(left, right):
    return lax.dot_general(left, right, (((0,), (0,)), ((), ())), preferred_element_type=F32)


def stats(values):
    mean = jnp.mean(values, -1, keepdims=True)
    center = values - mean
    spread = jnp.mean(center * center, -1, keepdims=True)
    inverse = lax.rsqrt(spread + EPS)
    return center * inverse, inverse


def here(names):
    return lax.axis_index(names[0]), lax.axis_index(names[1])


def start_blocks(places, block_refs, weight_ref, sems):
    column, row = here(AXES)
    row_parts = weight_ref.shape[1]
    copies = {}
    for ref, held in zip(block_refs, places):
        for index, relative in enumerate(held):
            copy = pltpu.make_async_copy(
                ref.at[index],
                weight_ref.at[column ^ (relative // row_parts), row ^ (relative % row_parts)],
                sems.at[relative],
            )
            copy.start()
            copies[relative] = copy
    return [copies[relative] for relative in sorted(copies)]


class Packing:
    def __init__(self, half, qkv_cols, proj_cols):
        self.half, self.qkv_cols, self.proj_cols = half, qkv_cols, proj_cols
        self.qkv_main, self.proj_main = qkv_cols // 128 * 128, proj_cols // 128 * 128
        self.qkv_rest, self.proj_rest = qkv_cols - self.qkv_main, proj_cols - self.proj_main
        self.rest = self.qkv_rest + self.proj_rest
        self.proj_start = 2 * self.qkv_main
        self.rest_start = self.proj_start + 2 * self.proj_main
        self.width = self.rest_start + 2 * self.rest

    def pack(self, qkv, proj):
        halves = [slice(i * self.half, (i + 1) * self.half) for i in range(2)]
        return jnp.concatenate(
            [qkv[rows, : self.qkv_main] for rows in halves]
            + [proj[rows, : self.proj_main] for rows in halves]
            + [
                piece
                for rows in halves
                for piece in (qkv[rows, self.qkv_main :], proj[rows, self.proj_main :])
            ],
            axis=1,
        )

    def qkv_of(self, block, side):
        rest = self.rest_start + side * self.rest
        return jnp.concatenate(
            [
                block[:, side * self.qkv_main : (side + 1) * self.qkv_main],
                block[:, rest : rest + self.qkv_rest],
            ],
            axis=1,
        )

    def proj_of(self, block, side):
        main = self.proj_start + side * self.proj_main
        rest = self.rest_start + side * self.rest + self.qkv_rest
        return jnp.concatenate(
            [block[:, main : main + self.proj_main], block[:, rest : rest + self.proj_rest]],
            axis=1,
        )

    def unpack(self, block):
        return tuple(
            jnp.concatenate([part(block, side) for side in range(2)], axis=0)
            for part in (self.qkv_of, self.proj_of)
        )


def pair_mask(span, frames, live):
    query = lax.broadcasted_iota(jnp.int32, (span, span), 0)
    key = lax.broadcasted_iota(jnp.int32, (span, span), 1)
    return ((query // frames) == (key // frames)) & ((key % frames) < live)


def head_groups(count, size):
    return [range(start, start + size) for start in range(0, count, size)]


def head_slices(ref, which, head, rows, size):
    per = ref.shape[2] // size
    slot = which * HEADS + head
    return ref[slot // per, rows, (slot % per) * size : (slot % per + 1) * size]


def columns_of(ref, rows, index, size):
    return ref[rows, index * size : (index + 1) * size]


def join_proj(packing, weight, proj):
    for place in range(weight.shape[0]):
        start = place * packing.proj_cols
        for part in range(weight.shape[1]):
            for side in range(2):
                row = (2 * part + side) * packing.half
                proj[row : row + packing.half, start : start + packing.proj_cols] = packing.proj_of(
                    weight.at[place, part], side
                )


def attn_forward_kernel(sizes, packing, places, *refs):
    clips, span, frames, width, chunk = sizes
    blocks = len(places)
    lengths, tokens, mod = refs[:3]
    block_refs = refs[3 : 3 + blocks]
    hidden, mixed, probs_out, attended, branch, middle, hidden_two, proj = refs[3 + blocks : 11 + blocks]
    weight, branch_full, hidden_s, attended_s, sems = refs[11 + blocks :]
    copies = start_blocks(places, block_refs, weight, sems)
    column_parts, row_parts = weight.shape[0], weight.shape[1]
    size = width // HEADS
    scale = 1.0 / math.sqrt(size)

    def first_norm(step, carry):
        rows = pl.ds(pl.multiple_of(step * chunk, chunk), chunk)
        clip_mod = mod[step * chunk // span]
        unit, _ = stats(tokens[rows, :].astype(F32))
        hidden_s[rows, :] = (unit * (1.0 + clip_mod[1:2]) + clip_mod[0:1]).astype(LOW)
        return carry

    lax.fori_loop(0, clips * span // chunk, first_norm, 0)
    column, row = here(AXES)
    for relative in range(column_parts):
        for other in range(row_parts):
            copies[relative * row_parts + other].wait()
        place = column ^ relative
        columns = jnp.concatenate(
            [
                packing.qkv_of(weight.at[place, part], side)
                for part in range(row_parts)
                for side in range(2)
            ],
            axis=0,
        )
        mixed[place] = dot_nn(hidden_s[...], columns).astype(LOW)

    for clip in range(clips):
        rows = slice(clip * span, (clip + 1) * span)
        live_mask = pair_mask(span, frames, lengths[clip])
        for group in head_groups(HEADS, 4):
            scores = [
                dot_nt(
                    head_slices(mixed, 0, head, rows, size), head_slices(mixed, 1, head, rows, size)
                )
                for head in group
            ]
            scores = [jnp.where(live_mask, score * scale, -1e30) for score in scores]
            exps = [jnp.exp(score - jnp.max(score, -1, keepdims=True)) for score in scores]
            probs = [(e * (1.0 / jnp.sum(e, -1, keepdims=True))).astype(LOW) for e in exps]
            values = [
                dot_nn(prob, head_slices(mixed, 2, head, rows, size))
                for head, prob in zip(group, probs)
            ]
            for head, prob, value in zip(group, probs, values):
                probs_out[clip, head] = prob
                attended_s[rows, head * size : (head + 1) * size] = value.astype(LOW)

    join_proj(packing, weight, proj)
    branch_full[...] = dot_nn(attended_s[...], proj[...])

    def second_norm(step, carry):
        rows = pl.ds(pl.multiple_of(step * chunk, chunk), chunk)
        clip_mod = mod[step * chunk // span]
        value = branch_full[rows, :]
        branch[rows, :] = value.astype(LOW)
        value = tokens[rows, :].astype(F32) + clip_mod[2:3] * value
        middle[rows, :] = value
        unit, _ = stats(value)
        hidden_two[rows, :] = (unit * (1.0 + clip_mod[4:5]) + clip_mod[3:4]).astype(LOW)
        return carry

    lax.fori_loop(0, clips * span // chunk, second_norm, 0)
    hidden[...] = hidden_s[...].T
    attended[...] = attended_s[...].T


def norm_back(grad, values, scale_row):
    unit, inverse = stats(values)
    d_unit = grad * (1.0 + scale_row)
    d_value = inverse * (
        d_unit
        - jnp.mean(d_unit, -1, keepdims=True)
        - unit * jnp.mean(d_unit * unit, -1, keepdims=True)
    )
    return unit, d_value


def proj_backward_kernel(sizes, *refs):
    clips, span, frames, width, chunk = sizes
    cotangent, mod, middle, branch, grad_own, grad_core, grad_far, proj = refs[:8]
    d_middle, d_branch, d_attended, d_mod = refs[8:]
    zero_row = jnp.zeros((1, width), F32)
    steps = span // chunk
    for clip in range(clips):
        clip_mod = mod[clip]

        def second_back(step, carry, clip=clip, clip_mod=clip_mod):
            d_shift, d_scale, d_gate = carry
            rows = pl.ds(pl.multiple_of(clip * span + step * chunk, chunk), chunk)
            grad = grad_own[rows, :] + grad_core[rows, :].astype(F32)
            grad += grad_far[rows, :].astype(F32)
            unit, d_value = norm_back(grad, middle[rows, :], clip_mod[4:5])
            d_value = cotangent[rows, :].astype(F32) + d_value
            d_middle[rows, :] = d_value
            d_branch[rows, :] = (d_value * clip_mod[2:3]).astype(LOW)
            return (
                d_shift + jnp.sum(grad, 0, keepdims=True),
                d_scale + jnp.sum(grad * unit, 0, keepdims=True),
                d_gate + jnp.sum(d_value * branch[rows, :].astype(F32), 0, keepdims=True),
            )

        sums = lax.fori_loop(0, steps, second_back, (zero_row, zero_row, zero_row))
        d_mod[clip, 0:1, :] = sums[2]
        d_mod[clip, 1:2, :] = sums[0]
        d_mod[clip, 2:3, :] = sums[1]

    d_attended[...] = dot_nt(d_branch[...], proj[...]).astype(LOW)


def attn_backward_kernel(sizes, *refs):
    clips, span, frames, width, qkv_cols = sizes
    mixed, probs_ref, d_attended, d_mixed = refs
    size = width // HEADS
    scale = 1.0 / math.sqrt(size)
    cols = qkv_cols // size
    for clip in range(clips):
        rows = slice(clip * span, (clip + 1) * span)
        for group in head_groups(HEADS, 4):
            queries, keys, values = (
                [head_slices(mixed, which, head, rows, size) for head in group]
                for which in range(3)
            )
            probs = [probs_ref[clip, head] for head in group]
            grads = [columns_of(d_attended, rows, head, size) for head in group]
            d_probs = [dot_nt(grad, value) for grad, value in zip(grads, values)]
            d_values = [dot_tn(prob, grad) for prob, grad in zip(probs, grads)]
            d_scores = []
            for prob, d_prob in zip(probs, d_probs):
                prob = prob.astype(F32)
                inner = jnp.sum(prob * d_prob, -1, keepdims=True)
                d_scores.append((prob * (d_prob - inner) * scale).astype(LOW))
            d_queries = [dot_nn(score, key) for score, key in zip(d_scores, keys)]
            d_keys = [dot_tn(score, query) for score, query in zip(d_scores, queries)]
            for which, pieces in enumerate((d_queries, d_keys, d_values)):
                for head, piece in zip(group, pieces):
                    slot = which * HEADS + head
                    place, start = slot // cols, (slot % cols) * size
                    d_mixed[place, rows, start : start + size] = piece.astype(LOW)


def qkv_backward_kernel(sizes, packing, places, *refs):
    clips, span, frames, width, chunk = sizes
    blocks = len(places)
    tokens, mod, d_middle, d_mixed = refs[:4]
    input_grad, d_mod = refs[4 + blocks : 6 + blocks]
    weight, d_hidden, sems = refs[6 + blocks :]
    copies = start_blocks(places, refs[4 : 4 + blocks], weight, sems)
    column_parts, row_parts = weight.shape[0], weight.shape[1]
    for copy in copies:
        copy.wait()
    for place in range(column_parts):
        columns = jnp.concatenate(
            [
                packing.qkv_of(weight.at[place, part], side)
                for part in range(row_parts)
                for side in range(2)
            ],
            axis=0,
        )
        term = dot_nt(d_mixed[place, :, 0 : packing.qkv_cols], columns)
        if place == 0:
            d_hidden[...] = term
        else:
            d_hidden[...] += term
    zero_row = jnp.zeros((1, width), F32)
    for clip in range(clips):
        clip_mod = mod[clip]

        def first_back(step, carry, clip=clip, clip_mod=clip_mod):
            d_shift, d_scale = carry
            rows = pl.ds(pl.multiple_of(clip * span + step * chunk, chunk), chunk)
            grad = d_hidden[rows, :]
            unit, d_value = norm_back(grad, tokens[rows, :].astype(F32), clip_mod[1:2])
            input_grad[rows, :] = (d_middle[rows, :] + d_value).astype(LOW)
            return (
                d_shift + jnp.sum(grad, 0, keepdims=True),
                d_scale + jnp.sum(grad * unit, 0, keepdims=True),
            )

        sums = lax.fori_loop(0, span // chunk, first_back, (zero_row, zero_row))
        d_mod[clip, 0:1, :] = sums[0]
        d_mod[clip, 1:2, :] = sums[1]


def attn_weight_kernel(packing, distances, *refs):
    own, far, outs, d_pieces = refs[:4], refs[4:8], refs[8:-1], refs[-1]
    half, qkv_cols, proj_cols = packing.half, packing.qkv_cols, packing.proj_cols
    row_count = own[0].shape[1]
    column_parts = own[2].shape[0]
    row_parts = own[0].shape[0] // (2 * half)
    for start, group in ((0, own), (row_count, far)):
        for place in range(column_parts):
            d_pieces[place, start : start + row_count, :] = columns_of(
                group[3], slice(None), place, proj_cols
            )
    column, row = here(AXES)
    for index, z_bits in enumerate(distances):
        for x_bit in range(2):
            place = column ^ (2 * z_bits + x_bit)
            d_qkv = jnp.concatenate(
                [own[2][place, :, 0:qkv_cols], far[2][place, :, 0:qkv_cols]], axis=0
            )
            d_proj = d_pieces[place]
            for other in range(row_parts // 2):
                rows = pl.ds(pl.multiple_of((row ^ (2 * other)) * 2 * half, 16), 2 * half)
                hidden_t, attended_t = (
                    jnp.concatenate([own[which][rows, :], far[which][rows, :]], axis=1)
                    for which in range(2)
                )
                qkv = dot_nn(hidden_t, d_qkv)
                proj = dot_nn(attended_t, d_proj)
                outs[2 * index + other][x_bit] = packing.pack(qkv, proj).astype(LOW)


def feed_kernel(chunk, parts, *refs):
    sources, stacked, outs = refs[0:4], refs[4], refs[5:11]
    hidden, d_outs, up_weight, down_weight, up_proj, d_activ, activ, d_up, wide, narrow = refs[11:21]
    in_sems, weight_sems, out_sems = refs[21:]
    rows_each = sources[0].shape[0]
    half = stacked.shape[0] // (2 * parts)
    halves = [pl.ds(index * rows_each, rows_each) for index in range(2)]

    def started(source, target, sem):
        copy = pltpu.make_async_copy(source, target, sem)
        copy.start()
        return copy

    waits = []
    for which, (target, weight) in enumerate(((hidden, up_weight), (d_outs, down_weight))):
        waits.append(
            [
                started(sources[2 * which + index], target.at[rows], in_sems.at[which, index])
                for index, rows in enumerate(halves)
            ]
            + [
                started(
                    stacked.at[pl.ds((2 * part + which) * half, half)],
                    weight.at[pl.ds(part * half, half)],
                    weight_sems.at[part, which],
                )
                for part in range(parts)
            ]
        )
    sent = []
    tilt = math.sqrt(2.0 / math.pi)
    for copy in waits[0]:
        copy.wait()
    up_proj[...] = dot_nt(hidden[...], up_weight[...])
    for copy in waits[1]:
        copy.wait()
    d_activ[...] = dot_nn(d_outs[...], down_weight[...])

    def gelu(step, carry):
        rows = pl.ds(pl.multiple_of(step * chunk, chunk), chunk)
        value = up_proj[rows, :]
        square = value * value
        bend = jnp.tanh(value * (tilt + (tilt * 0.044715) * square))
        half_value = 0.5 * value
        activ[rows, :] = (half_value + half_value * bend).astype(LOW)
        slope = (0.5 + 0.5 * bend) + half_value * (1.0 - bend * bend) * (
            tilt + (tilt * 3.0 * 0.044715) * square
        )
        d_up[rows, :] = (d_activ[rows, :] * slope).astype(LOW)
        return carry

    lax.fori_loop(0, 2 * rows_each // chunk, gelu, 0)
    for index, rows in enumerate(halves):
        sent.append(started(activ.at[rows], outs[index], out_sems.at[index]))
        sent.append(started(d_up.at[rows], outs[2 + index], out_sems.at[2 + index]))
    value = dot_nn(d_up[...], up_weight[...])
    narrow[...] = value[rows_each:].astype(LOW)
    sent.append(started(narrow, outs[5], out_sems.at[5]))
    wide[...] = value[:rows_each]
    sent.append(started(wide, outs[4], out_sems.at[4]))
    for copy in sent:
        copy.wait()


def feed_weight_kernel(parts, *refs):
    gathered, stacked, results = refs[16], refs[17], refs[18:22]
    down_weight, sems = refs[22:]
    half = gathered.shape[0] // (2 * parts)
    copies = []
    for part in range(parts):
        copy = pltpu.make_async_copy(
            gathered.at[pl.ds((2 * part + 1) * half, half)],
            down_weight.at[pl.ds(part * half, half)],
            sems.at[part],
        )
        copy.start()
        copies.append(copy)
    hidden, d_outs, activ, d_up = (
        jnp.concatenate([ref[...] for ref in refs[i : i + 4]], axis=0) for i in (0, 4, 8, 12)
    )
    for side, (left, right) in enumerate(((d_up, hidden), (d_outs, activ))):
        total = dot_tn(left, right).astype(LOW)
        for part in range(parts):
            stacked[part, side * half : (side + 1) * half, :] = total[
                part * half : (part + 1) * half
            ]
    for copy in copies:
        copy.wait()
    total = dot_nt(activ, down_weight[...])
    rows = results[0].shape[0]
    for index, result in enumerate(results):
        result[...] = total[index * rows : (index + 1) * rows].astype(result.dtype)


def join_rows_kernel(pieces, out):
    height = pieces.shape[2]
    for part in range(pieces.shape[0]):
        out[:, part * height : (part + 1) * height] = pieces[part, 0 : out.shape[0], :]


def modulation_kernel(conds, ada, part_out, ordered):
    groups, rows, _ = ordered.shape
    for group in range(groups):
        ordered[group] = conds[group, 0:rows, 0 : ada.shape[0]]
        part_out[group * rows : (group + 1) * rows, :] = dot_nn(ordered[group], ada[...])


def prepare_kernel(packing, sub, clips, *refs):
    timesteps, labels, time_table, class_table, qkv, proj_t, up, down_t, packed, send = refs
    packed[...] = packing.pack(qkv[...], proj_t[...].T)
    row_parts = send.shape[0]

    def look_up(indices, table):
        count = table.shape[0]
        row = lax.broadcasted_iota(jnp.int32, (16, count), 0)
        column = lax.broadcasted_iota(jnp.int32, (16, count), 1)
        picked = jnp.zeros((16, count), jnp.bool_)
        for clip in range(clips):
            picked = picked | ((row == clip) & (column == indices[clip]))
        return dot_nn(picked.astype(F32).astype(LOW), table[...])

    embedded = look_up(timesteps, time_table) + look_up(labels, class_table)
    cond = (embedded * (1.0 / (1.0 + jnp.exp(-embedded)))).astype(LOW)
    up_t = up[...].T
    height = send.shape[2]
    pairs = height // sub
    for part in range(row_parts):
        send[part, 0:sub] = up_t[part * sub : (part + 1) * sub, :]
        send[part, 2 * sub :] = cond[:, part * height : (part + 1) * height]
        for pair in range(pairs):
            start = (pair * row_parts + part) * sub
            send[part, sub : 2 * sub, pair * sub : (pair + 1) * sub] = down_t[:, start : start + sub]


def cut_rows_kernel(total, out):
    parts, sides, half, height = out.shape
    for part in range(parts):
        for side in range(sides):
            out[part, side] = total[
                side * half : (side + 1) * half, part * height : (part + 1) * height
            ]


def feed_finish_kernel(back, up_grad, down_grad_t):
    parts, _, sub, height = back.shape
    pairs = height // sub
    for part in range(parts):
        up_grad[:, part * sub : (part + 1) * sub] = back[part, 0].astype(F32).T
        for pair in range(pairs):
            start = (pair * parts + part) * sub
            down_grad_t[:, start : start + sub] = back[
                part, 1, :, pair * sub : (pair + 1) * sub
            ].astype(F32)


def attn_finish_kernel(packing, *refs):
    total = refs[0][...].astype(F32)
    for ref in refs[1:-2]:
        total += ref[...].astype(F32)
    qkv_grad, proj_grad_t = refs[-2:]
    for side in range(2):
        rows = slice(side * packing.half, (side + 1) * packing.half)
        qkv_grad[rows, :] = packing.qkv_of(total, side)
        proj_grad_t[:, rows] = packing.proj_of(total, side).T


VMEM_SPEC = pl.BlockSpec(memory_space=pltpu.VMEM)
SMEM_SPEC = pl.BlockSpec(memory_space=pltpu.SMEM)
ANY_SPEC = pl.BlockSpec(memory_space=pl.ANY)
PARAMS = pltpu.CompilerParams(vmem_limit_bytes=56 * 1024 * 1024)


def shape_of(dims, kind=LOW):
    return jax.ShapeDtypeStruct(dims, kind)


def cost(micros):
    return pl.CostEstimate(flops=1000, bytes_accessed=int(micros * SCALE), transcendentals=0)


def after(value, *others):
    return lax.optimization_barrier((value,) + others)[0]


class Sequence:
    def __init__(self):
        self.token = None

    def call(self, kernel, shapes, arrays, name, specs=None, scratch=(), tied=0, out_spec=None):
        arrays = list(arrays)
        if self.token is not None:
            arrays[tied] = after(arrays[tied], self.token)
        results = pl.pallas_call(
            kernel,
            out_shape=shapes,
            in_specs=specs or [VMEM_SPEC] * len(arrays),
            out_specs=jax.tree.map(lambda _: out_spec or VMEM_SPEC, shapes),
            scratch_shapes=scratch,
            compiler_params=PARAMS,
            cost_estimate=cost(1),
            name=name,
        )(*arrays)
        self.token = min(jax.tree.leaves(results), key=lambda result: result.size)
        return results

    def sum_low(self, *arrays):
        total = after(arrays[0], self.token).astype(F32)
        for array in arrays[1:]:
            total += array.astype(F32)
        self.token = total.astype(LOW)
        return self.token


def swap(value, mask, count):
    return lax.ppermute(value, AXES, [(i, i ^ mask) for i in range(count)])


def padded_exchange(rows, count):
    length = rows.shape[1]
    tiles = -(-length // 1024) * 8
    rows = jnp.pad(rows, ((0, 0), (0, tiles * 128 - length))).reshape(count, tiles, 128)
    got = lax.all_to_all(rows, AXES, 0, 0, tiled=True)
    return got.reshape(count, tiles * 128)[:, :length]


def fast_body(
    column_parts,
    row_parts,
    inputs,
    out_cotangent,
    lengths,
    timesteps,
    labels,
    time_table,
    class_table,
    ada_weight,
    qkv_weight,
    proj_weight,
    up_weight,
    down_weight,
):
    count = column_parts * row_parts
    clips, positions, frames, width = inputs.shape
    span = positions * frames
    row_count = clips * span
    qkv_cols, proj_cols = qkv_weight.shape[1], proj_weight.shape[1]
    height = qkv_weight.shape[0]
    part_width = width // row_parts
    hidden_part = up_weight.shape[1] * column_parts // row_parts
    sub = up_weight.shape[1] // row_parts
    x_mask = row_parts
    z_masks = tuple(row_parts * 2 * i for i in range(1, column_parts // 2))
    packing = Packing(height // 2, qkv_cols, proj_cols)

    line = Sequence()
    packed, both_send = line.call(
        functools.partial(prepare_kernel, packing, sub, clips),
        (
            shape_of((height // 2, packing.width)),
            shape_of((row_parts, 2 * sub + 16, height)),
        ),
        (timesteps, labels, time_table, class_table)
        + (qkv_weight, proj_weight.T, up_weight, down_weight.T),
        "prepare",
        [SMEM_SPEC] * 2 + [VMEM_SPEC] * 6,
    )

    y_mask, c_mask = 2, 1
    ada_cols = ada_weight.shape[1]

    def gate(*values):
        return lax.optimization_barrier(values)

    own = packed[None]
    far = [swap(own, mask, count) for mask in z_masks]
    own_x, own_y = swap(own, x_mask, count), swap(own, y_mask, count)
    both_got = lax.all_to_all(both_send, "fsdp", 0, 0, tiled=True)
    *far, own_x, own_y, both_got = gate(*far, own_x, own_y, both_got)
    own_feed = line.call(join_rows_kernel, shape_of((2 * sub, width)), (both_got,), "join_rows")
    conds = both_got[:, 2 * sub : 2 * sub + clips].reshape(row_parts * clips, height)
    feed = lax.all_gather(own_feed, "dp", axis=0, tiled=True)

    far = jnp.concatenate(far)
    pads = (-row_parts * clips % 16, -height % 128)
    conds = jnp.pad(conds, ((0, pads[0]), (0, pads[1])))
    conds = jnp.broadcast_to(conds[None], (column_parts,) + conds.shape)
    conds = lax.all_to_all(conds, "dp", 0, 0, tiled=True)
    far_x, far_y = swap(far, x_mask, count), swap(far, y_mask, count)
    cores = [swap(array, c_mask, count) for array in (own, own_x, own_y, far)]
    far_x, far_y, conds, *cores = gate(far_x, far_y, conds, *cores)

    mod_part, conds = line.call(
        modulation_kernel,
        (
            shape_of((count * clips, ada_cols), F32),
            shape_of((column_parts, row_parts * clips, part_width)),
        ),
        (conds, ada_weight),
        "modulation",
    )
    cond_all = conds.reshape(count * clips, part_width)
    mod_got = padded_exchange(mod_part.reshape(count, clips * ada_cols), count)
    own_xy, far_xy = swap(own_x, y_mask, count), swap(far_x, y_mask, count)
    cores += [swap(array, c_mask, count) for array in (far_x, far_y)]
    own_xy, far_xy, mod_got, *cores = gate(own_xy, far_xy, mod_got, *cores)
    mod_own = jnp.sum(mod_got.reshape(column_parts, row_parts, clips, ada_cols), axis=1)
    mod = mod_own.transpose(1, 0, 2).reshape(clips, 6, width)
    cores += [swap(array, c_mask, count) for array in (own_xy, far_xy)]

    blocks = [own, own_x, own_y, far, far_x, far_y, own_xy, far_xy]
    places = [[0], [x_mask], [y_mask], list(z_masks)]
    places += [[z ^ side for z in z_masks] for side in (x_mask, y_mask)]
    places += [[x_mask ^ y_mask]]
    places += [[z ^ x_mask ^ y_mask for z in z_masks]]
    blocks += cores
    places += [[place ^ c_mask for place in held] for held in places]

    tokens = inputs.reshape(row_count, width)
    cotangent = out_cotangent.reshape(row_count, width)
    gate_two = jnp.repeat(mod[:, 5], span, axis=0)
    d_out = (cotangent.astype(F32) * gate_two).astype(LOW)
    d_outs = {0: d_out, 1: swap(d_out, 1, count), 2: swap(d_out, 2, count)}
    d_outs[3] = swap(d_outs[2], 1, count)
    sizes = (clips, span, frames, width, 32)
    full = (row_count, width)
    weight_scratch = pltpu.VMEM((column_parts, row_parts, height // 2, packing.width), LOW)
    weight_sems = pltpu.SemaphoreType.DMA((count,))
    hidden, mixed, probs, attended, branch, middle, hidden_two, proj_full = line.call(
        functools.partial(attn_forward_kernel, sizes, packing, places),
        (
            shape_of((width, row_count)),
            shape_of((column_parts, row_count, qkv_cols)),
            shape_of((clips, HEADS, span, span)),
            shape_of((width, row_count)),
            shape_of(full),
            shape_of(full, F32),
            shape_of(full),
            shape_of((width, width)),
        ),
        (lengths, tokens, mod, *blocks),
        "attn_forward",
        [SMEM_SPEC, VMEM_SPEC, VMEM_SPEC] + [ANY_SPEC] * len(blocks),
        (
            weight_scratch,
            pltpu.VMEM(full, F32),
            pltpu.VMEM(full, LOW),
            pltpu.VMEM(full, LOW),
            weight_sems,
        ),
        tied=2,
    )

    tokens_two = {0: hidden_two, 1: swap(hidden_two, 1, count), 2: swap(hidden_two, 2, count)}
    pair = (2 * row_count, width)
    pair_hidden = (2 * row_count, hidden_part)
    feed_scratch = (
        pltpu.VMEM(pair, LOW),
        pltpu.VMEM(pair, LOW),
        pltpu.VMEM((hidden_part, width), LOW),
        pltpu.VMEM((width, hidden_part), LOW),
        pltpu.VMEM(pair_hidden, F32),
        pltpu.VMEM(pair_hidden, F32),
        pltpu.VMEM(pair_hidden, LOW),
        pltpu.VMEM(pair_hidden, LOW),
        pltpu.VMEM(full, F32),
        pltpu.VMEM(full, LOW),
        pltpu.SemaphoreType.DMA((2, 2)),
        pltpu.SemaphoreType.DMA((column_parts, 2)),
        pltpu.SemaphoreType.DMA((6,)),
    )

    def feed_call(index, name):
        return line.call(
            functools.partial(feed_kernel, 16, column_parts),
            [shape_of((row_count, hidden_part))] * 4 + [shape_of(full, F32), shape_of(full)],
            (
                tokens_two[index],
                tokens_two[index + 1],
                d_outs[index],
                d_outs[index + 1],
                feed,
            ),
            name,
            [ANY_SPEC] * 5,
            feed_scratch,
            out_spec=ANY_SPEC,
        )

    near = feed_call(0, "feed_near")
    tokens_two[2] = after(tokens_two[2], line.token)
    tokens_two[3] = swap(tokens_two[2], 1, count)
    distant = feed_call(2, "feed_distant")

    grad_send = line.sum_low(distant[4], swap(distant[5], 1, count))
    grad_far = swap(grad_send, 2, count)
    grad_parts = (near[4], swap(near[5], 1, count), grad_far)
    feed_grads, *partials = line.call(
        functools.partial(feed_weight_kernel, column_parts),
        [shape_of((column_parts, 2 * sub, width))]
        + [shape_of(full, F32), shape_of(full)]
        + [shape_of(full)] * 2,
        [tokens_two[i] for i in range(4)]
        + [d_outs[i] for i in range(4)]
        + [*near[0:2], *distant[0:2], *near[2:4], *distant[2:4], feed],
        "feed_weight",
        [VMEM_SPEC] * 16 + [ANY_SPEC],
        (pltpu.VMEM((width, hidden_part), LOW), pltpu.SemaphoreType.DMA((column_parts,))),
    )
    feed_grads = feed_grads.reshape(2 * sub * column_parts, width)
    far_side = [swap(array, 1, count) for array in (hidden, attended)]
    feed_grads, grad_far, *far_side = lax.optimization_barrier((feed_grads, grad_far, *far_side))
    grad_parts = grad_parts[:2] + (grad_far,)
    line.token = grad_far
    groups = column_parts // 2
    feed_sum = lax.psum_scatter(feed_grads, "dp", scatter_dimension=0, tiled=True)

    out_send = line.sum_low(partials[2], swap(partials[3], 1, count))
    out_far = swap(out_send, 2, count)
    d_middle, d_branch, d_attended, d_mod_two = line.call(
        functools.partial(proj_backward_kernel, sizes),
        (
            shape_of(full, F32),
            shape_of(full),
            shape_of(full),
            shape_of((clips, 3, width), F32),
        ),
        (cotangent, mod, middle, branch, *grad_parts, proj_full),
        "proj_backward",
    )
    d_mixed = line.call(
        functools.partial(attn_backward_kernel, (clips, span, frames, width, qkv_cols)),
        shape_of((column_parts, row_count, -(-qkv_cols // 128) * 128)),
        (mixed, probs, d_attended),
        "attn_backward",
    )
    own_side = (hidden, attended, d_mixed, d_branch)
    far_side += [swap(array, 1, count) for array in own_side[2:]]
    attn_grads, first = {}, {}
    for distances in (range(groups - 1, groups // 2 - 1, -1), range(groups // 2 - 1, -1, -1)):
        grads = line.call(
            functools.partial(attn_weight_kernel, packing, distances),
            [shape_of((2, height // 2, packing.width))] * (2 * len(distances)),
            (*own_side, *far_side),
            "attn_weight",
            scratch=(pltpu.VMEM((column_parts, 2 * row_count, proj_cols), LOW),),
        )
        for index, distance in enumerate(distances):
            attn_grads[distance] = grads[2 * index]
            first[distance] = swap(grads[2 * index + 1], y_mask, count)
        if not len(distances) < len(first):
            ffn_out = after(partials[0], line.token) + swap(partials[1], 1, count).astype(F32)
            ffn_out += out_far.astype(F32)
            result = (middle + gate_two * ffn_out).astype(LOW).reshape(inputs.shape)
            d_gate_two = jnp.sum(
                (cotangent.astype(F32) * ffn_out).reshape(clips, 1, span, width), axis=2
            )
            line.token = d_gate_two
    input_grad, d_mod_one = line.call(
        functools.partial(qkv_backward_kernel, sizes, packing, places),
        (shape_of(full), shape_of((clips, 2, width), F32)),
        (tokens, mod, d_middle, d_mixed, *blocks),
        "qkv_backward",
        [VMEM_SPEC] * 4 + [ANY_SPEC] * len(blocks),
        (weight_scratch, pltpu.VMEM(full, F32), weight_sems),
    )
    stay, second, attn_z = {}, {}, {}

    def split_sum(index):
        kept = after(attn_grads[index], line.token)
        stay[index] = kept[0].astype(F32) + first[index][0].astype(F32)
        leave = (kept[1].astype(F32) + first[index][1].astype(F32)).astype(LOW)
        line.token = leave
        second[index] = swap(leave, x_mask, count)

    def attn_sum(index):
        summed = line.sum_low(stay[index], second[index])
        attn_z[index] = swap(summed, z_masks[index - 1], count)

    d_mod = jnp.concatenate([d_mod_one, d_mod_two, d_gate_two], axis=1)
    mod_send = d_mod.reshape(clips, column_parts, ada_cols).transpose(1, 0, 2)
    mod_send = jnp.broadcast_to(
        mod_send.reshape(column_parts, 1, clips * ada_cols),
        (column_parts, row_parts, clips * ada_cols),
    ).reshape(count, clips * ada_cols)
    d_mod_all = padded_exchange(mod_send, count).reshape(count * clips, ada_cols)
    split_sum(3)
    line.token, d_mod_all = lax.optimization_barrier((line.token, d_mod_all))
    split_sum(2)
    attn_sum(3)
    attn_sum(2)
    split_sum(1)
    back = line.call(
        cut_rows_kernel, shape_of((row_parts, 2, sub, height)), (feed_sum,), "cut_rows"
    )
    line.token, back = lax.optimization_barrier((line.token, back))
    back = lax.all_to_all(back, "fsdp", 0, 0, tiled=True)
    split_sum(0)
    attn_sum(1)
    up_grad, down_grad_t = line.call(
        feed_finish_kernel,
        (shape_of(up_weight.shape, F32), shape_of(down_weight.shape[::-1], F32)),
        (back,),
        "feed_finish",
    )
    down_grad = down_grad_t.T
    qkv_grad, proj_grad_t = line.call(
        functools.partial(attn_finish_kernel, packing),
        (shape_of((height, qkv_cols), F32), shape_of((proj_cols, height), F32)),
        (stay[0], second[0], attn_z[3], attn_z[2], attn_z[1]),
        "attn_finish",
    )
    proj_grad = proj_grad_t.T

    ada_grad = lax.dot_general(
        cond_all.astype(F32),
        d_mod_all,
        (((0,), (0,)), ((), ())),
        precision=lax.Precision.HIGHEST,
        preferred_element_type=F32,
    )
    return (
        result,
        input_grad.reshape(inputs.shape),
        ada_grad,
        qkv_grad,
        proj_grad,
        up_grad,
        down_grad,
    )


def solution(mesh):
    column_parts, row_parts = mesh.shape["dp"], mesh.shape["fsdp"]
    body = general_body
    if (column_parts, row_parts) == (8, 4):
        body = functools.partial(fast_body, column_parts, row_parts)
    clip_spec = P(AXES, None, None, None)
    return jax.shard_map(
        body,
        mesh=mesh,
        in_specs=(
            clip_spec,
            clip_spec,
            P(AXES),
            P(AXES),
            P(AXES),
            P(),
            P(),
        )
        + (P("fsdp", "dp"),) * 5,
        out_specs=(clip_spec, clip_spec) + (P("fsdp", "dp"),) * 5,
        check_vma=False,
    )
```
